32 devices in a mesh: seq: 8 (over y, x, core), tp: 4 (over z).
Axes of the slice: x: 2, y: 2, z: 4, core: 2. Of those that a mesh axis runs over, the one named last changes fastest.
Arguments:
- inputs: bfloat16 [16384, 1024], P(('seq', 'tp')), may hold values from -6 to 6
- segment_ids: int32 [8, 2048], P('seq'), may hold values from 0 to 5, never falling along the last dimension, each value on 1 to 512 neighbouring positions
- row_lengths: int32 [8], P('seq'), may hold values from 1536 to 2048
- norm1_gain: float32 [1024], replicated, may hold values from 0.5 to 1.5
- norm1_shift: float32 [1024], replicated, may hold values from -4 to 4
- w_query: bfloat16 [1024, 1024], P(None, 'tp'), may hold values from -0.1875 to 0.1875
- w_key: bfloat16 [1024, 1024], P(None, 'tp'), may hold values from -0.1875 to 0.1875
- w_value: bfloat16 [1024, 1024], P(None, 'tp'), may hold values from -0.1875 to 0.1875
- b_query: float32 [1024], P('tp'), may hold values from -6 to 6
- b_value: float32 [1024], P('tp'), may hold values from -6 to 6
- w_out: bfloat16 [1024, 1024], P('tp'), may hold values from -2 to 2
- b_out: float32 [1024], replicated, may hold values from -6 to 6
- norm2_gain: float32 [1024], replicated, may hold values from 0.5 to 1.5
- norm2_shift: float32 [1024], replicated, may hold values from -4 to 4
- w_up: bfloat16 [1024, 1024], P(None, 'tp'), may hold values from -0.1875 to 0.1875
- b_up: float32 [1024], P('tp'), may hold values from -6 to 6
- w_down: bfloat16 [1024, 1024], P('tp'), may hold values from -0.1875 to 0.1875
- b_down: float32 [1024], replicated, may hold values from -6 to 6
- out_grad: bfloat16 [16384, 1024], P(('seq', 'tp')), may hold values from -6 to 6
Outputs:
- output: bfloat16 [16384, 1024], P(('seq', 'tp'))
- grad_inputs: bfloat16 [16384, 1024], P(('seq', 'tp'))
- grad_norm1_gain: float32 [1024], replicated
- grad_norm1_shift: float32 [1024], replicated
- grad_w_query: float32 [1024, 1024], P(None, 'tp')
- grad_w_key: float32 [1024, 1024], P(None, 'tp')
- grad_w_value: float32 [1024, 1024], P(None, 'tp')
- grad_b_query: float32 [1024], P('tp')
- grad_b_value: float32 [1024], P('tp')
- grad_w_out: float32 [1024, 1024], P('tp')
- grad_b_out: float32 [1024], replicated
- grad_norm2_gain: float32 [1024], replicated
- grad_norm2_shift: float32 [1024], replicated
- grad_w_up: float32 [1024, 1024], P(None, 'tp')
- grad_b_up: float32 [1024], P('tp')
- grad_w_down: float32 [1024, 1024], P('tp')
- grad_b_down: float32 [1024], replicated
The draws below stay inside these ranges and needn't reach their ends.
Inputs may be any that keep to these rules, and one draw needn't show every extreme that they name: `segment_ids`: along a row segment numbers never fall, and one number covers at most 512 positions; positions at or past a row's length are padding.
All inputs are finite; a program needn't handle non-finite values.
Results may differ from the reference program's by a relative error of at most 0.018.
Values may be sent and summed in bfloat16 or wider, within the bound.
No kernel may reach another device: no remote copies, remote signals or barrier semaphores. Data moves between devices by JAX's collectives and lax.ppermute only.
A program may use at most 128 MiB of HBM per device.

```python
import math
import jax
import jax.numpy as jnp
import numpy as np
from jax import lax

D = 1024
HEADS = 8
HEAD_DIM = 128
FF = 1024
ROW_LEN = 2048
SEG_MOST = 512
SEGMENTS = 6
ROWS = 8
TOKENS = 16384


def set_ends(entries, stream_key, least, top_value):
    shape = entries.shape
    index_at = [jax.random.randint(jax.random.fold_in(stream_key, axis), (), 0, shape[axis]) for axis in range(len(shape))]
    entries = entries.at[tuple(index_at)].set(least)
    longest = shape.index(max(shape))
    index_at[longest] = (index_at[longest] + 1) % shape[longest]
    return entries.at[tuple(index_at)].set(top_value)


def level_of(own_key, dims, shards, smallest, largest):
    def one(dim, parts):
        draws = jax.random.uniform(jax.random.fold_in(jax.random.fold_in(own_key, 6), dim), (parts,), jnp.float32, smallest / len(shards), largest / len(shards))
        return jnp.repeat(jnp.exp(draws), dims[dim] // parts).reshape((-1,) + (1,) * (len(dims) - dim - 1))

    gain = one(*shards[0])
    for cut in shards[1:]:
        gain = gain * one(*cut)
    return gain


def split_up(number_of, total, reach, lean):
    portions = [(1 << 20) // math.isqrt(rank ** lean) + 1 for rank in range(2, number_of + 1)]
    rest, holding = total - reach - (number_of - 1), [1] * (number_of - 1)
    while rest > 0:
        movable = [i for i in range(number_of - 1) if holding[i] < reach]
        whole, budget = sum([portions[i] for i in movable]), rest
        for i in movable:
            extra = min(reach - holding[i], max(1, budget * portions[i] // whole), rest)
            holding[i] = holding[i] + extra
            rest = rest - extra
    return np.array([reach] + holding)


def uneven(key, number_of, total, reach, skew):
    if number_of == 2:
        one = jax.random.randint(key, (), max(1, total - reach), min(reach, total - 1) + 1)
        return jnp.stack([one, total - one])
    sizes = jnp.asarray(split_up(number_of, total, reach, skew), jnp.int32)
    couples = (number_of - 1) // 2
    donor, receiver = sizes[1:1 + 2 * couples:2], sizes[2:2 + 2 * couples:2]
    slack = jnp.minimum(donor - 1, reach - receiver)
    passed = jax.random.randint(jax.random.fold_in(key, 1), (couples,), 0, 1 << 20) % (slack + 1)
    sizes = sizes.at[1:1 + 2 * couples:2].set(donor - passed).at[2:2 + 2 * couples:2].set(receiver + passed)
    return sizes[jax.random.permutation(jax.random.fold_in(key, 2), number_of)]


def normal_values(rng, shape, scale, bound, shards=(), held_as=jnp.bfloat16):
    entries = jax.random.normal(rng, shape, jnp.float32) * scale
    if len(shards) > 0:
        entries = level_of(rng, shape, shards, -0.22, 0.18) * entries
    return jnp.clip(entries, min=-bound, max=bound).astype(held_as)


def setup_inputs(seed: int = 0) -> dict:
    arg_keys = jax.random.split(jax.random.key(seed), 20)
    inputs = normal_values(arg_keys[0], (TOKENS, D), 1.0, 6.0, ((0, 32),))
    segment_ids = jax.vmap(lambda own: jnp.searchsorted(jnp.cumsum(uneven(own, SEGMENTS, ROW_LEN, SEG_MOST, 1)), jnp.arange(ROW_LEN), side="right"))(jax.random.split(arg_keys[1], ROWS)).reshape((ROWS, ROW_LEN)).astype(jnp.int32)
    row_lengths = set_ends(jax.random.randint(arg_keys[2], (ROWS,), ROW_LEN - ROW_LEN // 4, ROW_LEN + 1), jax.random.fold_in(arg_keys[2], 1), ROW_LEN - ROW_LEN // 4, ROW_LEN).astype(jnp.int32)
    norm1_gain = jnp.clip(1.0 + 0.1 * jax.random.normal(arg_keys[3], (D,), jnp.float32), 0.5, 1.5)
    norm1_shift = normal_values(arg_keys[4], (D,), 0.3, 4.0, (), jnp.float32)
    w_query = normal_values(arg_keys[5], (D, D), D ** -0.5, 0.1875, ((1, 4),))
    w_key = normal_values(arg_keys[6], (D, D), D ** -0.5, 0.1875, ((1, 4),))
    w_value = normal_values(arg_keys[7], (D, D), D ** -0.5, 0.1875, ((1, 4),))
    b_query = normal_values(arg_keys[8], (D,), 0.5, 6.0, ((0, 4),), jnp.float32)
    b_value = normal_values(arg_keys[9], (D,), 0.5, 6.0, ((0, 4),), jnp.float32)
    w_out = normal_values(arg_keys[10], (D, D), (max(D // 128, 4)) ** -0.5, 2.0, ((0, 4),))
    b_out = normal_values(arg_keys[11], (D,), 0.5, 6.0, (), jnp.float32)
    norm2_gain = jnp.clip(1.0 + 0.1 * jax.random.normal(arg_keys[12], (D,), jnp.float32), 0.5, 1.5)
    norm2_shift = normal_values(arg_keys[13], (D,), 0.3, 4.0, (), jnp.float32)
    w_up = normal_values(arg_keys[14], (D, FF), D ** -0.5, 0.1875, ((1, 4),))
    b_up = normal_values(arg_keys[15], (FF,), 0.5, 6.0, ((0, 4),), jnp.float32)
    w_down = normal_values(arg_keys[16], (FF, D), FF ** -0.5, 0.1875, ((0, 4),))
    b_down = normal_values(arg_keys[17], (D,), 0.5, 6.0, (), jnp.float32)
    out_grad = normal_values(arg_keys[18], (TOKENS, D), 1.0, 6.0, ((0, 32),))
    return dict(inputs=inputs, segment_ids=segment_ids, row_lengths=row_lengths, norm1_gain=norm1_gain, norm1_shift=norm1_shift, w_query=w_query, w_key=w_key, w_value=w_value, b_query=b_query, b_value=b_value, w_out=w_out, b_out=b_out, norm2_gain=norm2_gain, norm2_shift=norm2_shift, w_up=w_up, b_up=b_up, w_down=w_down, b_down=b_down, out_grad=out_grad)


@jax.custom_vjp
def low(v):
    return lax.optimization_barrier(v.astype(jnp.bfloat16)).astype(jnp.float32)

@jax.custom_vjp
def low_back(v):
    return v

def low_keep(v):
    return (low(v), None)

def low_pass(kept, grad):
    return (grad,)

def back_keep(v):
    return (v, None)

def back_low(kept, grad):
    return (low(grad),)
low.defvjp(low_keep, low_pass)
low_back.defvjp(back_keep, back_low)
norm_eps = 1e-05
mask_fill = -1000000000.0

def norm_rows(values, gain_vec, shift_vec):
    centre = values - lax.optimization_barrier(jnp.mean(values, axis=-1, keepdims=True))
    spread = lax.optimization_barrier(jnp.mean(centre * centre, axis=-1, keepdims=True))
    return centre * lax.rsqrt(spread + norm_eps) * gain_vec + shift_vec

def matmul_high(left, right):
    return jnp.dot(left, right, precision=lax.Precision.HIGHEST)

def allowed_pairs(seg_row, row_length):
    position = jnp.arange(ROW_LEN, dtype=jnp.int32)
    inside = position < row_length
    same_image = seg_row[:, None] == seg_row[None, :]
    both_inside = inside[:, None] & inside[None, :]
    itself = position[:, None] == position[None, :]
    return same_image & (both_inside | itself)

def row_attention(queries, keys_row, values_row, allowed):
    scores = jnp.einsum('qhe,khe->hqk', queries, keys_row, precision=lax.Precision.HIGHEST) * HEAD_DIM ** (-0.5)
    scores = low_back(scores)
    scores = jnp.where(allowed[None], scores, mask_fill)
    weights = low(jax.nn.softmax(scores, axis=-1))
    return jnp.einsum('hqk,khe->qhe', weights, values_row, precision=lax.Precision.HIGHEST)

def layer(wide_in, norm1_gain, norm1_shift, w_query, w_key, w_value, b_query, b_value, w_out, b_out, norm2_gain, norm2_shift, w_up, b_up, w_down, b_down, segment_ids, row_lengths):
    first_low = low(norm_rows(wide_in, norm1_gain, norm1_shift))
    queries = low(low_back(matmul_high(first_low, w_query) + b_query))
    keys_all = low(low_back(matmul_high(first_low, w_key)))
    values_all = low(low_back(matmul_high(first_low, w_value) + b_value))
    shape_rows = (ROWS, ROW_LEN, HEADS, HEAD_DIM)
    attend = jax.checkpoint(row_attention)

    def step_row(carry_value, item):
        query_row, key_row, value_row, seg_row, row_length = item
        return (carry_value, attend(query_row, key_row, value_row, allowed_pairs(seg_row, row_length)))
    _, mixed = lax.scan(step_row, jnp.zeros((), jnp.float32), (queries.reshape(shape_rows), keys_all.reshape(shape_rows), values_all.reshape(shape_rows), segment_ids, row_lengths))
    mixed = low(low_back(mixed.reshape(TOKENS, D)))
    first_resid = wide_in + low_back(matmul_high(mixed, w_out)) + b_out
    second_low = low(norm_rows(first_resid, norm2_gain, norm2_shift))
    hidden = low(jax.nn.gelu(low_back(matmul_high(second_low, w_up) + b_up), approximate=False))
    return first_resid + low_back(matmul_high(hidden, w_down)) + b_down

def reference(inputs, segment_ids, row_lengths, norm1_gain, norm1_shift, w_query, w_key, w_value, b_query, b_value, w_out, b_out, norm2_gain, norm2_shift, w_up, b_up, w_down, b_down, out_grad):

    def forward(*floats):
        return layer(*floats, segment_ids, row_lengths)
    primals = [inputs, norm1_gain, norm1_shift, w_query, w_key, w_value, b_query, b_value, w_out, b_out, norm2_gain, norm2_shift, w_up, b_up, w_down, b_down]
    primals = [item.astype(jnp.float32) for item in primals]
    result, pull_back = jax.vjp(forward, *primals)
    grads = pull_back(out_grad.astype(jnp.float32))
    return (result.astype(jnp.bfloat16), grads[0].astype(jnp.bfloat16), grads[1], grads[2], grads[3], grads[4], grads[5], grads[6], grads[7], grads[8], grads[9], grads[10], grads[11], grads[12], grads[13], grads[14], grads[15])
```

```python
import jax
import jax.numpy as jnp
from jax import lax
from jax.experimental import pallas as pl
from jax.experimental.pallas import tpu as pltpu
from jax.sharding import PartitionSpec as P

HEAD_DIM = 128
ROW_LEN = 2048
NORM_EPS = 1e-05
MASKED = -1000000000.0
LOG2E = 1.4426950408889634
BQ = 256
BK = 256
F32 = jnp.float32
BF16 = jnp.bfloat16
VMEM_LIMIT = 56 * 1024 * 1024


def dot_nn(a, b):
    return lax.dot_general(a, b, (((1,), (0,)), ((), ())), preferred_element_type=F32)


def dot_nt(a, b):
    return lax.dot_general(a, b, (((1,), (1,)), ((), ())), preferred_element_type=F32)


def dot_tn(a, b):
    return lax.dot_general(a, b, (((0,), (0,)), ((), ())), preferred_element_type=F32)


def normalise(x):
    centre = x - jnp.mean(x, axis=-1, keepdims=True)
    rstd = lax.rsqrt(jnp.mean(centre * centre, axis=-1, keepdims=True) + NORM_EPS)
    return centre * rstd, rstd


def norm_back(grad, hat, rstd, gain):
    t = gain * grad
    mean_t = jnp.mean(t, axis=-1, keepdims=True)
    mean_th = jnp.mean(t * hat, axis=-1, keepdims=True)
    return (t - mean_t - hat * mean_th) * rstd


def attend_kernel(rng, segq, segk, q, k, v, mixed, lse, s_scr, m_scr, l_scr, acc):
    heads = q.shape[1] // HEAD_DIM
    coef = HEAD_DIM**-0.5 * LOG2E
    for qb in range(q.shape[0] // BQ):
        rows = slice(qb * BQ, (qb + 1) * BQ)
        lo = rng[0, qb]
        hi = rng[1, qb]
        sq = segq[rows, :]
        m_scr[...] = jnp.full(m_scr.shape, -3e38, F32)
        l_scr[...] = jnp.zeros(l_scr.shape, F32)
        acc[...] = jnp.zeros(acc.shape, F32)

        @pl.loop(lo, hi)
        def _(kc):
            ks = pl.multiple_of(kc * BK, BK)
            bias = jnp.where(sq == segk[:, pl.ds(ks, BK)], 0.0, MASKED)
            for h in range(heads):
                cols = slice(h * HEAD_DIM, (h + 1) * HEAD_DIM)
                s = dot_nt(q[rows, cols], k[pl.ds(ks, BK), cols]) * coef + bias
                s_scr[kc, h] = s
                m = m_scr[h]
                for c in range(0, BK, 128):
                    m = jnp.maximum(m, s[:, c : c + 128])
                m_scr[h] = m

        for h in range(heads):
            m_scr[h] = jnp.broadcast_to(jnp.max(m_scr[h], axis=1, keepdims=True), (BQ, 128))

        @pl.loop(lo, hi)
        def _(kc):
            ks = pl.multiple_of(kc * BK, BK)
            for h in range(heads):
                cols = slice(h * HEAD_DIM, (h + 1) * HEAD_DIM)
                m = m_scr[h]
                p = jnp.exp2(s_scr[kc, h] - jnp.concatenate([m] * (BK // 128), axis=1))
                total = l_scr[h]
                for c in range(0, BK, 128):
                    total = total + p[:, c : c + 128]
                l_scr[h] = total
                acc[h] += dot_nn(p.astype(BF16), v[pl.ds(ks, BK), cols])

        for h in range(heads):
            cols = slice(h * HEAD_DIM, (h + 1) * HEAD_DIM)
            total = jnp.broadcast_to(jnp.sum(l_scr[h], axis=1, keepdims=True), (BQ, 128))
            mixed[rows, cols] = (acc[h] / total).astype(BF16)
            log_total = m_scr[h] + jnp.log2(total)
            for r in range(0, BQ, 128):
                part = jnp.transpose(log_total[r : r + 128])
                lse[h : h + 1, qb * BQ + r : qb * BQ + r + 128] = part[:1]


def attend(rng, segq, segk, q, k, v):
    tokens, width = q.shape
    window = k.shape[0]
    heads = width // HEAD_DIM
    smem = pl.BlockSpec(memory_space=pltpu.SMEM)
    vmem = pl.BlockSpec(memory_space=pltpu.VMEM)
    return pl.pallas_call(
        attend_kernel,
        out_shape=(
            jax.ShapeDtypeStruct((tokens, width), BF16),
            jax.ShapeDtypeStruct((heads, tokens), F32),
        ),
        in_specs=[smem] + [vmem] * 5,
        out_specs=(vmem, vmem),
        scratch_shapes=[
            pltpu.VMEM((window // BK, heads, BQ, BK), F32),
            pltpu.VMEM((heads, BQ, 128), F32),
            pltpu.VMEM((heads, BQ, 128), F32),
            pltpu.VMEM((heads, BQ, HEAD_DIM), F32),
        ],
        compiler_params=pltpu.CompilerParams(vmem_limit_bytes=VMEM_LIMIT),
        name="attend",
    )(rng, segq, segk, q, k, v)


def attend_back_kernel(
    rng, segq, segk, lse, delta, q, do, k, v, dq, dk, dv, dq_acc, dk_acc, dv_acc
):
    heads = q.shape[1] // HEAD_DIM
    scale = HEAD_DIM**-0.5
    coef = scale * LOG2E
    dk_acc[...] = jnp.zeros(dk_acc.shape, F32)
    dv_acc[...] = jnp.zeros(dv_acc.shape, F32)
    for qb in range(q.shape[0] // BQ):
        rows = slice(qb * BQ, (qb + 1) * BQ)
        lo = rng[0, qb]
        hi = rng[1, qb]
        sq = segq[:, rows]
        dq_acc[...] = jnp.zeros(dq_acc.shape, F32)

        @pl.loop(lo, hi)
        def _(kc):
            ks = pl.ds(pl.multiple_of(kc * BK, BK), BK)
            bias = jnp.where(segk[ks, :] == sq, 0.0, MASKED)
            for h in range(heads):
                cols = slice(h * HEAD_DIM, (h + 1) * HEAD_DIM)
                qh = q[rows, cols]
                doh = do[rows, cols]
                kh = k[ks, cols]
                s = dot_nt(kh, qh) * coef + (bias - lse[h : h + 1, rows])
                p = jnp.exp2(s)
                dp = dot_nt(v[ks, cols], doh)
                ds = (p * (dp - delta[h : h + 1, rows])).astype(BF16)
                dv_acc[ks, cols] += dot_nn(p.astype(BF16), doh)
                dk_acc[ks, cols] += dot_nn(ds, qh)
                dq_acc[:, cols] += dot_tn(ds, kh)

        dq[rows, :] = (dq_acc[...] * scale).astype(BF16)
    dk[...] = (dk_acc[...] * scale).astype(BF16)
    dv[...] = dv_acc[...].astype(BF16)


def attend_back(rng, segq, segk, lse, delta, q, do, k, v):
    tokens, width = q.shape
    window = k.shape[0]
    smem = pl.BlockSpec(memory_space=pltpu.SMEM)
    vmem = pl.BlockSpec(memory_space=pltpu.VMEM)
    return pl.pallas_call(
        attend_back_kernel,
        out_shape=(
            jax.ShapeDtypeStruct((tokens, width), BF16),
            jax.ShapeDtypeStruct((window, width), BF16),
            jax.ShapeDtypeStruct((window, width), BF16),
        ),
        in_specs=[smem] + [vmem] * 8,
        out_specs=(vmem, vmem, vmem),
        scratch_shapes=[
            pltpu.VMEM((BQ, width), F32),
            pltpu.VMEM((window, width), F32),
            pltpu.VMEM((window, width), F32),
        ],
        compiler_params=pltpu.CompilerParams(vmem_limit_bytes=VMEM_LIMIT),
        name="attend_back",
    )(rng, segq, segk, lse, delta, q, do, k, v)


def make_body(n_seq, n_tp):
    def shift(x, by):
        pairs = [(i, i + by) for i in range(n_tp) if 0 <= i + by < n_tp]
        return lax.ppermute(x, "tp", pairs)

    def gather_cols(parts):
        m = len(parts)
        rows, width = parts[0].shape
        piece = rows // n_seq
        mine = lax.axis_index("seq") * piece
        cut = jnp.concatenate([lax.dynamic_slice_in_dim(p, mine, piece, 0) for p in parts], axis=1)
        full = lax.all_gather(cut, ("seq", "tp"), axis=0)
        full = full.reshape(n_seq, n_tp, piece, m, width)
        full = jnp.transpose(full, (3, 0, 2, 1, 4)).reshape(m, rows, n_tp * width)
        return [full[i] for i in range(m)]

    def reduce_cols(grads):
        m = len(grads)
        rows, cols = grads[0].shape
        piece, width = rows // n_seq, cols // n_tp
        x = jnp.stack(grads).astype(BF16).reshape(m, n_seq, piece, n_tp, width)
        x = jnp.transpose(x, (1, 3, 2, 0, 4)).reshape(n_seq, n_tp, piece, m * width)
        x = lax.psum_scatter(x, "seq", scatter_dimension=0, tiled=True)
        x = lax.psum_scatter(x, "tp", scatter_dimension=1, tiled=True)
        x = lax.all_gather(x, "seq", axis=0, tiled=True)
        x = x.reshape(rows, m, width).astype(F32)
        return [x[:, i] for i in range(m)]

    def body(
        inputs,
        segment_ids,
        row_lengths,
        norm1_gain,
        norm1_shift,
        w_query,
        w_key,
        w_value,
        b_query,
        b_value,
        w_out,
        b_out,
        norm2_gain,
        norm2_shift,
        w_up,
        b_up,
        w_down,
        b_down,
        out_grad,
    ):
        tokens, width = inputs.shape
        halo = tokens
        heads = width // HEAD_DIM
        tp_at = lax.axis_index("tp")

        wq, wk, wv = gather_cols([w_query, w_key, w_value])
        wo_t, wup, wdn_t = gather_cols([w_out.T, w_up, w_down.T])
        wo, wdn = wo_t.T, wdn_t.T
        biases = lax.all_gather(jnp.stack([b_query, b_value, b_up]), "tp", axis=1, tiled=True)
        bq, bv, bup = biases[0], biases[1], biases[2]

        left = shift(inputs, 1)
        right = shift(inputs, -1)
        window = jnp.concatenate([left, inputs, right], axis=0)
        position = jnp.arange(ROW_LEN, dtype=jnp.int32)
        numbers = jnp.where(position < row_lengths[0], segment_ids[0], 4096 + position)
        numbers = jnp.concatenate(
            [jnp.full((halo,), -1, jnp.int32), numbers, jnp.full((halo,), 1 << 20, jnp.int32)]
        )
        seg_win = lax.dynamic_slice_in_dim(numbers, tp_at * tokens, tokens + 2 * halo, 0)
        seg_mine = seg_win[halo : halo + tokens]
        first = seg_mine[::BQ]
        last = seg_mine[BQ - 1 :: BQ]
        low = jnp.sum((seg_win[None, :] < first[:, None]).astype(jnp.int32), axis=1)
        high = jnp.sum((seg_win[None, :] <= last[:, None]).astype(jnp.int32), axis=1)
        rng = jnp.stack([low // BK, (high + BK - 1) // BK])

        wide = window.astype(F32)
        hat1, rstd1 = normalise(wide)
        first_low = (hat1 * norm1_gain + norm1_shift).astype(BF16)
        own = first_low[halo : halo + tokens]
        q = (dot_nn(own, wq) + bq).astype(BF16)
        k = dot_nn(first_low, wk).astype(BF16)
        v = (dot_nn(first_low, wv) + bv).astype(BF16)
        mixed, lse = attend(rng, seg_mine[:, None], seg_win[None, :], q, k, v)

        wide_in = wide[halo : halo + tokens]
        first_resid = wide_in + dot_nn(mixed, wo) + b_out
        hat2, rstd2 = normalise(first_resid)
        second_low = (hat2 * norm2_gain + norm2_shift).astype(BF16)
        up = dot_nn(second_low, wup) + bup
        hidden_act, pull_gelu = jax.vjp(lambda u: jax.nn.gelu(u, approximate=False), up)
        hidden = hidden_act.astype(BF16)
        output = (first_resid + dot_nn(hidden, wdn) + b_down).astype(BF16)

        grad_out = out_grad.astype(F32)
        g_wdn = dot_tn(hidden, out_grad)
        g_up = pull_gelu(dot_nt(out_grad, wdn))[0].astype(BF16)
        g_wup = dot_tn(second_low, g_up)
        g_second = dot_nt(g_up, wup)
        g_resid = grad_out + norm_back(g_second, hat2, rstd2, norm2_gain)
        resid_low = g_resid.astype(BF16)
        g_wo = dot_tn(mixed, resid_low)
        g_mixed = dot_nt(resid_low, wo).astype(BF16)
        delta = jnp.sum(
            (g_mixed.astype(F32) * mixed.astype(F32)).reshape(tokens, heads, HEAD_DIM), axis=2
        ).T
        out_wo_t, out_wup, out_wdn_t = reduce_cols([g_wo.T, g_wup, g_wdn.T])

        dq, dk, dv = attend_back(
            rng, seg_mine[None, :], seg_win[:, None], lse, delta, q, g_mixed, k, v
        )
        g_wq = dot_tn(own, dq)
        g_wk = dot_tn(first_low, dk)
        g_wv = dot_tn(first_low, dv)
        out_wq, out_wk, out_wv = reduce_cols([g_wq, g_wk, g_wv])
        dx = dot_nt(dk, wk) + dot_nt(dv, wv)
        to_left = shift(dx[:halo].astype(BF16), -1)
        to_right = shift(dx[halo + tokens :].astype(BF16), 1)
        g_first = dx[halo : halo + tokens] + dot_nt(dq, wq)
        g_first = g_first + to_left.astype(F32) + to_right.astype(F32)
        hat_own = hat1[halo : halo + tokens]
        rstd_own = rstd1[halo : halo + tokens]
        g_inputs = (g_resid + norm_back(g_first, hat_own, rstd_own, norm1_gain)).astype(BF16)

        def over_tokens(x):
            return jnp.sum(x.astype(F32), axis=0)

        vectors = jnp.stack(
            [
                over_tokens(g_first * hat_own),
                over_tokens(g_first),
                over_tokens(dq),
                over_tokens(dv),
                over_tokens(g_resid),
                over_tokens(g_second * hat2),
                over_tokens(g_second),
                over_tokens(g_up),
                over_tokens(grad_out),
            ]
        )
        vectors = lax.psum(vectors, ("seq", "tp"))
        n1g, n1s, g_bq, g_bv, g_bo, n2g, n2s, g_bup, g_bdn = [vectors[i] for i in range(9)]

        def shard(x):
            size = width // n_tp
            return lax.dynamic_slice_in_dim(x, tp_at * size, size, 0)

        return (
            output,
            g_inputs,
            n1g,
            n1s,
            out_wq,
            out_wk,
            out_wv,
            shard(g_bq),
            shard(g_bv),
            out_wo_t.T,
            g_bo,
            n2g,
            n2s,
            out_wup,
            shard(g_bup),
            out_wdn_t.T,
            g_bdn,
        )

    return body


def solution(mesh):
    tok = P(("seq", "tp"), None)
    col, row, vec, rep = P(None, "tp"), P("tp", None), P("tp"), P()
    in_specs = (
        tok, P("seq", None), P("seq"), rep, rep, col, col, col, vec, vec,
        row, rep, rep, rep, col, vec, row, rep, tok,
    )
    out_specs = (
        tok, tok, rep, rep, col, col, col, vec, vec,
        row, rep, rep, rep, col, vec, row, rep,
    )
    body = make_body(mesh.shape["seq"], mesh.shape["tp"])
    return jax.shard_map(body, mesh=mesh, in_specs=in_specs, out_specs=out_specs, check_vma=False)
```

```python
import functools
import math

import jax
import jax.numpy as jnp
from jax import lax
from jax.experimental import pallas as pl
from jax.experimental.pallas import tpu as pltpu
from jax.sharding import PartitionSpec as P

HEAD_DIM = 128
ROW_LEN = 2048
NORM_EPS = 1e-05
MASKED = -1000000000.0
LOG2E = 1.4426950408889634
SHARD = 256
TILE = 256
BQ = 256
BK = 128
FAR = 256
ROWS = 32
F32 = jnp.float32
BF16 = jnp.bfloat16
VMEM_LIMIT = 56 * 1024 * 1024


def dot_nn(a, b):
    return lax.dot_general(a, b, (((1,), (0,)), ((), ())), preferred_element_type=F32)


def dot_nt(a, b):
    return lax.dot_general(a, b, (((1,), (1,)), ((), ())), preferred_element_type=F32)


def dot_tn(a, b):
    return lax.dot_general(a, b, (((0,), (0,)), ((), ())), preferred_element_type=F32)


def normalise(x):
    centre = x - jnp.mean(x, axis=-1, keepdims=True)
    rstd = lax.rsqrt(jnp.mean(centre * centre, axis=-1, keepdims=True) + NORM_EPS)
    return centre * rstd, rstd


def norm_back(grad, hat, rstd, gain):
    t = gain * grad
    mean_t = jnp.mean(t, axis=-1, keepdims=True)
    mean_th = jnp.mean(t * hat, axis=-1, keepdims=True)
    return (t - mean_t - hat * mean_th) * rstd


def load_weights(meta, own, off, per, pieces, kinds, dst, sems):
    s, t = meta[0], meta[1]
    n_tp = dst[0].shape[0] // SHARD
    size = pieces[0].shape[1]
    for m, kind in enumerate(kinds):
        mine = pl.ds(pl.multiple_of(t * per, per), per)
        if kind == "col":
            source, target = own[m].at[:, off : off + per], dst[m].at[:, mine]
        else:
            source, target = own[m], dst[m].at[mine, :]
        pltpu.make_async_copy(source, target, sems.at[m]).start()
        for j, piece in enumerate(pieces):
            at = pl.ds(pl.multiple_of((s ^ j) * size, size), size)
            for r in range(n_tp - 1):
                u = pl.multiple_of(lax.rem(t + r + 1, n_tp) * per, per)
                if kind == "col":
                    pltpu.make_async_copy(
                        piece.at[r, :, m * per : (m + 1) * per],
                        dst[m].at[at, pl.ds(u, per)],
                        sems.at[m],
                    ).start()
                else:
                    for i in range(per // size):
                        c = m * per + i * size
                        pltpu.make_async_copy(
                            piece.at[r, :, c : c + size],
                            dst[m].at[pl.ds(u + i * size, size), at],
                            sems.at[m],
                        ).start()

    def wait(m):
        pltpu.make_async_copy(dst[m], dst[m], sems.at[m]).wait()

    return wait


def put_piece(keep, send, j, t, cols, value):
    jj = j >> 1
    even = (j & 1) == 0

    @pl.when(even)
    def _():
        keep[jj, t, :, cols] = value

    @pl.when(jnp.logical_not(even))
    def _():
        send[jj, t, :, cols] = value


def put_col_rows(keep, send, s, row, m, per, tile):
    size = keep.shape[2]
    for i in range(tile.shape[0] // size):
        j = (row // size + i) ^ s
        for t in range(tile.shape[1] // per):
            part = tile[i * size : (i + 1) * size, t * per : (t + 1) * per]
            put_piece(keep, send, j, t, slice(m * per, (m + 1) * per), part)


def put_row_rows(keep, send, s, t, m, tile):
    size = keep.shape[2]
    for p in range(tile.shape[1] // size):
        j = p ^ s
        for i in range(SHARD // size):
            at = m * SHARD + i * size
            part = tile[i * size : (i + 1) * size, p * size : (p + 1) * size]
            put_piece(keep, send, j, t, slice(at, at + size), part)


def call(kernel, outs, ins, scratch, name, smem=0, anys=0, out_anys=0, gflop=50):
    spaces = [pltpu.SMEM] * smem + [pltpu.VMEM] * (len(ins) - smem - anys) + [pl.ANY] * anys
    out_spaces = [pltpu.VMEM] * (len(outs) - out_anys) + [pl.ANY] * out_anys
    return pl.pallas_call(
        kernel,
        out_shape=tuple(jax.ShapeDtypeStruct(*o) for o in outs),
        in_specs=[pl.BlockSpec(memory_space=m) for m in spaces],
        out_specs=tuple(pl.BlockSpec(memory_space=m) for m in out_spaces),
        scratch_shapes=scratch,
        compiler_params=pltpu.CompilerParams(vmem_limit_bytes=VMEM_LIMIT),
        cost_estimate=pl.CostEstimate(
            flops=gflop * 10**9, bytes_accessed=1000000, transcendentals=0
        ),
        name=name,
    )(*ins)


def attend(rng, segq, segk, q, k, v, mixed, lse, s_scr, m_scr, l_scr, acc):
    heads = q.shape[1] // HEAD_DIM
    coef = HEAD_DIM**-0.5 * LOG2E
    for qb in range(q.shape[0] // BQ):
        rows = slice(qb * BQ, (qb + 1) * BQ)
        lo = rng[0, qb]
        hi = rng[1, qb]
        sq = segq[rows, :]
        m_scr[...] = jnp.full(m_scr.shape, -3e38, F32)
        l_scr[...] = jnp.zeros(l_scr.shape, F32)
        acc[...] = jnp.zeros(acc.shape, F32)

        @pl.loop(lo, hi)
        def _(kc):
            ks = pl.multiple_of(kc * BK, BK)
            bias = jnp.where(sq == segk[:, pl.ds(ks, BK)], 0.0, MASKED)
            for h in range(heads):
                cols = slice(h * HEAD_DIM, (h + 1) * HEAD_DIM)
                s = dot_nt(q[rows, cols], k[pl.ds(ks, BK), cols]) * coef + bias
                s_scr[kc, h] = s
                m_scr[h] = jnp.maximum(m_scr[h], s)

        for h in range(heads):
            m_scr[h] = jnp.broadcast_to(jnp.max(m_scr[h], axis=1, keepdims=True), (BQ, BK))

        @pl.loop(lo, hi)
        def _(kc):
            ks = pl.multiple_of(kc * BK, BK)
            for h in range(heads):
                cols = slice(h * HEAD_DIM, (h + 1) * HEAD_DIM)
                p = jnp.exp2(s_scr[kc, h] - m_scr[h])
                l_scr[h] += p
                acc[h] += dot_nn(p.astype(BF16), v[pl.ds(ks, BK), cols])

        for h in range(heads):
            cols = slice(h * HEAD_DIM, (h + 1) * HEAD_DIM)
            total = jnp.broadcast_to(jnp.sum(l_scr[h], axis=1, keepdims=True), (BQ, BK))
            mixed[rows, cols] = (acc[h] / total).astype(BF16)
            log_total = m_scr[h] + jnp.log2(total)
            for r in range(0, BQ, BK):
                part = jnp.transpose(log_total[r : r + BK])
                lse[h : h + 1, qb * BQ + r : qb * BQ + r + BK] = part[:1]


def attend_scratch(window, heads):
    return [
        pltpu.VMEM((window // BK, heads, BQ, BK), F32),
        pltpu.VMEM((heads, BQ, BK), F32),
        pltpu.VMEM((heads, BQ, BK), F32),
        pltpu.VMEM((heads, BQ, HEAD_DIM), F32),
    ]


def attend_back(rng, segq, segk, lse, delta, q, do, k, v, dq, dk_acc, dv_acc, dq_acc):
    heads = q.shape[1] // HEAD_DIM
    scale = HEAD_DIM**-0.5
    coef = scale * LOG2E
    for qb in range(q.shape[0] // BQ):
        rows = slice(qb * BQ, (qb + 1) * BQ)
        lo = rng[0, qb]
        hi = rng[1, qb]
        sq = segq[:, rows]
        dq_acc[...] = jnp.zeros(dq_acc.shape, F32)

        @pl.loop(lo, hi)
        def _(kc):
            ks = pl.ds(pl.multiple_of(kc * BK, BK), BK)
            bias = jnp.where(segk[ks, :] == sq, 0.0, MASKED)
            for h in range(heads):
                cols = slice(h * HEAD_DIM, (h + 1) * HEAD_DIM)
                qh = q[rows, cols]
                doh = do[rows, cols]
                kh = k[ks, cols]
                p = jnp.exp2(dot_nt(kh, qh) * coef + (bias - lse[h : h + 1, rows]))
                dp = dot_nt(v[ks, cols], doh)
                ds = (p * (dp - delta[h : h + 1, rows])).astype(BF16)
                dv_acc[ks, cols] += dot_nn(p.astype(BF16), doh)
                dk_acc[ks, cols] += dot_nn(ds, qh)
                dq_acc[:, cols] += dot_tn(ds, kh)

        dq[rows, :] = (dq_acc[...] * scale).astype(BF16)


def used_chunks(rng):
    window = 3 * BQ * rng.shape[1]
    before = rng[0, 0] < (window // 3 - FAR) // BK
    after = rng[1, rng.shape[1] - 1] > (2 * window // 3 + FAR) // BK
    return before, after


def forward_kernel(
    n_pieces, meta, rng, segq, segk, left, own, right, gain, shift, bq, bv, w0, w1, w2, *rest
):
    pieces = rest[:n_pieces]
    mixed, lse, q_out, k_out, v_out, low_out = rest[n_pieces : n_pieces + 6]
    q, k, v, low, wq, wk, wv, s_scr, m_scr, l_scr, acc, sems, out_sems = rest[n_pieces + 6 :]
    wait = load_weights(meta, (w0, w1, w2), 0, SHARD, pieces, ("col",) * 3, (wq, wk, wv), sems)
    tokens = own.shape[0]
    for base, src in ((0, left), (tokens, own), (2 * tokens, right)):

        @pl.loop(0, tokens // ROWS, unroll=2)
        def _(i):
            at = pl.multiple_of(i * ROWS, ROWS)
            hat, _ = normalise(src[pl.ds(at, ROWS), :].astype(F32))
            low[pl.ds(base + at, ROWS), :] = (hat * gain[...] + shift[...]).astype(BF16)

    middle = slice(tokens, 2 * tokens)
    near = slice(tokens - FAR, 2 * tokens + FAR)
    before, after = used_chunks(rng)

    def out_copy(i, src, dst):
        return pltpu.make_async_copy(src, dst, out_sems.at[i])

    outs = ((low, low_out), (q, q_out), (k, k_out), (v, v_out))
    out_copy(0, *outs[0]).start()
    wait(0)
    q[...] = (dot_nn(low[middle, :], wq[...]) + bq[...]).astype(BF16)
    out_copy(1, *outs[1]).start()
    wait(1)
    k[near, :] = dot_nn(low[near, :], wk[...]).astype(BF16)
    wait(2)
    v[near, :] = (dot_nn(low[near, :], wv[...]) + bv[...]).astype(BF16)
    for used, rows in ((before, slice(0, tokens - FAR)), (after, slice(2 * tokens + FAR, None))):

        @pl.when(used)
        def _():
            k[rows, :] = dot_nn(low[rows, :], wk[...]).astype(BF16)
            v[rows, :] = (dot_nn(low[rows, :], wv[...]) + bv[...]).astype(BF16)

    out_copy(2, *outs[2]).start()
    out_copy(3, *outs[3]).start()
    attend(rng, segq, segk, q, k, v, mixed, lse, s_scr, m_scr, l_scr, acc)
    for i in range(4):
        out_copy(i, *outs[i]).wait()


def forward(meta, rng, segq, segk, left, own, right, gain, shift, bq, bv, shards, pieces):
    tokens, width = own.shape
    ins = [meta, rng, segq, segk, left, own, right, gain, shift, bq, bv, *shards, *pieces]
    whole = pltpu.VMEM((width, width), BF16)
    window = 3 * tokens
    slim, wide = (tokens, width), (window, width)
    heads = width // HEAD_DIM
    return call(
        functools.partial(forward_kernel, len(pieces)),
        [(slim, BF16), ((heads, tokens), F32), (slim, BF16)] + [(wide, BF16)] * 3,
        ins,
        [pltpu.VMEM(x, BF16) for x in (slim, wide, wide, wide)]
        + [whole, whole, whole]
        + attend_scratch(window, heads)
        + [pltpu.SemaphoreType.DMA((3,)), pltpu.SemaphoreType.DMA((4,))],
        "forward_attention",
        smem=2,
        anys=3 + len(pieces),
        out_anys=4,
    )


def feed_kernel(n_pieces, meta, mixed, inputs, dout, bo, gain, shift, bup, bdn, w0, w1, w2, *rest):
    pieces = rest[:n_pieces]
    (output, g_resid, g_mixed, delta, keep, send, sums) = rest[n_pieces : n_pieces + 7]
    wo, wup, wdn, resid, hat, rstd, second, hidden, g_up, g_sec, low, sems = rest[n_pieces + 7 :]
    wait = load_weights(
        meta, (w0, w1, w2), 0, SHARD, pieces, ("row", "col", "row"), (wo, wup, wdn), sems
    )
    s = meta[0]
    tokens, width = inputs.shape
    tiles = width // TILE
    sums[...] = jnp.zeros(sums.shape, F32)
    wait(0)
    resid[...] = inputs[...].astype(F32) + dot_nn(mixed[...], wo[...]) + bo[...]

    @pl.loop(0, tokens // ROWS, unroll=2)
    def _(i):
        rows = pl.ds(pl.multiple_of(i * ROWS, ROWS), ROWS)
        h, r = normalise(resid[rows, :])
        hat[rows, :] = h
        rstd[rows, :] = jnp.broadcast_to(r, (ROWS, 128))
        second[rows, :] = (h * gain[...] + shift[...]).astype(BF16)

    wait(1)
    wait(2)
    for n in range(tiles):
        cols = slice(n * TILE, (n + 1) * TILE)
        up = dot_nn(second[...], wup[:, cols]) + bup[:, cols]
        d_hidden = dot_nt(dout[...], wdn[cols, :])
        phi = 0.5 + 0.5 * lax.erf(up * (0.5**0.5))
        hidden[:, cols] = (up * phi).astype(BF16)
        slope = phi + up * (jnp.exp(-0.5 * up * up) * (0.5 / math.pi) ** 0.5)
        grad = (d_hidden * slope).astype(BF16)
        g_up[:, cols] = grad
        sums[3:4, cols] = jnp.sum(grad.astype(F32), axis=0, keepdims=True)
    g_sec[...] = dot_nt(g_up[...], wup[...])
    output[...] = (resid[...] + dot_nn(hidden[...], wdn[...]) + bdn[...]).astype(BF16)
    for r in range(tiles):
        rows = slice(r * TILE, (r + 1) * TILE)
        tile = dot_tn(hidden[:, rows], dout[...]).astype(BF16)
        put_row_rows(keep, send, s, r, 2, tile)
        tile = dot_tn(second[:, rows], g_up[...]).astype(BF16)
        put_col_rows(keep, send, s, r * TILE, 1, SHARD, tile)

    @pl.loop(0, tokens // ROWS, unroll=2)
    def _(i):
        rows = pl.ds(pl.multiple_of(i * ROWS, ROWS), ROWS)
        h, g = hat[rows, :], g_sec[rows, :]
        d = dout[rows, :].astype(F32)
        res = d + norm_back(g, h, rstd[rows, :1], gain[...])
        g_resid[rows, :] = res
        low[rows, :] = res.astype(BF16)
        for n, x in enumerate((res, g * h, g)):
            sums[n : n + 1, :] += jnp.sum(x, axis=0, keepdims=True)
        sums[4:5, :] += jnp.sum(d, axis=0, keepdims=True)

    for r in range(tiles):
        rows = slice(r * TILE, (r + 1) * TILE)
        put_row_rows(keep, send, s, r, 0, dot_tn(mixed[:, rows], low[...]).astype(BF16))
    ones = jnp.ones((8, HEAD_DIM), BF16)
    for n in range(tiles):
        cols = slice(n * TILE, (n + 1) * TILE)
        grad = dot_nt(low[...], wo[cols, :]).astype(BF16)
        g_mixed[:, cols] = grad
        prod = grad.astype(F32) * mixed[:, cols].astype(F32)
        high = prod.astype(BF16)
        rest_of = (prod - high.astype(F32)).astype(BF16)
        for i in range(TILE // HEAD_DIM):
            part = slice(i * HEAD_DIM, (i + 1) * HEAD_DIM)
            total = dot_nt(ones, high[:, part]) + dot_nt(ones, rest_of[:, part])
            h = n * (TILE // HEAD_DIM) + i
            delta[h : h + 1, :] = total[:1]


def feed_forward(meta, mixed, inputs, dout, bo, gain, shift, bup, bdn, shards, pieces):
    tokens, width = inputs.shape
    half = max(len(pieces) // 2, 1)
    n_tp = width // SHARD
    grads = ((half, n_tp, width // len(pieces), 3 * SHARD), BF16)
    ins = [meta, mixed, inputs, dout, bo, gain, shift, bup, bdn, *shards, *pieces]
    whole = pltpu.VMEM((width, width), BF16)
    wide = pltpu.VMEM((tokens, width), F32)
    slim = pltpu.VMEM((tokens, width), BF16)
    return call(
        functools.partial(feed_kernel, len(pieces)),
        [
            ((tokens, width), BF16),
            ((tokens, width), F32),
            ((tokens, width), BF16),
            ((width // HEAD_DIM, tokens), F32),
            grads,
            grads,
            ((8, width), F32),
        ],
        ins,
        [whole, whole, whole, wide, wide, pltpu.VMEM((tokens, 128), F32)]
        + [slim, slim, slim, wide, slim, pltpu.SemaphoreType.DMA((3,))],
        "feed_forward",
        smem=1,
        anys=3 + len(pieces),
    )


def backward_kernel(
    n_pieces, meta, rng, segq, segk, lse, delta, q, do, k, v, low, w0, w1, w2, *rest
):
    pieces = rest[:n_pieces]
    left, own, right, keep, send, sums = rest[n_pieces : n_pieces + 6]
    wq, wk, wv, dq, dk, dv, dk_acc, dv_acc, dq_acc, sems = rest[n_pieces + 6 :]
    wait = load_weights(meta, (w0, w1, w2), 0, SHARD, pieces, ("col",) * 3, (wq, wk, wv), sems)
    s = meta[0]
    tokens, width = q.shape
    near = slice(tokens - FAR, 2 * tokens + FAR)
    middle = slice(tokens, 2 * tokens)
    before, after = used_chunks(rng)
    distant = jnp.logical_or(before, after)
    scale = HEAD_DIM**-0.5

    def on_rows(rows):
        def zero():
            dk_acc[rows, :] = jnp.zeros((rows.stop - rows.start, width), F32)
            dv_acc[rows, :] = jnp.zeros((rows.stop - rows.start, width), F32)

        def narrow():
            dk[rows, :] = (dk_acc[rows, :] * scale).astype(BF16)
            dv[rows, :] = dv_acc[rows, :].astype(BF16)

        return zero, narrow

    parts = [on_rows(near), on_rows(slice(0, tokens - FAR))]
    parts.append(on_rows(slice(2 * tokens + FAR, 3 * tokens)))
    parts[0][0]()
    pl.when(distant)(parts[1][0])
    pl.when(distant)(parts[2][0])
    attend_back(rng, segq, segk, lse, delta, q, do, k, v, dq, dk_acc, dv_acc, dq_acc)
    parts[0][1]()
    pl.when(distant)(parts[1][1])
    pl.when(distant)(parts[2][1])

    sums[...] = jnp.zeros(sums.shape, F32)
    sums[0:1, :] = jnp.sum(dq[...].astype(F32), axis=0, keepdims=True)

    def weight_grads(rows):
        sums[1:2, :] = jnp.sum(dv[rows, :].astype(F32), axis=0, keepdims=True)
        for r in range(width // TILE):
            cols = slice(r * TILE, (r + 1) * TILE)
            for m, (x, g) in enumerate(
                ((low[middle, cols], dq[...]), (low[rows, cols], dk[rows, :]),
                 (low[rows, cols], dv[rows, :]))
            ):
                put_col_rows(keep, send, s, r * TILE, m, SHARD, dot_tn(x, g).astype(BF16))

    pl.when(distant)(lambda: weight_grads(slice(0, 3 * tokens)))
    pl.when(jnp.logical_not(distant))(lambda: weight_grads(near))

    for m in range(3):
        wait(m)

    def halo_grads(out, to, rows):
        out[to, :] = (dot_nt(dk[rows, :], wk[...]) + dot_nt(dv[rows, :], wv[...])).astype(BF16)

    for out, used, far_to, near_to, base in (
        (left, before, slice(0, tokens - FAR), slice(tokens - FAR, tokens), 0),
        (right, after, slice(FAR, tokens), slice(0, FAR), 2 * tokens),
    ):
        halo_grads(out, near_to, slice(base + near_to.start, base + near_to.stop))

        @pl.when(used)
        def _():
            halo_grads(out, far_to, slice(base + far_to.start, base + far_to.stop))

        @pl.when(jnp.logical_not(used))
        def _():
            out[far_to, :] = jnp.zeros((tokens - FAR, width), BF16)

    own[...] = (
        dot_nt(dk[middle, :], wk[...])
        + dot_nt(dv[middle, :], wv[...])
        + dot_nt(dq[...], wq[...])
    )


def backward(meta, rng, segq, segk, lse, delta, q, do, k, v, low, shards, pieces):
    tokens, width = q.shape
    window = 3 * tokens
    grads = ((max(len(pieces) // 2, 1), width // SHARD, width // len(pieces), 3 * SHARD), BF16)
    whole = pltpu.VMEM((width, width), BF16)
    slim, wide = (tokens, width), (window, width)
    return call(
        functools.partial(backward_kernel, len(pieces)),
        [(slim, BF16), (slim, F32), (slim, BF16), grads, grads, ((8, width), F32)],
        [meta, rng, segq, segk, lse, delta, q, do, k, v, low, *shards, *pieces],
        [whole, whole, whole, pltpu.VMEM(slim, BF16), pltpu.VMEM(wide, BF16)]
        + [pltpu.VMEM(wide, BF16), pltpu.VMEM(wide, F32), pltpu.VMEM(wide, F32)]
        + [pltpu.VMEM((BQ, width), F32), pltpu.SemaphoreType.DMA((3,))],
        "backward_attention",
        smem=2,
        anys=3 + len(pieces),
    )


def last_kernel(inputs, g_resid, own, from_left, from_right, gain, g_inputs, sums):
    sums[...] = jnp.zeros(sums.shape, F32)

    @pl.loop(0, inputs.shape[0] // ROWS, unroll=2)
    def _(i):
        rows = pl.ds(pl.multiple_of(i * ROWS, ROWS), ROWS)
        hat, rstd = normalise(inputs[rows, :].astype(F32))
        g = own[rows, :] + from_left[rows, :].astype(F32) + from_right[rows, :].astype(F32)
        g_inputs[rows, :] = (g_resid[rows, :] + norm_back(g, hat, rstd, gain[...])).astype(BF16)
        sums[0:1, :] += jnp.sum(g * hat, axis=0, keepdims=True)
        sums[1:2, :] += jnp.sum(g, axis=0, keepdims=True)


def last_step(inputs, g_resid, own, from_left, from_right, gain):
    return call(
        last_kernel,
        [(inputs.shape, BF16), ((8, inputs.shape[1]), F32)],
        [inputs, g_resid, own, from_left, from_right, gain],
        [],
        "input_norm_grads",
    )


def lay_out_kernel(kinds, n_pieces, meta, *rest):
    pieces, outs = rest[:n_pieces], rest[n_pieces:]
    s = meta[0]
    size = pieces[0].shape[0]
    for j, piece in enumerate(pieces):
        at = pl.ds(pl.multiple_of((s ^ j) * size, size), size)
        for m, kind in enumerate(kinds):
            if kind == "col":
                outs[m][at, :] = piece[:, m * SHARD : (m + 1) * SHARD].astype(F32)
            else:
                for i in range(SHARD // size):
                    c = m * SHARD + i * size
                    outs[m][i * size : (i + 1) * size, at] = piece[:, c : c + size].astype(F32)


def lay_out(meta, pieces, kinds):
    width = pieces[0].shape[0] * len(pieces)
    shapes = {"col": (width, SHARD), "row": (SHARD, width)}
    return call(
        functools.partial(lay_out_kernel, kinds, len(pieces)),
        [(shapes[kind], F32) for kind in kinds],
        [meta, *pieces],
        [],
        "lay_out_grads",
        smem=1,
    )


def make_body(n_seq, n_tp):
    inner = min(n_seq, 8)
    outer = n_seq // inner
    half = inner // 2
    masks = [2 * jj for jj in range(1, half)]

    def shift(x, by):
        pairs = [(i, i + by) for i in range(n_tp) if 0 <= i + by < n_tp]
        return lax.ppermute(x, "tp", pairs)

    def swap(x, mask):
        return lax.ppermute(x, "seq", [(i, i ^ mask) for i in range(n_seq)])

    def cut(w, kind, s):
        size = (w.shape[0] if kind == "col" else w.shape[1]) // inner
        if kind == "col":
            return lax.dynamic_slice_in_dim(w, s * size, size, 0)
        part = lax.dynamic_slice_in_dim(w, s * size, size, 1)
        return jnp.concatenate([part[i : i + size] for i in range(0, part.shape[0], size)], axis=1)

    def over_tp(shards, kinds, biases, s, t, after):
        piece = jnp.concatenate([cut(w, k, s) for w, k in zip(shards, kinds)], axis=1)
        parts = []
        rest = jnp.concatenate(biases)
        for _ in range(3):
            part = rest.astype(BF16)
            rest = rest - part.astype(F32)
            parts.append(part)
        rows = jnp.stack(parts + [jnp.zeros_like(parts[0])] * 13)
        piece = jnp.concatenate([piece, rows], axis=0)
        block = jnp.broadcast_to(piece[None], (n_tp, *piece.shape))
        if after is not None:
            block, _ = lax.optimization_barrier((block, after))
        got = lax.all_to_all(block, "tp", 0, 0, tiled=True)
        size = piece.shape[0] - 16
        others = jnp.stack(
            [lax.dynamic_index_in_dim(got, lax.rem(t + r + 1, n_tp), 0, keepdims=False)[:size]
             for r in range(n_tp - 1)]
        )
        whole = jnp.sum(got[:, size : size + 3].astype(F32), axis=1)
        n = len(biases)
        whole = [b.reshape(1, -1) for b in jnp.split(whole, [SHARD * i for i in range(1, n)], axis=1)]
        return others, whole, got

    def from_chips(x):
        return [x] + [swap(x, mask) for mask in masks]

    def from_cores(even):
        odd = [swap(e, 1) for e in even]
        return [e for pair in zip(even, odd) for e in pair]

    def over_cores(keep, send):
        got = swap(send, 1)
        return [(keep[jj].astype(F32) + got[jj].astype(F32)).astype(BF16) for jj in range(half)]

    def over_chips(sums):
        moved = [swap(sums[jj], 2 * jj) for jj in range(1, half)]
        total = sums[0].astype(F32)
        for x in moved:
            total = total + x.astype(F32)
        total = total.astype(BF16)
        if outer > 1:
            groups = [[i + inner * o for o in range(outer)] for i in range(inner)]
            total = lax.psum(total, "seq", axis_index_groups=groups)
        return total

    def own_shard(total):
        got = lax.all_to_all(total, "tp", 0, 0, tiled=True)
        return jnp.sum(got.astype(F32), axis=0).astype(BF16)

    def tie(*xs):
        return lax.optimization_barrier(xs)

    def body(
        inputs, segment_ids, row_lengths, norm1_gain, norm1_shift, w_query, w_key, w_value,
        b_query, b_value, w_out, b_out, norm2_gain, norm2_shift, w_up, b_up, w_down, b_down,
        out_grad,
    ):
        tokens, width = inputs.shape
        halo = tokens
        t = lax.axis_index("tp")
        s = lax.rem(lax.axis_index("seq"), inner)
        meta = jnp.stack([s, t]).astype(jnp.int32)
        attn_w, attn_kinds = [w_query, w_key, w_value], ("col", "col", "col")
        feed_w, feed_kinds = [w_out, w_up, w_down], ("row", "col", "row")

        def row(x):
            return x.reshape(1, -1)

        zero = jnp.zeros_like(b_query)
        attn_z, (bq, _, bv), done = over_tp(
            attn_w, attn_kinds, [b_query, zero, b_value], s, t, None
        )
        inputs_later, _ = lax.optimization_barrier((inputs, done))
        attn_p = from_cores(from_chips(attn_z))
        left = shift(inputs_later, 1)
        right = shift(inputs_later, -1)
        feed_z, (bup, _, _), done = over_tp(feed_w, feed_kinds, [b_up, zero, zero], s, t, done)
        feed_p = from_chips(feed_z)

        position = jnp.arange(ROW_LEN, dtype=jnp.int32)
        numbers = jnp.where(position < row_lengths[0], segment_ids[0], 4096 + position)
        numbers = jnp.concatenate(
            [jnp.full((halo,), -1, jnp.int32), numbers, jnp.full((halo,), 1 << 20, jnp.int32)]
        )
        seg_win = lax.dynamic_slice_in_dim(numbers, t * tokens, tokens + 2 * halo, 0)
        seg_mine = seg_win[halo : halo + tokens]
        first = seg_mine[::BQ]
        last = seg_mine[BQ - 1 :: BQ]
        low = jnp.sum((seg_win[None, :] < first[:, None]).astype(jnp.int32), axis=1)
        high = jnp.sum((seg_win[None, :] <= last[:, None]).astype(jnp.int32), axis=1)
        rng = jnp.stack([low // BK, (high + BK - 1) // BK])

        mixed, lse, q, k, v, first_low = forward(
            meta, rng, seg_mine[:, None], seg_win[None, :], left, inputs, right,
            row(norm1_gain), row(norm1_shift), bq, bv, attn_w, attn_p,
        )
        mixed, *feed_p = tie(mixed, *feed_p)
        feed_p = from_cores(feed_p)
        output, g_resid, g_mixed, delta, keep, send, sums_feed = feed_forward(
            meta, mixed, inputs, out_grad, row(b_out), row(norm2_gain), row(norm2_shift),
            bup, row(b_down), feed_w, feed_p,
        )
        feed_sums = over_cores(keep, send)
        g_mixed, *feed_sums = tie(g_mixed, *feed_sums)
        feed_total = over_chips(feed_sums)
        dx_left, dx_own, dx_right, keep, send, sums_qkv = backward(
            meta, rng, seg_mine[None, :], seg_win[:, None], lse, delta, q, g_mixed, k, v,
            first_low, attn_w, attn_p,
        )
        send, dx_left, dx_right, feed_total = tie(send, dx_left, dx_right, feed_total)
        attn_sums = over_cores(keep, send)
        dx_own, *attn_sums = tie(dx_own, *attn_sums)
        attn_total = over_chips(attn_sums)
        feed_g = own_shard(feed_total)
        from_right = shift(dx_left, -1)
        from_left = shift(dx_right, 1)
        g_inputs, sums_in = last_step(
            inputs, g_resid, dx_own, from_left, from_right, row(norm1_gain)
        )

        vectors = jnp.concatenate([sums_in[:2], sums_qkv[:2], sums_feed[:5]])
        vectors, feed_g = tie(vectors, feed_g)
        n_vec = vectors.shape[0]
        vectors = vectors.reshape(n_seq * n_tp, -1)
        vectors = lax.all_to_all(vectors, ("seq", "tp"), 0, 0, tiled=True)
        vectors = jnp.broadcast_to(jnp.sum(vectors, axis=0, keepdims=True), vectors.shape)
        vectors = lax.all_to_all(vectors, ("seq", "tp"), 0, 0, tiled=True)
        attn_total, vectors = tie(attn_total, vectors)
        attn_g = own_shard(attn_total)
        vectors = vectors.reshape(n_vec, width)
        n1g, n1s, g_bq, g_bv, g_bo, n2g, n2s, g_bup, g_bdn = [vectors[i] for i in range(9)]

        g_wo, g_wup, g_wdn = lay_out(meta, from_cores(from_chips(feed_g)), feed_kinds)
        g_wq, g_wk, g_wv = lay_out(meta, from_cores(from_chips(attn_g)), attn_kinds)

        def shard(x):
            return lax.dynamic_slice_in_dim(x, t * SHARD, SHARD, 0)

        return (
            output, g_inputs, n1g, n1s, g_wq, g_wk, g_wv, shard(g_bq), shard(g_bv),
            g_wo, g_bo, n2g, n2s, g_wup, shard(g_bup), g_wdn, g_bdn,
        )

    return body


def solution(mesh):
    tok = P(("seq", "tp"), None)
    col, row, vec, rep = P(None, "tp"), P("tp", None), P("tp"), P()
    in_specs = (
        tok, P("seq", None), P("seq"), rep, rep, col, col, col, vec, vec,
        row, rep, rep, rep, col, vec, row, rep, tok,
    )
    out_specs = (
        tok, tok, rep, rep, col, col, col, vec, vec,
        row, rep, rep, rep, col, vec, row, rep,
    )
    body = make_body(mesh.shape["seq"], mesh.shape["tp"])
    return jax.shard_map(body, mesh=mesh, in_specs=in_specs, out_specs=out_specs, check_vma=False)
```

```python
import functools
import math

import jax
import jax.numpy as jnp
from jax import lax
from jax.experimental import pallas as pl
from jax.experimental.pallas import tpu as pltpu
from jax.sharding import PartitionSpec as P

HEAD_DIM = 128
ROW_LEN = 2048
NORM_EPS = 1e-05
MASKED = -1000000000.0
LOG2E = 1.4426950408889634
TILE = 256
BLOCK = 256
FAR = 256
ROWS = 128
GROUPS = 1
F32 = jnp.float32
BF16 = jnp.bfloat16
VMEM_LIMIT = 58 * 1024 * 1024


def dot_nn(a, b):
    return lax.dot_general(a, b, (((1,), (0,)), ((), ())), preferred_element_type=F32)


def dot_nt(a, b):
    return lax.dot_general(a, b, (((1,), (1,)), ((), ())), preferred_element_type=F32)


def dot_tn(a, b):
    return lax.dot_general(a, b, (((0,), (0,)), ((), ())), preferred_element_type=F32)


def normalise(x):
    centre = x - jnp.mean(x, axis=-1, keepdims=True)
    rstd = lax.rsqrt(jnp.mean(centre * centre, axis=-1, keepdims=True) + NORM_EPS)
    return centre * rstd, rstd


def norm_back(grad, hat, rstd, gain):
    t = gain * grad
    mean_t = jnp.mean(t, axis=-1, keepdims=True)
    mean_th = jnp.mean(t * hat, axis=-1, keepdims=True)
    return (t - mean_t - hat * mean_th) * rstd


def call(kernel, outs, ins, scratch, name, smem=0, anys=0, out_anys=0, gflop=50):
    spaces = [pltpu.SMEM] * smem + [pltpu.VMEM] * (len(ins) - smem - anys) + [pl.ANY] * anys
    out_spaces = [pltpu.VMEM] * (len(outs) - out_anys) + [pl.ANY] * out_anys
    return pl.pallas_call(
        kernel,
        out_shape=tuple(jax.ShapeDtypeStruct(*o) for o in outs),
        in_specs=[pl.BlockSpec(memory_space=m) for m in spaces],
        out_specs=tuple(pl.BlockSpec(memory_space=m) for m in out_spaces),
        scratch_shapes=scratch,
        compiler_params=pltpu.CompilerParams(vmem_limit_bytes=VMEM_LIMIT),
        cost_estimate=pl.CostEstimate(
            flops=gflop * 10**9, bytes_accessed=1000000, transcendentals=0
        ),
        name=name,
    )(*ins)


def load_weights(meta, shards, off, pieces, dst, sem):
    s, t = meta[0], meta[1]
    count, size, per = pieces[0].shape[1:]
    n_tp = dst.shape[2] // per
    if len(pieces) == 1:
        for i in range(pieces[0].shape[0]):
            at, to = i // n_tp * size, i % n_tp * per
            target = dst.at[:, at : at + size, to : to + per]
            pltpu.make_async_copy(pieces[0].at[i], target, sem).start()
        return pltpu.make_async_copy(dst, dst, sem).wait
    mine = pl.ds(pl.multiple_of(t * per, per), per)
    for m in range(count):
        source = shards[m].at[:, off : off + per]
        pltpu.make_async_copy(source, dst.at[m, :, mine], sem).start()
    for j, piece in enumerate(pieces):
        at = pl.ds(pl.multiple_of((s ^ j) * size, size), size)
        for r in range(n_tp - 1):
            u = pl.multiple_of(lax.rem(t + r + 1, n_tp) * per, per)
            pltpu.make_async_copy(piece.at[r], dst.at[:, at, pl.ds(u, per)], sem).start()
    return pltpu.make_async_copy(dst, dst, sem).wait


def store_grads(meta, grads, keep, send, sems, first, last):
    s = meta[0]
    half, n_tp, _, size, per = keep.shape
    for parity, dst in enumerate((keep, send)):
        for jj in range(half):
            p = pl.ds(pl.multiple_of((s ^ (2 * jj + parity)) * size, size), size)
            for t in range(n_tp):
                pltpu.make_async_copy(
                    grads.at[first:last, p, t * per : (t + 1) * per],
                    dst.at[jj, t, first:last],
                    sems.at[parity],
                ).start()


def grads_stored(keep, send, sems):
    for parity, dst in enumerate((keep, send)):
        pltpu.make_async_copy(dst, dst, sems.at[parity]).wait()


def attend(rng, segq, segk, q, k, v, mixed, lse, s_scr, m_scr, l_scr, acc):
    heads = q.shape[1] // HEAD_DIM
    coef = HEAD_DIM**-0.5 * LOG2E
    of = [slice(h * HEAD_DIM, (h + 1) * HEAD_DIM) for h in range(heads)]

    def fold(x, op):
        x = x.reshape(BLOCK // 8, 8, BLOCK)
        res = x[0]
        for i in range(1, BLOCK // 8):
            res = op(res, x[i])
        return res

    @pl.loop(0, q.shape[0] // BLOCK)
    def _(qb):
        rows = pl.ds(pl.multiple_of(qb * BLOCK, BLOCK), BLOCK)
        lo = rng[0, qb]
        hi = rng[1, qb]
        sq = segq[:, rows]
        m_scr[...] = jnp.full(m_scr.shape, -3e38, F32)
        l_scr[...] = jnp.zeros(l_scr.shape, F32)
        acc[...] = jnp.zeros(acc.shape, F32)

        @pl.loop(lo, hi)
        def _(kc):
            ks = pl.ds(pl.multiple_of(kc * BLOCK, BLOCK), BLOCK)
            bias = jnp.where(segk[ks, :] == sq, 0.0, MASKED)
            for h in range(0, heads, 2):
                pair = (h, h + 1)
                scores = [dot_nt(k[ks, of[i]], q[rows, of[i]]) * coef + bias for i in pair]
                for i, s in zip(pair, scores):
                    s_scr[kc, i] = s
                    m_scr[i] = jnp.maximum(m_scr[i], fold(s, jnp.maximum))

        for h in range(heads):
            m_scr[h] = jnp.broadcast_to(jnp.max(m_scr[h], axis=0, keepdims=True), (8, BLOCK))

        @pl.loop(lo, hi)
        def _(kc):
            ks = pl.ds(pl.multiple_of(kc * BLOCK, BLOCK), BLOCK)
            for h in range(0, heads, 2):
                pair = (h, h + 1)
                probs = [jnp.exp2(s_scr[kc, i] - m_scr[i, :1]) for i in pair]
                outs = [dot_tn(v[ks, of[i]], p.astype(BF16)) for i, p in zip(pair, probs)]
                for i, p, o in zip(pair, probs, outs):
                    l_scr[i] += fold(p, jnp.add)
                    acc[i] += o

        for h in range(heads):
            total = jnp.sum(l_scr[h], axis=0, keepdims=True)
            mixed[rows, of[h]] = jnp.transpose(acc[h] / total).astype(BF16)
            lse[h : h + 1, rows] = m_scr[h, :1] + jnp.log2(total)


def attend_back(rng, segq, segk, lse, delta, q, do, k, v, dq, dk_acc, dv_acc, dq_acc):
    heads = q.shape[1] // HEAD_DIM
    scale = HEAD_DIM**-0.5
    coef = scale * LOG2E
    of = [slice(h * HEAD_DIM, (h + 1) * HEAD_DIM) for h in range(heads)]

    @pl.loop(0, q.shape[0] // BLOCK)
    def _(qb):
        rows = pl.ds(pl.multiple_of(qb * BLOCK, BLOCK), BLOCK)
        lo = rng[0, qb]
        hi = rng[1, qb]
        sq = segq[:, rows]
        dq_acc[...] = jnp.zeros(dq_acc.shape, F32)

        @pl.loop(lo, hi)
        def _(kc):
            ks = pl.ds(pl.multiple_of(kc * BLOCK, BLOCK), BLOCK)
            bias = jnp.where(segk[ks, :] == sq, 0.0, MASKED)

            def probs(h):
                s = dot_nt(k[ks, of[h]], q[rows, of[h]]) * coef
                p = jnp.exp2(s + (bias - lse[h : h + 1, rows]))
                return p, dot_nt(v[ks, of[h]], do[rows, of[h]])

            def products(h, p, dp):
                ds = (p * (dp - delta[h : h + 1, rows])).astype(BF16)
                return (
                    dot_nn(p.astype(BF16), do[rows, of[h]]),
                    dot_nn(ds, q[rows, of[h]]),
                    dot_tn(k[ks, of[h]], ds),
                )

            for h in range(0, heads, 2):
                pair = (h, h + 1)
                both = [probs(i) for i in pair]
                terms = [products(i, *b) for i, b in zip(pair, both)]
                for i, (a, b, c) in zip(pair, terms):
                    dv_acc[ks, of[i]] += a
                    dk_acc[ks, of[i]] += b
                    dq_acc[i] += c

        for h in range(heads):
            dq[rows, of[h]] = (jnp.transpose(dq_acc[h]) * scale).astype(BF16)


def used_chunks(rng):
    tokens = BLOCK * rng.shape[1]
    before = rng[0, 0] * BLOCK < tokens - FAR
    after = rng[1, rng.shape[1] - 1] * BLOCK > 2 * tokens + FAR
    return before, after


def forward_kernel(first, n_pieces, off, meta, rng, segq, segk, *refs):
    if first:
        gain, shift, bq, bv, left, own, right, *refs = refs
    else:
        bq, bv, low_in, *refs = refs
    shards, pieces, refs = refs[:3], refs[3 : 3 + n_pieces], refs[3 + n_pieces :]
    mixed, lse, q_out, k_out, v_out, *refs = refs
    if first:
        low_out, *refs = refs
    q, k, v, low, w, s_scr, m_scr, l_scr, acc, sem, out_sems, *refs = refs
    tokens = q.shape[0]
    before, after = used_chunks(rng)
    lo = jnp.where(before, 0, (tokens - FAR) // BLOCK)
    hi = jnp.where(after, 3 * tokens, 2 * tokens + FAR) // BLOCK

    def copy(i, src, dst):
        return pltpu.make_async_copy(src, dst, out_sems.at[i])

    def chunk(c):
        return pl.ds(pl.multiple_of(c * BLOCK, BLOCK), BLOCK)

    if first:
        (window,) = refs
        ins = [
            copy(i, x, window.at[i * tokens : (i + 1) * tokens])
            for i, x in enumerate((left, own, right))
        ]
    else:
        ins = [copy(3, low_in, low)]
    for x in ins:
        x.start()
    wait = load_weights(meta, shards, off, pieces, w, sem)
    for x in ins:
        x.wait()
    outs = [(q, q_out), (k, k_out), (v, v_out)]
    if first:

        @pl.loop(lo, hi)
        def _(c):
            hat, _ = normalise(window[chunk(c), :].astype(F32))
            low[chunk(c), :] = (hat * gain[...] + shift[...]).astype(BF16)

        outs.append((low, low_out))
        copy(3, *outs[3]).start()
    wait()
    q[...] = (dot_nn(low[tokens : 2 * tokens, :], w[0]) + bq[...]).astype(BF16)
    copy(0, *outs[0]).start()

    @pl.loop(lo, hi)
    def _(c):
        k[chunk(c), :] = dot_nn(low[chunk(c), :], w[1]).astype(BF16)
        v[chunk(c), :] = (dot_nn(low[chunk(c), :], w[2]) + bv[...]).astype(BF16)

    copy(1, *outs[1]).start()
    copy(2, *outs[2]).start()
    attend(rng, segq, segk, q, k, v, mixed, lse, s_scr, m_scr, l_scr, acc)
    for i, x in enumerate(outs):
        copy(i, *x).wait()


def forward(group, meta, rng, segq, segk, source, bq, bv, shards, pieces):
    first = group == 0
    width = shards[0].shape[0]
    window = segk.shape[0]
    tokens = window // 3
    per = pieces[0].shape[3]
    cols = bq.shape[1]
    heads = cols // HEAD_DIM
    slim, wide = (tokens, cols), (window, cols)
    kept = ((window, width), BF16)
    ins = [meta, rng, segq, segk]
    ins += [*source[:2], bq, bv, *source[2:]] if first else [bq, bv, source]
    return call(
        functools.partial(forward_kernel, first, len(pieces), group * per),
        [(slim, BF16), ((heads, tokens), F32), (slim, BF16), (wide, BF16), (wide, BF16)]
        + [kept] * first,
        [*ins, *shards, *pieces],
        [
            pltpu.VMEM(slim, BF16),
            pltpu.VMEM(wide, BF16),
            pltpu.VMEM(wide, BF16),
            pltpu.VMEM(*kept),
            pltpu.VMEM((3, width, cols), BF16),
            pltpu.VMEM((window // BLOCK, heads, BLOCK, BLOCK), F32),
            pltpu.VMEM((heads, 8, BLOCK), F32),
            pltpu.VMEM((heads, 8, BLOCK), F32),
            pltpu.VMEM((heads, HEAD_DIM, BLOCK), F32),
            pltpu.SemaphoreType.DMA,
            pltpu.SemaphoreType.DMA((4,)),
        ]
        + [pltpu.VMEM(*kept)] * first,
        "forward_attention",
        smem=2,
        anys=3 + len(pieces) + (3 if first else 1),
        out_anys=3 + first,
    )


def feed_kernel(n_pieces, groups, meta, inputs, dout, bo, gain, shift, bup, bdn, *refs):
    parts, refs = refs[:groups], refs[groups:]
    pieces, refs = refs[:n_pieces], refs[n_pieces:]
    g_parts, refs = refs[:groups], refs[groups:]
    deltas, refs = refs[:groups], refs[groups:]
    sums, output_out, g_resid_out, keep, send, *refs = refs
    w, mixed, resid, hat, rstd, second, hidden, g_up, g_sec, low, output, grads, *sems = refs
    sem, grad_sems, out_sems = sems
    wait = load_weights(meta, None, 0, pieces, w, sem)
    wo_t, wup, wdn_t = w.at[0], w.at[1], w.at[2]
    tokens, width = inputs.shape
    per = SHARD // groups
    for g in range(groups):
        for t in range(width // SHARD):
            at = t * SHARD + g * per
            mixed[:, at : at + per] = parts[g][:, t * per : (t + 1) * per]
    sums[...] = jnp.zeros(sums.shape, F32)
    sums[4:5, :] = jnp.sum(dout[...].astype(F32), axis=0, keepdims=True)
    wait()
    resid[...] = inputs[...].astype(F32) + dot_nt(mixed[...], wo_t[...]) + bo[...]

    @pl.loop(0, tokens // BLOCK)
    def _(i):
        rows = pl.ds(pl.multiple_of(i * BLOCK, BLOCK), BLOCK)
        h, r = normalise(resid[rows, :])
        hat[rows, :] = h
        rstd[rows, :] = jnp.broadcast_to(r, (BLOCK, 128))
        second[rows, :] = (h * gain[...] + shift[...]).astype(BF16)

    for n in range(width // TILE):
        cols = slice(n * TILE, (n + 1) * TILE)
        up = dot_nn(second[...], wup[:, cols]) + bup[:, cols]
        d_hidden = dot_nn(dout[...], wdn_t[:, cols])
        phi = 0.5 + 0.5 * lax.erf(up * (0.5**0.5))
        hidden[:, cols] = (up * phi).astype(BF16)
        slope = phi + up * (jnp.exp(-0.5 * up * up) * (0.5 / math.pi) ** 0.5)
        grad = (d_hidden * slope).astype(BF16)
        g_up[:, cols] = grad
        sums[3:4, cols] = jnp.sum(grad.astype(F32), axis=0, keepdims=True)
    g_sec[...] = dot_nt(g_up[...], wup[...])
    output[...] = (resid[...] + dot_nt(hidden[...], wdn_t[...]) + bdn[...]).astype(BF16)
    out_copy = pltpu.make_async_copy(output, output_out, out_sems.at[0])
    out_copy.start()
    grads[2] = dot_tn(dout[...], hidden[...]).astype(BF16)
    grads[1] = dot_tn(second[...], g_up[...]).astype(BF16)
    store_grads(meta, grads, keep, send, grad_sems, 1, 3)

    @pl.loop(0, tokens // ROWS)
    def _(i):
        rows = pl.ds(pl.multiple_of(i * ROWS, ROWS), ROWS)
        h, g = hat[rows, :], g_sec[rows, :]
        res = dout[rows, :].astype(F32) + norm_back(g, h, rstd[rows, :1], gain[...])
        resid[rows, :] = res
        low[rows, :] = res.astype(BF16)
        for n, x in enumerate((res, g * h, g)):
            sums[n : n + 1, :] += jnp.sum(x, axis=0, keepdims=True)

    resid_copy = pltpu.make_async_copy(resid, g_resid_out, out_sems.at[1])
    resid_copy.start()
    grads[0] = dot_tn(low[...], mixed[...]).astype(BF16)
    store_grads(meta, grads, keep, send, grad_sems, 0, 1)
    ones = jnp.ones((8, HEAD_DIM), BF16)
    for n in range(width // TILE):
        cols = slice(n * TILE, (n + 1) * TILE)
        grad = dot_nn(low[...], wo_t[:, cols]).astype(BF16)
        prod = grad.astype(F32) * mixed[:, cols].astype(F32)
        high = prod.astype(BF16)
        rest_of = (prod - high.astype(F32)).astype(BF16)
        for i in range(TILE // HEAD_DIM):
            part = slice(i * HEAD_DIM, (i + 1) * HEAD_DIM)
            total = dot_nt(ones, high[:, part]) + dot_nt(ones, rest_of[:, part])
            at = n * TILE + i * HEAD_DIM
            t, g, inside = at // SHARD, at % SHARD // per, at % per
            to = t * per + inside
            g_parts[g][:, to : to + HEAD_DIM] = grad[:, part]
            h = to // HEAD_DIM
            deltas[g][h : h + 1, :] = total[:1]
    out_copy.wait()
    resid_copy.wait()
    grads_stored(keep, send, grad_sems)


def feed_forward(meta, inner, inputs, dout, bo, gain, shift, bup, bdn, parts, pieces):
    tokens, width = inputs.shape
    groups = len(parts)
    half = max(inner // 2, 1)
    travel = ((half, width // SHARD, 3, width // inner, SHARD), BF16)
    wide = pltpu.VMEM((tokens, width), F32)
    slim = pltpu.VMEM((tokens, width), BF16)
    return call(
        functools.partial(feed_kernel, len(pieces), groups),
        [(parts[0].shape, BF16)] * groups
        + [((width // HEAD_DIM // groups, tokens), F32)] * groups
        + [((8, width), F32), ((tokens, width), BF16), ((tokens, width), F32), travel, travel],
        [meta, inputs, dout, bo, gain, shift, bup, bdn, *parts, *pieces],
        [
            pltpu.VMEM((3, width, width), BF16),
            slim,
            wide,
            wide,
            pltpu.VMEM((tokens, 128), F32),
            slim,
            slim,
            slim,
            wide,
            slim,
            slim,
            pltpu.VMEM((3, width, width), BF16),
            pltpu.SemaphoreType.DMA,
            pltpu.SemaphoreType.DMA((2,)),
            pltpu.SemaphoreType.DMA((2,)),
        ],
        "feed_forward",
        smem=1,
        anys=len(pieces),
        out_anys=4,
    )


def backward_kernel(n_pieces, off, more, meta, rng, segq, segk, lse, delta, q, do, k, v, *refs):
    if more:
        left_in, right_in, *refs = refs
    low_in, *refs = refs
    shards, pieces, refs = refs[:3], refs[3 : 3 + n_pieces], refs[3 + n_pieces :]
    left, own, right, sums, keep, send, *refs = refs
    low, w, dq, dk, dv, dk_acc, dv_acc, dq_acc, grads, sem, low_sem, grad_sems = refs
    low_copy = pltpu.make_async_copy(low_in, low, low_sem)
    low_copy.start()
    wait = load_weights(meta, shards, off, pieces, w, sem)
    tokens, width = q.shape
    start, stop = tokens - FAR, 2 * tokens + FAR
    near, middle = slice(start, stop), slice(tokens, 2 * tokens)
    before, after = used_chunks(rng)
    scale = HEAD_DIM**-0.5

    def zero(rows):
        dk_acc[rows, :] = jnp.zeros((rows.stop - rows.start, width), F32)
        dv_acc[rows, :] = jnp.zeros((rows.stop - rows.start, width), F32)

    def narrow(rows):
        dk[rows, :] = (dk_acc[rows, :] * scale).astype(BF16)
        dv[rows, :] = dv_acc[rows, :].astype(BF16)

    def ends(act):
        pl.when(before)(lambda: act(slice(0, start)))
        pl.when(after)(lambda: act(slice(stop, 3 * tokens)))

    zero(near)
    ends(zero)
    attend_back(rng, segq, segk, lse, delta, q, do, k, v, dq, dk_acc, dv_acc, dq_acc)
    narrow(near)
    ends(narrow)

    low_copy.wait()
    grads[0] = dot_tn(low[middle, :], dq[...]).astype(BF16)
    sums[...] = jnp.zeros(sums.shape, F32)
    sums[0:1, :] = jnp.sum(dq[...].astype(F32), axis=0, keepdims=True)

    sums[1:2, :] = jnp.sum(dv[near, :].astype(F32), axis=0, keepdims=True)
    grads[1] = dot_tn(low[near, :], dk[near, :]).astype(BF16)
    grads[2] = dot_tn(low[near, :], dv[near, :]).astype(BF16)

    for i, used in enumerate((before, after)):

        @pl.when(used)
        def _():
            rows = slice(i * stop, i * stop + start)
            sums[1:2, :] += jnp.sum(dv[rows, :].astype(F32), axis=0, keepdims=True)
            for m, x in ((1, dk), (2, dv)):
                more = dot_tn(low[rows, :], x[rows, :])
                grads[m] = (grads[m].astype(F32) + more).astype(BF16)

    store_grads(meta, grads, keep, send, grad_sems, 0, 3)

    wait()

    def halo_grads(out, old, to, rows):
        res = dot_nt(dk[rows, :], w[1]) + dot_nt(dv[rows, :], w[2])
        if more:
            res = res + old[to, :].astype(F32)
        out[to, :] = res.astype(BF16)

    lows, highs = slice(0, tokens - FAR), slice(tokens - FAR, tokens)
    firsts, others = slice(0, FAR), slice(FAR, tokens)
    for out, old, used, far_to, near_to, base in (
        (left, left_in if more else None, before, lows, highs, 0),
        (right, right_in if more else None, after, others, firsts, 2 * tokens),
    ):
        halo_grads(out, old, near_to, slice(base + near_to.start, base + near_to.stop))

        @pl.when(used)
        def _():
            halo_grads(out, old, far_to, slice(base + far_to.start, base + far_to.stop))

        @pl.when(jnp.logical_not(used))
        def _():
            if more:
                out[far_to, :] = old[far_to, :]
            else:
                out[far_to, :] = jnp.zeros((tokens - FAR, out.shape[1]), BF16)

    own[...] = (
        dot_nt(dk[middle, :], w[1]) + dot_nt(dv[middle, :], w[2]) + dot_nt(dq[...], w[0])
    )
    grads_stored(keep, send, grad_sems)


def backward(group, meta, rng, segq, segk, lse, delta, q, do, k, v, old, low, shards, pieces):
    tokens, cols = q.shape
    width = low.shape[1]
    window = 3 * tokens
    per = pieces[0].shape[3]
    travel = ((max(len(pieces) // 2, 1), cols // per, *pieces[0].shape[1:]), BF16)
    slim, wide, full = (tokens, cols), (window, cols), (tokens, width)
    return call(
        functools.partial(backward_kernel, len(pieces), group * per, len(old) > 0),
        [(full, BF16), (full, F32), (full, BF16), ((8, cols), F32), travel, travel],
        [meta, rng, segq, segk, lse, delta, q, do, k, v, *old, low, *shards, *pieces],
        [
            pltpu.VMEM((window, width), BF16),
            pltpu.VMEM((3, width, cols), BF16),
            pltpu.VMEM(slim, BF16),
            pltpu.VMEM(wide, BF16),
            pltpu.VMEM(wide, BF16),
            pltpu.VMEM(wide, F32),
            pltpu.VMEM(wide, F32),
            pltpu.VMEM((cols // HEAD_DIM, HEAD_DIM, BLOCK), F32),
            pltpu.VMEM((3, width, cols), BF16),
            pltpu.SemaphoreType.DMA,
            pltpu.SemaphoreType.DMA,
            pltpu.SemaphoreType.DMA((2,)),
        ],
        "backward_attention",
        smem=2,
        anys=4 + len(pieces),
        out_anys=2,
    )


def last_kernel(inputs, g_resid, from_left, from_right, gain, *refs):
    *owns, g_inputs, sums = refs
    sums[...] = jnp.zeros(sums.shape, F32)

    @pl.loop(0, inputs.shape[0] // ROWS)
    def _(i):
        rows = pl.ds(pl.multiple_of(i * ROWS, ROWS), ROWS)
        hat, rstd = normalise(inputs[rows, :].astype(F32))
        g = from_left[rows, :].astype(F32) + from_right[rows, :].astype(F32)
        for own in owns:
            g = g + own[rows, :]
        g_inputs[rows, :] = (g_resid[rows, :] + norm_back(g, hat, rstd, gain[...])).astype(BF16)
        sums[0:1, :] += jnp.sum(g * hat, axis=0, keepdims=True)
        sums[1:2, :] += jnp.sum(g, axis=0, keepdims=True)


def last_step(inputs, g_resid, from_left, from_right, gain, owns):
    return call(
        last_kernel,
        [(inputs.shape, BF16), ((8, inputs.shape[1]), F32)],
        [inputs, g_resid, from_left, from_right, gain, *owns],
        [],
        "input_norm_grads",
    )


def lay_out_kernel(turned, groups, meta, *refs):
    outs = refs[-len(turned) :]
    pieces = refs[: -len(turned)]
    n = len(pieces) // groups
    s = meta[0]
    size, per = pieces[0].shape[-2:]
    for g in range(groups):
        to = slice(g * per, (g + 1) * per)
        if n == 1:
            whole = [
                (pieces[g].at[i], slice(i * size, (i + 1) * size))
                for i in range(pieces[g].shape[0])
            ]
        else:
            whole = [
                (pieces[g * n + j], pl.ds(pl.multiple_of((s ^ j) * size, size), size))
                for j in range(n)
            ]
        for piece, at in whole:
            for m, turn in enumerate(turned):
                if turn:
                    outs[m][to, at] = jnp.transpose(piece[m].astype(F32))
                else:
                    outs[m][at, to] = piece[m].astype(F32)


def lay_out(meta, groups, turned):
    first = groups[0]
    width = first[0].shape[-2] * (len(first) if len(first) > 1 else first[0].shape[0])
    shapes = [(SHARD, width) if turn else (width, SHARD) for turn in turned]
    return call(
        functools.partial(lay_out_kernel, turned, len(groups)),
        [(shape, F32) for shape in shapes],
        [meta, *[piece for group in groups for piece in group]],
        [],
        "lay_out_grads",
        smem=1,
    )


SHARD = 256


def make_body(n_seq, n_tp):
    inner = min(n_seq, 8)
    outer = n_seq // inner
    half = inner // 2
    masks = [2 * jj for jj in range(1, half)]

    def shift(x, by):
        pairs = [(i, i + by) for i in range(n_tp) if 0 <= i + by < n_tp]
        return lax.ppermute(x, "tp", pairs)

    def swap(x, mask):
        return lax.ppermute(x, "seq", [(i, i ^ mask) for i in range(n_seq)])

    def tie(*xs):
        return lax.optimization_barrier(xs)

    def over_tp(shards, biases, off, per, s, t, after):
        size = shards[0].shape[0] // inner
        cut = jnp.stack([lax.dynamic_slice(w, (s * size, off), (size, per)) for w in shards])
        parts = []
        rest = jnp.stack([b[off : off + per] for b in biases])
        for _ in range(3):
            part = rest.astype(BF16)
            rest = rest - part.astype(F32)
            parts.append(part)
        parts = jnp.stack(parts + [jnp.zeros_like(parts[0])] * 13, axis=1)
        block = jnp.concatenate([cut, parts], axis=1)
        block = jnp.broadcast_to(block[None], (n_tp, *block.shape))
        if after is not None:
            block, _ = tie(block, after)
        got = lax.all_to_all(block, "tp", 0, 0, tiled=True)
        others = jnp.stack(
            [lax.dynamic_index_in_dim(got, lax.rem(t + r + 1, n_tp), 0, keepdims=False)[:, :size]
             for r in range(n_tp - 1)]
        )
        whole = jnp.sum(got[:, :, size : size + 3].astype(F32), axis=2)
        whole = [whole[:, m].reshape(1, n_tp * per) for m in range(len(biases))]
        return others, whole, got

    def from_chips(x):
        return [x] + [swap(x, mask) for mask in masks]

    def from_cores(even):
        odd = [swap(e, 1) for e in even]
        return [e for pair in zip(even, odd) for e in pair]

    def over_cores(keep, send):
        got = swap(send, 1)
        return [(keep[jj].astype(F32) + got[jj].astype(F32)).astype(BF16) for jj in range(half)]

    def over_chips(sums):
        moved = [swap(sums[jj], 2 * jj) for jj in range(1, half)]
        total = sums[0].astype(F32)
        for x in moved:
            total = total + x.astype(F32)
        total = total.astype(BF16)
        if outer > 1:
            groups = [[i + inner * o for o in range(outer)] for i in range(inner)]
            total = lax.psum(total, "seq", axis_index_groups=groups)
        return total

    def own_shard(total):
        got = lax.all_to_all(total, "tp", 0, 0, tiled=True)
        return jnp.sum(got.astype(F32), axis=0).astype(BF16)

    def body(
        inputs, segment_ids, row_lengths, norm1_gain, norm1_shift, w_query, w_key, w_value,
        b_query, b_value, w_out, b_out, norm2_gain, norm2_shift, w_up, b_up, w_down, b_down,
        out_grad,
    ):
        tokens, width = inputs.shape
        halo = tokens
        t = lax.axis_index("tp")
        s = lax.rem(lax.axis_index("seq"), inner)
        meta = jnp.stack([s, t]).astype(jnp.int32)
        per = SHARD // GROUPS
        every = range(GROUPS)
        zero = jnp.zeros_like(b_query)

        def row(x):
            return x.reshape(1, -1)

        def by_shard(groups):
            cols = [x.reshape(n_tp, per) for x in groups]
            return jnp.concatenate(cols, axis=1).reshape(1, width)

        attn_w = [w_query, w_key, w_value]
        attn_b = [b_query, b_up, b_value]
        done, dones = None, []
        attn_p, attn_whole = [], []
        for g in every:
            others, whole, done = over_tp(attn_w, attn_b, g * per, per, s, t, done)
            dones.append(done)
            even = from_chips(others)
            even[0], _ = tie(even[0], even[-1])
            attn_p.append(from_cores(even))
            attn_whole.append(whole)
        feed_w = [w_out.T, w_up, w_down.T]
        size = width // n_seq
        at = lax.axis_index("seq") * size
        cut = jnp.stack([lax.dynamic_slice_in_dim(w, at, size, 0) for w in feed_w])
        feed_p = [lax.all_gather(cut, ("seq", "tp"), axis=0)]
        inputs_later, _ = tie(inputs, dones[0])
        left = shift(inputs_later, 1)
        right = shift(inputs_later, -1)

        position = jnp.arange(ROW_LEN, dtype=jnp.int32)
        numbers = jnp.where(position < row_lengths[0], segment_ids[0], 4096 + position)
        numbers = jnp.concatenate(
            [jnp.full((halo,), -1, jnp.int32), numbers, jnp.full((halo,), 1 << 20, jnp.int32)]
        )
        seg_win = lax.dynamic_slice_in_dim(numbers, t * tokens, tokens + 2 * halo, 0)
        seg_mine = seg_win[halo : halo + tokens]
        first = seg_mine[::BLOCK]
        last = seg_mine[BLOCK - 1 :: BLOCK]
        low = jnp.sum((seg_win[None, :] < first[:, None]).astype(jnp.int32), axis=1)
        high = jnp.sum((seg_win[None, :] <= last[:, None]).astype(jnp.int32), axis=1)
        rng = jnp.stack([low // BLOCK, (high + BLOCK - 1) // BLOCK])
        segq, segk = seg_mine[None, :], seg_win[:, None]

        source = (row(norm1_gain), row(norm1_shift), left, inputs, right)
        saved = []
        for g in every:
            bq, _, bv = attn_whole[g]
            res = forward(g, meta, rng, segq, segk, source, bq, bv, attn_w, attn_p[g])
            mixed, lse, q, k, v = res[:5]
            if g == 0:
                source = first_low = res[5]
            saved.append((mixed, lse, q, k, v))
        bup = by_shard([x[1] for x in attn_whole])
        res = feed_forward(
            meta, inner, inputs, out_grad, row(b_out), row(norm2_gain), row(norm2_shift), bup,
            row(b_down), [x[0] for x in saved], feed_p,
        )
        g_mixed, delta = list(res[:GROUPS]), res[GROUPS : 2 * GROUPS]
        sums_feed, output, g_resid, keep, send = res[2 * GROUPS :]

        sums = over_cores(keep, send)
        g_mixed[0], *sums = tie(g_mixed[0], *sums)
        feed_total = over_chips(sums)
        old, owns, sums_qkv, totals = (), [], [], []
        for g in every:
            _, lse, q, k, v = saved[g]
            dx_left, own, dx_right, vec, keep, send = backward(
                g, meta, rng, segq, segk, lse, delta[g], q, g_mixed[g], k, v, old,
                first_low, attn_w, attn_p[g],
            )
            old = (dx_left, dx_right)
            owns.append(own)
            sums_qkv.append(vec)
            if g > 0:
                send, totals[g - 1] = tie(send, totals[g - 1])
            else:
                send, feed_total = tie(send, feed_total)
            sums = over_cores(keep, send)
            if g + 1 < GROUPS:
                g_mixed[g + 1], *sums = tie(g_mixed[g + 1], *sums)
            else:
                owns[g], *sums = tie(owns[g], *sums)
            totals.append(over_chips(sums))
        from_right = shift(dx_left, -1)
        from_left = shift(dx_right, 1)
        piece = feed_total.shape[1:]
        feed_g = feed_total.reshape(-1, SHARD)
        feed_g = lax.psum_scatter(feed_g, "tp", scatter_dimension=0, tiled=True)
        shards = []
        for g in every:
            shards.append(own_shard(totals[g]))
        g_inputs, sums_in = last_step(
            inputs, g_resid, from_left, from_right, row(norm1_gain), owns
        )

        g_inputs, feed_g = tie(g_inputs, feed_g)
        feed_g = lax.all_gather(feed_g.reshape(piece), "seq", axis=0)[:inner]
        vectors = [by_shard([x[i] for x in sums_qkv]) for i in range(2)]
        vectors = [sums_in[:2], *vectors, sums_feed[:5]]
        vectors = jnp.concatenate(vectors)
        n_vec = vectors.shape[0]
        vectors, shards[-1] = tie(vectors, shards[-1])
        vectors = vectors.reshape(n_seq * n_tp, -1)
        vectors = lax.all_to_all(vectors, ("seq", "tp"), 0, 0, tiled=True)
        vectors = jnp.broadcast_to(jnp.sum(vectors, axis=0, keepdims=True), vectors.shape)
        vectors = lax.all_to_all(vectors, ("seq", "tp"), 0, 0, tiled=True)
        vectors = vectors.reshape(n_vec, width)
        n1g, n1s, g_bq, g_bv, g_bo, n2g, n2s, g_bup, g_bdn = [vectors[i] for i in range(9)]

        pieces = [from_cores(from_chips(x)) for x in shards]
        g_wq, g_wk, g_wv = lay_out(meta, pieces, (False, False, False))
        g_wo, g_wup, g_wdn = lay_out(meta, [[feed_g]], (True, False, True))

        def shard(x):
            return lax.dynamic_slice_in_dim(x, t * SHARD, SHARD, 0)

        return (
            output, g_inputs, n1g, n1s, g_wq, g_wk, g_wv, shard(g_bq), shard(g_bv),
            g_wo, g_bo, n2g, n2s, g_wup, shard(g_bup), g_wdn, g_bdn,
        )

    return body


def solution(mesh):
    tok = P(("seq", "tp"), None)
    col, row, vec, rep = P(None, "tp"), P("tp", None), P("tp"), P()
    in_specs = (
        tok, P("seq", None), P("seq"), rep, rep, col, col, col, vec, vec,
        row, rep, rep, rep, col, vec, row, rep, tok,
    )
    out_specs = (
        tok, tok, rep, rep, col, col, col, vec, vec,
        row, rep, rep, rep, col, vec, row, rep,
    )
    body = make_body(mesh.shape["seq"], mesh.shape["tp"])
    return jax.shard_map(body, mesh=mesh, in_specs=in_specs, out_specs=out_specs, check_vma=False)
```

```python
import functools
import math

import jax
import jax.numpy as jnp
from jax import lax
from jax.experimental import pallas as pl
from jax.experimental.pallas import tpu as pltpu
from jax.sharding import PartitionSpec as P

HEAD_DIM = 128
ROW_LEN = 2048
NORM_EPS = 1e-05
MASKED = -1000000000.0
LOG2E = 1.4426950408889634
TILE = 256
BLOCK = 256
FAR = 256
ROWS = 128
GROUPS = 1
F32 = jnp.float32
BF16 = jnp.bfloat16
VMEM_LIMIT = 58 * 1024 * 1024


def dot_nn(a, b):
    return lax.dot_general(a, b, (((1,), (0,)), ((), ())), preferred_element_type=F32)


def dot_nt(a, b):
    return lax.dot_general(a, b, (((1,), (1,)), ((), ())), preferred_element_type=F32)


def dot_tn(a, b):
    return lax.dot_general(a, b, (((0,), (0,)), ((), ())), preferred_element_type=F32)


def normalise(x):
    centre = x - jnp.mean(x, axis=-1, keepdims=True)
    rstd = lax.rsqrt(jnp.mean(centre * centre, axis=-1, keepdims=True) + NORM_EPS)
    return centre * rstd, rstd


def norm_back(grad, hat, rstd, gain):
    t = gain * grad
    mean_t = jnp.mean(t, axis=-1, keepdims=True)
    mean_th = jnp.mean(t * hat, axis=-1, keepdims=True)
    return (t - mean_t - hat * mean_th) * rstd


def call(kernel, outs, ins, scratch, name, smem=0, anys=0, out_anys=0, gflop=50):
    spaces = [pltpu.SMEM] * smem + [pltpu.VMEM] * (len(ins) - smem - anys) + [pl.ANY] * anys
    out_spaces = [pltpu.VMEM] * (len(outs) - out_anys) + [pl.ANY] * out_anys
    return pl.pallas_call(
        kernel,
        out_shape=tuple(jax.ShapeDtypeStruct(*o) for o in outs),
        in_specs=[pl.BlockSpec(memory_space=m) for m in spaces],
        out_specs=tuple(pl.BlockSpec(memory_space=m) for m in out_spaces),
        scratch_shapes=scratch,
        compiler_params=pltpu.CompilerParams(vmem_limit_bytes=VMEM_LIMIT),
        cost_estimate=pl.CostEstimate(
            flops=gflop * 10**9, bytes_accessed=1000000, transcendentals=0
        ),
        name=name,
    )(*ins)


def load_weights(meta, shards, off, pieces, dst, sem):
    s, t = meta[0], meta[1]
    count, size, per = pieces[0].shape[1:]
    n_tp = dst.shape[2] // per
    mine = pl.ds(pl.multiple_of(t * per, per), per)
    for m in range(count):
        source = shards[m].at[:, off : off + per]
        pltpu.make_async_copy(source, dst.at[m, :, mine], sem).start()
    for j, piece in enumerate(pieces):
        at = pl.ds(pl.multiple_of((s ^ j) * size, size), size)
        for r in range(n_tp - 1):
            u = pl.multiple_of(lax.rem(t + r + 1, n_tp) * per, per)
            pltpu.make_async_copy(piece.at[r], dst.at[:, at, pl.ds(u, per)], sem).start()
    return pltpu.make_async_copy(dst, dst, sem).wait


def store_grads(meta, grads, keep, send, sems, first, last):
    s = meta[0]
    n_tp, _, size, per = keep[0].shape
    for parity, dst in enumerate((keep, send)):
        for jj, piece in enumerate(dst):
            p = pl.ds(pl.multiple_of((s ^ (2 * jj + parity)) * size, size), size)
            for t in range(n_tp):
                pltpu.make_async_copy(
                    grads.at[first:last, p, t * per : (t + 1) * per],
                    piece.at[t, first:last],
                    sems.at[parity, jj],
                ).start()


def grads_stored(keep, send, sems):
    for parity, dst in enumerate((keep, send)):
        for jj, piece in enumerate(dst):
            pltpu.make_async_copy(piece, piece, sems.at[parity, jj]).wait()


def travelling(inner, width, per):
    half = max(inner // 2, 1)
    return half, (width // SHARD, 3, width // inner, per)


def attend(rng, segq, segk, q, k, v, mixed, lse, s_scr, m_scr, l_scr, acc):
    heads = q.shape[1] // HEAD_DIM
    coef = HEAD_DIM**-0.5 * LOG2E
    of = [slice(h * HEAD_DIM, (h + 1) * HEAD_DIM) for h in range(heads)]

    def fold(x, op):
        x = x.reshape(BLOCK // 8, 8, BLOCK)
        res = x[0]
        for i in range(1, BLOCK // 8):
            res = op(res, x[i])
        return res

    @pl.loop(0, q.shape[0] // BLOCK)
    def _(qb):
        rows = pl.ds(pl.multiple_of(qb * BLOCK, BLOCK), BLOCK)
        lo = rng[0, qb]
        hi = rng[1, qb]
        sq = segq[:, rows]
        m_scr[...] = jnp.full(m_scr.shape, -3e38, F32)
        l_scr[...] = jnp.zeros(l_scr.shape, F32)
        acc[...] = jnp.zeros(acc.shape, F32)

        @pl.loop(lo, hi)
        def _(kc):
            ks = pl.ds(pl.multiple_of(kc * BLOCK, BLOCK), BLOCK)
            bias = jnp.where(segk[ks, :] == sq, 0.0, MASKED)
            for h in range(0, heads, 2):
                pair = (h, h + 1)
                scores = [dot_nt(k[ks, of[i]], q[rows, of[i]]) * coef + bias for i in pair]
                for i, s in zip(pair, scores):
                    s_scr[kc, i] = s
                    m_scr[i] = jnp.maximum(m_scr[i], fold(s, jnp.maximum))

        for h in range(heads):
            m_scr[h] = jnp.broadcast_to(jnp.max(m_scr[h], axis=0, keepdims=True), (8, BLOCK))

        @pl.loop(lo, hi)
        def _(kc):
            ks = pl.ds(pl.multiple_of(kc * BLOCK, BLOCK), BLOCK)
            for h in range(0, heads, 2):
                pair = (h, h + 1)
                probs = [jnp.exp2(s_scr[kc, i] - m_scr[i, :1]) for i in pair]
                outs = [dot_tn(v[ks, of[i]], p.astype(BF16)) for i, p in zip(pair, probs)]
                for i, p, o in zip(pair, probs, outs):
                    l_scr[i] += fold(p, jnp.add)
                    acc[i] += o

        for h in range(heads):
            total = jnp.sum(l_scr[h], axis=0, keepdims=True)
            mixed[rows, of[h]] = jnp.transpose(acc[h] / total).astype(BF16)
            lse[h : h + 1, rows] = m_scr[h, :1] + jnp.log2(total)


def attend_back(rng, segq, segk, lse, delta, q, do, k, v, dq, dk_acc, dv_acc, dq_acc):
    heads = q.shape[1] // HEAD_DIM
    scale = HEAD_DIM**-0.5
    coef = scale * LOG2E
    of = [slice(h * HEAD_DIM, (h + 1) * HEAD_DIM) for h in range(heads)]

    @pl.loop(0, q.shape[0] // BLOCK)
    def _(qb):
        rows = pl.ds(pl.multiple_of(qb * BLOCK, BLOCK), BLOCK)
        lo = rng[0, qb]
        hi = rng[1, qb]
        sq = segq[:, rows]
        dq_acc[...] = jnp.zeros(dq_acc.shape, F32)

        @pl.loop(lo, hi)
        def _(kc):
            ks = pl.ds(pl.multiple_of(kc * BLOCK, BLOCK), BLOCK)
            bias = jnp.where(segk[ks, :] == sq, 0.0, MASKED)

            def probs(h):
                s = dot_nt(k[ks, of[h]], q[rows, of[h]]) * coef
                p = jnp.exp2(s + (bias - lse[h : h + 1, rows]))
                return p, dot_nt(v[ks, of[h]], do[rows, of[h]])

            def products(h, p, dp):
                ds = (p * (dp - delta[h : h + 1, rows])).astype(BF16)
                return (
                    dot_nn(p.astype(BF16), do[rows, of[h]]),
                    dot_nn(ds, q[rows, of[h]]),
                    dot_tn(k[ks, of[h]], ds),
                )

            for h in range(0, heads, 2):
                pair = (h, h + 1)
                both = [probs(i) for i in pair]
                terms = [products(i, *b) for i, b in zip(pair, both)]
                for i, (a, b, c) in zip(pair, terms):
                    dv_acc[ks, of[i]] += a
                    dk_acc[ks, of[i]] += b
                    dq_acc[i] += c

        for h in range(heads):
            dq[rows, of[h]] = (jnp.transpose(dq_acc[h]) * scale).astype(BF16)


def used_chunks(rng):
    tokens = BLOCK * rng.shape[1]
    before = rng[0, 0] * BLOCK < tokens - FAR
    after = rng[1, rng.shape[1] - 1] * BLOCK > 2 * tokens + FAR
    return before, after


def forward_kernel(first, n_pieces, off, meta, rng, segq, segk, *refs):
    if first:
        gain, shift, bq, bv, left, own, right, *refs = refs
    else:
        bq, bv, low_in, *refs = refs
    shards, pieces, refs = refs[:3], refs[3 : 3 + n_pieces], refs[3 + n_pieces :]
    mixed, lse, q_out, k_out, v_out, *refs = refs
    if first:
        low_out, *refs = refs
    q, k, v, low, w, s_scr, m_scr, l_scr, acc, sem, out_sems, *refs = refs
    tokens = q.shape[0]
    before, after = used_chunks(rng)
    lo = jnp.where(before, 0, (tokens - FAR) // BLOCK)
    hi = jnp.where(after, 3 * tokens, 2 * tokens + FAR) // BLOCK

    def copy(i, src, dst):
        return pltpu.make_async_copy(src, dst, out_sems.at[i])

    def chunk(c):
        return pl.ds(pl.multiple_of(c * BLOCK, BLOCK), BLOCK)

    if first:
        (window,) = refs
        ins = [
            copy(i, x, window.at[i * tokens : (i + 1) * tokens])
            for i, x in enumerate((left, own, right))
        ]
    else:
        ins = [copy(3, low_in, low)]
    for x in ins:
        x.start()
    wait = load_weights(meta, shards, off, pieces, w, sem)
    for x in ins:
        x.wait()
    outs = [(q, q_out), (k, k_out), (v, v_out)]
    if first:

        @pl.loop(lo, hi)
        def _(c):
            hat, _ = normalise(window[chunk(c), :].astype(F32))
            low[chunk(c), :] = (hat * gain[...] + shift[...]).astype(BF16)

        outs.append((low, low_out))
        copy(3, *outs[3]).start()
    wait()
    q[...] = (dot_nn(low[tokens : 2 * tokens, :], w[0]) + bq[...]).astype(BF16)
    copy(0, *outs[0]).start()

    @pl.loop(lo, hi)
    def _(c):
        k[chunk(c), :] = dot_nn(low[chunk(c), :], w[1]).astype(BF16)
        v[chunk(c), :] = (dot_nn(low[chunk(c), :], w[2]) + bv[...]).astype(BF16)

    copy(1, *outs[1]).start()
    copy(2, *outs[2]).start()
    attend(rng, segq, segk, q, k, v, mixed, lse, s_scr, m_scr, l_scr, acc)
    for i, x in enumerate(outs):
        copy(i, *x).wait()


def forward(group, meta, rng, segq, segk, source, bq, bv, shards, pieces):
    first = group == 0
    width = shards[0].shape[0]
    window = segk.shape[0]
    tokens = window // 3
    per = pieces[0].shape[3]
    cols = bq.shape[1]
    heads = cols // HEAD_DIM
    slim, wide = (tokens, cols), (window, cols)
    kept = ((window, width), BF16)
    ins = [meta, rng, segq, segk]
    ins += [*source[:2], bq, bv, *source[2:]] if first else [bq, bv, source]
    return call(
        functools.partial(forward_kernel, first, len(pieces), group * per),
        [(slim, BF16), ((heads, tokens), F32), (slim, BF16), (wide, BF16), (wide, BF16)]
        + [kept] * first,
        [*ins, *shards, *pieces],
        [
            pltpu.VMEM(slim, BF16),
            pltpu.VMEM(wide, BF16),
            pltpu.VMEM(wide, BF16),
            pltpu.VMEM(*kept),
            pltpu.VMEM((3, width, cols), BF16),
            pltpu.VMEM((window // BLOCK, heads, BLOCK, BLOCK), F32),
            pltpu.VMEM((heads, 8, BLOCK), F32),
            pltpu.VMEM((heads, 8, BLOCK), F32),
            pltpu.VMEM((heads, HEAD_DIM, BLOCK), F32),
            pltpu.SemaphoreType.DMA,
            pltpu.SemaphoreType.DMA((4,)),
        ]
        + [pltpu.VMEM(*kept)] * first,
        "forward_attention",
        smem=2,
        anys=3 + len(pieces) + (3 if first else 1),
        out_anys=3 + first,
    )


def feed_kernel(n_pieces, half, groups, meta, inputs, dout, bo, gain, shift, bup, bdn, *refs):
    parts, refs = refs[:groups], refs[groups:]
    shards, pieces, refs = refs[:3], refs[3 : 3 + n_pieces], refs[3 + n_pieces :]
    g_parts, refs = refs[:groups], refs[groups:]
    deltas, refs = refs[:groups], refs[groups:]
    sums, output_out, g_resid_out, *refs = refs
    keep, send, refs = refs[:half], refs[half : 2 * half], refs[2 * half :]
    w, mixed, resid, hat, rstd, second, hidden, g_up, g_sec, low, output, grads, *sems = refs
    sem, grad_sems, out_sems = sems
    wait = load_weights(meta, shards, 0, pieces, w, sem)
    wo_t, wup, wdn_t = w.at[0], w.at[1], w.at[2]
    tokens, width = inputs.shape
    per = SHARD // groups
    for g in range(groups):
        for t in range(width // SHARD):
            at = t * SHARD + g * per
            mixed[:, at : at + per] = parts[g][:, t * per : (t + 1) * per]
    sums[...] = jnp.zeros(sums.shape, F32)
    sums[4:5, :] = jnp.sum(dout[...].astype(F32), axis=0, keepdims=True)
    wait()
    resid[...] = inputs[...].astype(F32) + dot_nt(mixed[...], wo_t[...]) + bo[...]

    @pl.loop(0, tokens // BLOCK)
    def _(i):
        rows = pl.ds(pl.multiple_of(i * BLOCK, BLOCK), BLOCK)
        h, r = normalise(resid[rows, :])
        hat[rows, :] = h
        rstd[rows, :] = jnp.broadcast_to(r, (BLOCK, 128))
        second[rows, :] = (h * gain[...] + shift[...]).astype(BF16)

    for n in range(width // TILE):
        cols = slice(n * TILE, (n + 1) * TILE)
        up = dot_nn(second[...], wup[:, cols]) + bup[:, cols]
        d_hidden = dot_nn(dout[...], wdn_t[:, cols])
        phi = 0.5 + 0.5 * lax.erf(up * (0.5**0.5))
        hidden[:, cols] = (up * phi).astype(BF16)
        slope = phi + up * (jnp.exp(-0.5 * up * up) * (0.5 / math.pi) ** 0.5)
        grad = (d_hidden * slope).astype(BF16)
        g_up[:, cols] = grad
        sums[3:4, cols] = jnp.sum(grad.astype(F32), axis=0, keepdims=True)
    g_sec[...] = dot_nt(g_up[...], wup[...])
    output[...] = (resid[...] + dot_nt(hidden[...], wdn_t[...]) + bdn[...]).astype(BF16)
    out_copy = pltpu.make_async_copy(output, output_out, out_sems.at[0])
    out_copy.start()
    grads[2] = dot_tn(dout[...], hidden[...]).astype(BF16)
    grads[1] = dot_tn(second[...], g_up[...]).astype(BF16)
    store_grads(meta, grads, keep, send, grad_sems, 1, 3)

    @pl.loop(0, tokens // ROWS)
    def _(i):
        rows = pl.ds(pl.multiple_of(i * ROWS, ROWS), ROWS)
        h, g = hat[rows, :], g_sec[rows, :]
        res = dout[rows, :].astype(F32) + norm_back(g, h, rstd[rows, :1], gain[...])
        resid[rows, :] = res
        low[rows, :] = res.astype(BF16)
        for n, x in enumerate((res, g * h, g)):
            sums[n : n + 1, :] += jnp.sum(x, axis=0, keepdims=True)

    resid_copy = pltpu.make_async_copy(resid, g_resid_out, out_sems.at[1])
    resid_copy.start()
    grads[0] = dot_tn(low[...], mixed[...]).astype(BF16)
    store_grads(meta, grads, keep, send, grad_sems, 0, 1)
    ones = jnp.ones((8, HEAD_DIM), BF16)
    for n in range(width // TILE):
        cols = slice(n * TILE, (n + 1) * TILE)
        grad = dot_nn(low[...], wo_t[:, cols]).astype(BF16)
        prod = grad.astype(F32) * mixed[:, cols].astype(F32)
        high = prod.astype(BF16)
        rest_of = (prod - high.astype(F32)).astype(BF16)
        for i in range(TILE // HEAD_DIM):
            part = slice(i * HEAD_DIM, (i + 1) * HEAD_DIM)
            total = dot_nt(ones, high[:, part]) + dot_nt(ones, rest_of[:, part])
            at = n * TILE + i * HEAD_DIM
            t, g, inside = at // SHARD, at % SHARD // per, at % per
            to = t * per + inside
            g_parts[g][:, to : to + HEAD_DIM] = grad[:, part]
            h = to // HEAD_DIM
            deltas[g][h : h + 1, :] = total[:1]
    out_copy.wait()
    resid_copy.wait()
    grads_stored(keep, send, grad_sems)


def feed_forward(
    meta, inner, inputs, dout, bo, gain, shift, bup, bdn, parts, shards, pieces
):
    tokens, width = inputs.shape
    groups = len(parts)
    half, piece = travelling(inner, width, SHARD)
    travel = [(piece, BF16)] * (2 * half)
    wide = pltpu.VMEM((tokens, width), F32)
    slim = pltpu.VMEM((tokens, width), BF16)
    return call(
        functools.partial(feed_kernel, len(pieces), half, groups),
        [(parts[0].shape, BF16)] * groups
        + [((width // HEAD_DIM // groups, tokens), F32)] * groups
        + [((8, width), F32), ((tokens, width), BF16), ((tokens, width), F32)]
        + travel,
        [meta, inputs, dout, bo, gain, shift, bup, bdn, *parts, *shards, *pieces],
        [
            pltpu.VMEM((3, width, width), BF16),
            slim,
            wide,
            wide,
            pltpu.VMEM((tokens, 128), F32),
            slim,
            slim,
            slim,
            wide,
            slim,
            slim,
            pltpu.VMEM((3, width, width), BF16),
            pltpu.SemaphoreType.DMA,
            pltpu.SemaphoreType.DMA((2, half)),
            pltpu.SemaphoreType.DMA((2,)),
        ],
        "feed_forward",
        smem=1,
        anys=3 + len(pieces),
        out_anys=2 + 2 * half,
    )


def backward_kernel(half, meta, rng, segq, segk, lse, delta, q, do, k, v, low_in, *refs):
    sums, dq_out, dk_out, dv_out, keep, send, *refs = refs
    keep, send = [[x.at[jj] for jj in range(half)] for x in (keep, send)]
    low, dq, dk, dv, dk_acc, dv_acc, dq_acc, grads, sems, grad_sems = refs
    low_copy = pltpu.make_async_copy(low_in, low, sems.at[3])
    low_copy.start()
    tokens, width = q.shape
    start, stop = tokens - FAR, 2 * tokens + FAR
    near, middle = slice(start, stop), slice(tokens, 2 * tokens)
    before, after = used_chunks(rng)
    scale = HEAD_DIM**-0.5

    def zero(rows):
        dk_acc[rows, :] = jnp.zeros((rows.stop - rows.start, width), F32)
        dv_acc[rows, :] = jnp.zeros((rows.stop - rows.start, width), F32)

    def narrow(rows):
        dk[rows, :] = (dk_acc[rows, :] * scale).astype(BF16)
        dv[rows, :] = dv_acc[rows, :].astype(BF16)

    def ends(act):
        pl.when(before)(lambda: act(slice(0, start)))
        pl.when(after)(lambda: act(slice(stop, 3 * tokens)))

    zero(near)
    ends(zero)
    attend_back(rng, segq, segk, lse, delta, q, do, k, v, dq, dk_acc, dv_acc, dq_acc)
    narrow(near)
    ends(narrow)
    outs = [
        pltpu.make_async_copy(x, out, sems.at[i])
        for i, (x, out) in enumerate(((dq, dq_out), (dk, dk_out), (dv, dv_out)))
    ]
    for x in outs:
        x.start()

    low_copy.wait()
    grads[0] = dot_tn(low[middle, :], dq[...]).astype(BF16)
    grads[1] = dot_tn(low[near, :], dk[near, :]).astype(BF16)
    grads[2] = dot_tn(low[near, :], dv[near, :]).astype(BF16)
    sums[...] = jnp.zeros(sums.shape, F32)
    sums[0:1, :] = jnp.sum(dq[...].astype(F32), axis=0, keepdims=True)
    sums[1:2, :] = jnp.sum(dv[near, :].astype(F32), axis=0, keepdims=True)
    for i, used in enumerate((before, after)):

        @pl.when(used)
        def _():
            rows = slice(i * stop, i * stop + start)
            sums[1:2, :] += jnp.sum(dv[rows, :].astype(F32), axis=0, keepdims=True)
            for m, x in ((1, dk), (2, dv)):
                more = dot_tn(low[rows, :], x[rows, :])
                grads[m] = (grads[m].astype(F32) + more).astype(BF16)

    store_grads(meta, grads, keep, send, grad_sems, 0, 3)
    for x in outs:
        x.wait()
    grads_stored(keep, send, grad_sems)


def backward(meta, rng, segq, segk, lse, delta, q, do, k, v, low, inner):
    tokens, cols = q.shape
    width = low.shape[1]
    window = 3 * tokens
    per = cols // (width // SHARD)
    half, piece = travelling(inner, width, per)
    travel = [((half, *piece), BF16)] * 2
    slim, wide = (tokens, cols), (window, cols)
    return call(
        functools.partial(backward_kernel, half),
        [((8, cols), F32), (slim, BF16), (wide, BF16), (wide, BF16)] + travel,
        [meta, rng, segq, segk, lse, delta, q, do, k, v, low],
        [
            pltpu.VMEM((window, width), BF16),
            pltpu.VMEM(slim, BF16),
            pltpu.VMEM(wide, BF16),
            pltpu.VMEM(wide, BF16),
            pltpu.VMEM(wide, F32),
            pltpu.VMEM(wide, F32),
            pltpu.VMEM((cols // HEAD_DIM, HEAD_DIM, BLOCK), F32),
            pltpu.VMEM((3, width, cols), BF16),
            pltpu.SemaphoreType.DMA((4,)),
            pltpu.SemaphoreType.DMA((2, half)),
        ],
        "backward_attention",
        smem=2,
        anys=1,
        out_anys=5,
    )


def halo_grads_kernel(n_pieces, off, more, meta, rng, *refs):
    if more:
        left_in, right_in, *refs = refs
    ins, refs = refs[:2], refs[2:]
    shards, pieces, refs = refs[:3], refs[3 : 3 + n_pieces], refs[3 + n_pieces :]
    left, right, dk, dv, w, sem, sems = refs
    wait = load_weights(meta, shards, off, pieces, w, sem)
    loads = [
        pltpu.make_async_copy(x, to, sems.at[i]) for i, (x, to) in enumerate(zip(ins, (dk, dv)))
    ]
    for x in loads:
        x.start()
    tokens = left.shape[0]
    before, after = used_chunks(rng)
    wait()
    for x in loads:
        x.wait()

    def halo_grads(out, old, to, rows):
        res = dot_nt(dk[rows, :], w[1]) + dot_nt(dv[rows, :], w[2])
        if more:
            res = res + old[to, :].astype(F32)
        out[to, :] = res.astype(BF16)

    lows, highs = slice(0, tokens - FAR), slice(tokens - FAR, tokens)
    firsts, others = slice(0, FAR), slice(FAR, tokens)
    for out, old, used, far_to, near_to, base in (
        (left, left_in if more else None, before, lows, highs, 0),
        (right, right_in if more else None, after, others, firsts, 2 * tokens),
    ):
        halo_grads(out, old, near_to, slice(base + near_to.start, base + near_to.stop))

        @pl.when(used)
        def _():
            halo_grads(out, old, far_to, slice(base + far_to.start, base + far_to.stop))

        @pl.when(jnp.logical_not(used))
        def _():
            if more:
                out[far_to, :] = old[far_to, :]
            else:
                out[far_to, :] = jnp.zeros((tokens - FAR, out.shape[1]), BF16)


def halo_grads(group, meta, rng, old, dk, dv, shards, pieces):
    cols = dk.shape[1]
    width = shards[0].shape[0]
    per = pieces[0].shape[3]
    full = (dk.shape[0] // 3, width)
    return call(
        functools.partial(halo_grads_kernel, len(pieces), group * per, len(old) > 0),
        [(full, BF16), (full, BF16)],
        [meta, rng, *old, dk, dv, *shards, *pieces],
        [
            pltpu.VMEM(dk.shape, BF16),
            pltpu.VMEM(dv.shape, BF16),
            pltpu.VMEM((3, width, cols), BF16),
            pltpu.SemaphoreType.DMA,
            pltpu.SemaphoreType.DMA((2,)),
        ],
        "halo_grads",
        smem=2,
        anys=5 + len(pieces),
    )


def input_grads_kernel(n_pieces, off, count, meta, rng, *refs):
    ins, refs = refs[:8], refs[8:]
    shards, pieces, refs = refs[:3], refs[3 : 3 + n_pieces], refs[3 + n_pieces :]
    own, sums, dq, dk, dv, *refs = refs
    x_left, x_own, x_right, left, right, w, sem, sems = refs
    tokens = dq.shape[0]
    wait = load_weights(meta, shards, off, pieces, w, sem)
    middle = pl.ds(tokens, tokens)
    ins = (ins[0], ins[1].at[middle], ins[2].at[middle], *ins[3:])
    loads = [
        pltpu.make_async_copy(x, to, sems.at[i])
        for i, (x, to) in enumerate(zip(ins, (dq, dk, dv, x_left, x_own, x_right, left, right)))
    ]
    for x in loads:
        x.start()
    before, after = used_chunks(rng)
    wait()
    for x in loads:
        x.wait()
    own[...] = dot_nt(dk[...], w[1]) + dot_nt(dv[...], w[2]) + dot_nt(dq[...], w[0])
    sums[...] = jnp.zeros(sums.shape, F32)

    def tally(grad, x, lo, hi):
        @pl.loop(lo, hi)
        def _(i):
            rows = pl.ds(pl.multiple_of(i * ROWS, ROWS), ROWS)
            hat, _ = normalise(x[rows, :].astype(F32))
            g = grad[rows, :].astype(F32)
            sums[0:1, :] += jnp.sum(g * hat, axis=0, keepdims=True)
            sums[1:2, :] += jnp.sum(g, axis=0, keepdims=True)

    tally(own, x_own, 0, tokens // ROWS)
    if count:
        tally(left, x_left, jnp.where(before, 0, (tokens - FAR) // ROWS), tokens // ROWS)
        tally(right, x_right, 0, jnp.where(after, tokens, FAR) // ROWS)


def input_grads(group, meta, rng, dq, dk, dv, window, halos, count, shards, pieces):
    tokens, cols = dq.shape
    width = shards[0].shape[0]
    per = pieces[0].shape[3]
    full = (tokens, width)
    return call(
        functools.partial(input_grads_kernel, len(pieces), group * per, count),
        [(full, F32), ((8, width), F32)],
        [meta, rng, dq, dk, dv, *window, *halos, *shards, *pieces],
        [pltpu.VMEM(dq.shape, BF16)] * 3
        + [pltpu.VMEM(full, BF16)] * 5
        + [
            pltpu.VMEM((3, width, cols), BF16),
            pltpu.SemaphoreType.DMA,
            pltpu.SemaphoreType.DMA((8,)),
        ],
        "input_grads",
        smem=2,
        anys=11 + len(pieces),
    )


def last_kernel(inputs, g_resid, from_left, from_right, gain, *refs):
    *owns, g_inputs = refs

    @pl.loop(0, inputs.shape[0] // ROWS)
    def _(i):
        rows = pl.ds(pl.multiple_of(i * ROWS, ROWS), ROWS)
        hat, rstd = normalise(inputs[rows, :].astype(F32))
        g = from_left[rows, :].astype(F32) + from_right[rows, :].astype(F32)
        for own in owns:
            g = g + own[rows, :]
        g_inputs[rows, :] = (g_resid[rows, :] + norm_back(g, hat, rstd, gain[...])).astype(BF16)


def last_step(inputs, g_resid, from_left, from_right, gain, owns):
    return call(
        last_kernel,
        [(inputs.shape, BF16)],
        [inputs, g_resid, from_left, from_right, gain, *owns],
        [],
        "input_norm_grads",
    )


def lay_out_kernel(turned, groups, size, meta, *refs):
    outs = refs[-len(turned) :]
    pieces = refs[: -len(turned)]
    n = len(pieces) // groups
    s = meta[0]
    per = pieces[0].shape[-1]
    for g in range(groups):
        to = slice(g * per, (g + 1) * per)
        if n == 1:
            whole = [
                (pieces[g].at[i], slice(i * size, (i + 1) * size))
                for i in range(pieces[g].shape[0])
            ]
        else:
            whole = [
                (pieces[g * n + j], pl.ds(pl.multiple_of((s ^ j) * size, size), size))
                for j in range(n)
            ]
        for piece, at in whole:
            for m, turn in enumerate(turned):
                part = piece[m, :size].astype(F32)
                if turn:
                    outs[m][to, at] = jnp.transpose(part)
                else:
                    outs[m][at, to] = part


def lay_out(meta, width, groups, turned):
    first = groups[0]
    size = width // (len(first) if len(first) > 1 else first[0].shape[0])
    shapes = [(SHARD, width) if turn else (width, SHARD) for turn in turned]
    return call(
        functools.partial(lay_out_kernel, turned, len(groups), size),
        [(shape, F32) for shape in shapes],
        [meta, *[piece for group in groups for piece in group]],
        [],
        "lay_out_grads",
        smem=1,
    )


def pause_kernel(x, out):
    out[...] = x[...]


def pause(x):
    (out,) = call(pause_kernel, [(x.shape, x.dtype)], [x], [], "pause")
    return out


SHARD = 256


def make_body(n_seq, n_tp):
    inner = min(n_seq, 8)
    outer = n_seq // inner
    half = inner // 2
    masks = [2 * jj for jj in range(1, half)]

    def shift(x, by):
        pairs = [(i, i + by) for i in range(n_tp) if 0 <= i + by < n_tp]
        return lax.ppermute(x, "tp", pairs)

    def swap(x, mask):
        return lax.ppermute(x, "seq", [(i, i ^ mask) for i in range(n_seq)])

    def tie(*xs):
        return lax.optimization_barrier(xs)

    def block_of(shards, biases, off, per, s):
        size = shards[0].shape[0] // inner
        cut = jnp.stack([lax.dynamic_slice(w, (s * size, off), (size, per)) for w in shards])
        if biases:
            parts = []
            rest = jnp.stack([b[off : off + per] for b in biases])
            for _ in range(3):
                part = rest.astype(BF16)
                rest = rest - part.astype(F32)
                parts.append(part)
            parts = jnp.stack(parts + [jnp.zeros_like(parts[0])] * 13, axis=1)
            cut = jnp.concatenate([cut, parts], axis=1)
        return jnp.broadcast_to(cut[None], (n_tp, *cut.shape))

    def over_tp(block):
        return lax.all_to_all(block, "tp", 0, 0, tiled=True)

    def others_of(got, size, t):
        return jnp.stack(
            [lax.dynamic_index_in_dim(got, lax.rem(t + r + 1, n_tp), 0, keepdims=False)[:, :size]
             for r in range(n_tp - 1)]
        )

    def biases_of(got, size):
        whole = jnp.sum(got[:, :, size : size + 3].astype(F32), axis=2)
        return [whole[:, m].reshape(1, -1) for m in range(whole.shape[1])]

    def from_chips(x):
        return [x] + [swap(x, mask) for mask in masks]

    def from_cores(even):
        odd = [swap(e, 1) for e in even]
        return [e for pair in zip(even, odd) for e in pair]

    def core_sums(keep, got):
        return [(k.astype(F32) + g.astype(F32)).astype(BF16) for k, g in zip(keep, got)]

    def over_chips(sums):
        return [sums[0]] + [swap(sums[jj], 2 * jj) for jj in range(1, half)]

    def chip_sum(moved):
        total = moved[0].astype(F32)
        for x in moved[1:]:
            total = total + x.astype(F32)
        total = total.astype(BF16)
        if outer > 1:
            groups = [[i + inner * o for o in range(outer)] for i in range(inner)]
            total = lax.psum(total, "seq", axis_index_groups=groups)
        return total

    def own_shard(total):
        got = lax.all_to_all(total, "tp", 0, 0, tiled=True)
        return jnp.sum(got.astype(F32), axis=0).astype(BF16)

    def body(
        inputs, segment_ids, row_lengths, norm1_gain, norm1_shift, w_query, w_key, w_value,
        b_query, b_value, w_out, b_out, norm2_gain, norm2_shift, w_up, b_up, w_down, b_down,
        out_grad,
    ):
        tokens, width = inputs.shape
        halo = tokens
        t = lax.axis_index("tp")
        s = lax.rem(lax.axis_index("seq"), inner)
        meta = jnp.stack([s, t]).astype(jnp.int32)
        per = SHARD // GROUPS
        every = range(GROUPS)
        zero = jnp.zeros_like(b_query)

        def row(x):
            return x.reshape(1, -1)

        def by_shard(groups):
            cols = [x.reshape(n_tp, per) for x in groups]
            return jnp.concatenate(cols, axis=1).reshape(1, width)

        attn_w = [w_query, w_key, w_value]
        attn_b = [b_query, b_up, b_value]
        size = width // inner
        feed_w = [w_out.T, w_up, w_down.T]
        feed_block = block_of(feed_w, [], 0, SHARD, s)
        attn_p, attn_whole = [], []
        for g in every:
            got = over_tp(block_of(attn_w, attn_b, g * per, per, s))
            got, feed_block = tie(got, feed_block)
            even = from_chips(others_of(got, size, t))
            even[0], even[-1] = tie(even[0], even[-1])
            attn_p.append(from_cores(even))
            attn_whole.append(biases_of(got, size))
        got = over_tp(feed_block)
        inputs_later, got = tie(inputs, got)
        feed_p = from_chips(others_of(got, size, t))
        left = shift(inputs_later, 1)
        right = shift(inputs_later, -1)

        position = jnp.arange(ROW_LEN, dtype=jnp.int32)
        numbers = jnp.where(position < row_lengths[0], segment_ids[0], 4096 + position)
        numbers = jnp.concatenate(
            [jnp.full((halo,), -1, jnp.int32), numbers, jnp.full((halo,), 1 << 20, jnp.int32)]
        )
        seg_win = lax.dynamic_slice_in_dim(numbers, t * tokens, tokens + 2 * halo, 0)
        seg_mine = seg_win[halo : halo + tokens]
        first = seg_mine[::BLOCK]
        last = seg_mine[BLOCK - 1 :: BLOCK]
        low = jnp.sum((seg_win[None, :] < first[:, None]).astype(jnp.int32), axis=1)
        high = jnp.sum((seg_win[None, :] <= last[:, None]).astype(jnp.int32), axis=1)
        rng = jnp.stack([low // BLOCK, (high + BLOCK - 1) // BLOCK])
        segq, segk = seg_mine[None, :], seg_win[:, None]

        gain1, feed_w[0], feed_w[2] = tie(norm1_gain, feed_w[0], feed_w[2])
        source = (row(gain1), row(norm1_shift), left, inputs, right)
        saved = []
        for g in every:
            bq, _, bv = attn_whole[g]
            res = forward(g, meta, rng, segq, segk, source, bq, bv, attn_w, attn_p[g])
            mixed, lse, q, k, v = res[:5]
            if g == 0:
                source = first_low = res[5]
                mixed, *feed_p = tie(mixed, *feed_p)
                feed_p = from_cores(feed_p)
            saved.append((mixed, lse, q, k, v))
        bup = by_shard([x[1] for x in attn_whole])
        res = feed_forward(
            meta, inner, inputs, out_grad, row(b_out), row(norm2_gain), row(norm2_shift), bup,
            row(b_down), [x[0] for x in saved], feed_w, feed_p,
        )
        g_mixed, delta = list(res[:GROUPS]), res[GROUPS : 2 * GROUPS]
        sums_feed, output, g_resid, *travel = res[2 * GROUPS :]

        sums = core_sums(travel[:half], [swap(x, 1) for x in travel[half:]])
        feed_moved = over_chips(sums)
        g_mixed[0], *feed_moved[:1] = tie(g_mixed[0], *feed_moved[:1])
        old, owns, sums_qkv, totals = (), [], [], []
        for g in every:
            _, lse, q, k, v = saved[g]
            vec, dq, dk, dv, keep, send = backward(
                meta, rng, segq, segk, lse, delta[g], q, g_mixed[g], k, v, first_low, inner
            )
            sums_qkv.append(vec)
            got = swap(send, 1)
            if g == 0:
                feed_total = chip_sum(feed_moved)
                feed_total, sums_feed = tie(feed_total, sums_feed)
                got, sums_feed = tie(got, pause(sums_feed))
            sums = [None] * half
            for jj in reversed(range(half)):
                (sums[jj],) = core_sums(keep[jj : jj + 1], got[jj : jj + 1])
                keep, got, sums[jj] = tie(keep, got, sums[jj])
            if g + 1 == GROUPS:
                dk, *sums = tie(dk, *sums)
            old = halo_grads(g, meta, rng, old, dk, dv, attn_w, attn_p[g])
            own, sums_in = input_grads(
                g, meta, rng, dq, dk, dv, (left, inputs, right), old, g + 1 == GROUPS,
                attn_w, attn_p[g],
            )
            if g + 1 < GROUPS:
                g_mixed[g + 1], own, *sums = tie(g_mixed[g + 1], own, *sums)
            owns.append(own)
            moved = over_chips(sums)
            if g + 1 == GROUPS:
                feed_g = feed_total.reshape(-1, SHARD)
                feed_g = lax.psum_scatter(feed_g, "tp", scatter_dimension=0, tiled=True)
                moved[0], sums_in, feed_g = tie(moved[0], sums_in, feed_g)
            totals.append(chip_sum(moved))
        from_right = shift(old[0], -1)
        from_left = shift(old[1], 1)
        piece = feed_total.shape[1:]
        feed_g = lax.all_gather(feed_g.reshape(piece), "seq", axis=0)[:inner]
        (g_inputs,) = last_step(
            inputs, g_resid, from_left, from_right, row(norm1_gain), owns
        )

        vectors = [by_shard([x[i] for x in sums_qkv]) for i in range(2)]
        vectors = jnp.concatenate([sums_in[:2], *vectors, sums_feed[:5]])
        if outer > 1:
            groups = [[i + inner * o for o in range(outer)] for i in range(inner)]
            vectors = lax.psum(vectors, "seq", axis_index_groups=groups)
        extra = -(-vectors.size // (48 * per)) * 16
        n_vec = vectors.size
        vectors = jnp.pad(vectors.astype(BF16).reshape(-1), (0, 3 * extra * per - n_vec))
        vectors = jnp.broadcast_to(vectors.reshape(1, 3, extra, per), (n_tp, 3, extra, per))
        totals[-1] = jnp.concatenate([totals[-1], vectors], axis=2)
        shards = [own_shard(x) for x in totals]
        shards[-1], g_inputs = tie(shards[-1], g_inputs)
        pieces = [from_cores(from_chips(x)) for x in shards]
        vectors = sum([x[:, size:].astype(F32) for x in pieces[-1]])
        vectors = vectors.reshape(-1)[:n_vec].reshape(-1, width)
        n1g, n1s, g_bq, g_bv, g_bo, n2g, n2s, g_bup, g_bdn = [vectors[i] for i in range(9)]

        g_wo, g_wup, g_wdn = lay_out(meta, width, [[feed_g]], (True, False, True))
        g_wup, pieces[-1][1] = tie(g_wup, pieces[-1][1])
        g_wq, g_wk, g_wv = lay_out(meta, width, pieces, (False, False, False))

        def shard(x):
            return lax.dynamic_slice_in_dim(x, t * SHARD, SHARD, 0)

        return (
            output, g_inputs, n1g, n1s, g_wq, g_wk, g_wv, shard(g_bq), shard(g_bv),
            g_wo, g_bo, n2g, n2s, g_wup, shard(g_bup), g_wdn, g_bdn,
        )

    return body


def solution(mesh):
    tok = P(("seq", "tp"), None)
    col, row, vec, rep = P(None, "tp"), P("tp", None), P("tp"), P()
    in_specs = (
        tok, P("seq", None), P("seq"), rep, rep, col, col, col, vec, vec,
        row, rep, rep, rep, col, vec, row, rep, tok,
    )
    out_specs = (
        tok, tok, rep, rep, col, col, col, vec, vec,
        row, rep, rep, rep, col, vec, row, rep,
    )
    body = make_body(mesh.shape["seq"], mesh.shape["tp"])
    return jax.shard_map(body, mesh=mesh, in_specs=in_specs, out_specs=out_specs, check_vma=False)
```

```python
import functools
import math

import jax
import jax.numpy as jnp
from jax import lax
from jax.experimental import pallas as pl
from jax.experimental.pallas import tpu as pltpu
from jax.sharding import PartitionSpec as P

HEAD_DIM = 128
ROW_LEN = 2048
NORM_EPS = 1e-05
MASKED = -1000000000.0
LOG2E = 1.4426950408889634
TILE = 256
BLOCK = 256
FAR = 256
ROWS = 128
GROUPS = 1
F32 = jnp.float32
BF16 = jnp.bfloat16
VMEM_LIMIT = 58 * 1024 * 1024


def dot_nn(a, b):
    return lax.dot_general(a, b, (((1,), (0,)), ((), ())), preferred_element_type=F32)


def dot_nt(a, b):
    return lax.dot_general(a, b, (((1,), (1,)), ((), ())), preferred_element_type=F32)


def dot_tn(a, b):
    return lax.dot_general(a, b, (((0,), (0,)), ((), ())), preferred_element_type=F32)


def normalise(x):
    centre = x - jnp.mean(x, axis=-1, keepdims=True)
    rstd = lax.rsqrt(jnp.mean(centre * centre, axis=-1, keepdims=True) + NORM_EPS)
    return centre * rstd, rstd


def norm_back(grad, hat, rstd, gain):
    t = gain * grad
    mean_t = jnp.mean(t, axis=-1, keepdims=True)
    mean_th = jnp.mean(t * hat, axis=-1, keepdims=True)
    return (t - mean_t - hat * mean_th) * rstd


def call(kernel, outs, ins, scratch, name, smem=0, anys=0, out_anys=0, gflop=50):
    spaces = [pltpu.SMEM] * smem + [pltpu.VMEM] * (len(ins) - smem - anys) + [pl.ANY] * anys
    out_spaces = [pltpu.VMEM] * (len(outs) - out_anys) + [pl.ANY] * out_anys
    return pl.pallas_call(
        kernel,
        out_shape=tuple(jax.ShapeDtypeStruct(*o) for o in outs),
        in_specs=[pl.BlockSpec(memory_space=m) for m in spaces],
        out_specs=tuple(pl.BlockSpec(memory_space=m) for m in out_spaces),
        scratch_shapes=scratch,
        compiler_params=pltpu.CompilerParams(vmem_limit_bytes=VMEM_LIMIT),
        cost_estimate=pl.CostEstimate(
            flops=gflop * 10**9, bytes_accessed=1000000, transcendentals=0
        ),
        name=name,
    )(*ins)


def load_weights(meta, shards, off, pieces, dst, sem, skipped=0):
    s, t = meta[0], meta[1]
    _, size, per = pieces[0].shape[1:]
    last = skipped + dst.shape[0]
    n_tp = dst.shape[2] // per
    mine = pl.ds(pl.multiple_of(t * per, per), per)
    for m in range(dst.shape[0]):
        source = shards[skipped + m].at[:, off : off + per]
        pltpu.make_async_copy(source, dst.at[m, :, mine], sem).start()
    for j, piece in enumerate(pieces):
        at = pl.ds(pl.multiple_of((s ^ j) * size, size), size)
        for r in range(n_tp - 1):
            u = pl.multiple_of(lax.rem(t + r + 1, n_tp) * per, per)
            source = piece.at[r, skipped:last]
            pltpu.make_async_copy(source, dst.at[:, at, pl.ds(u, per)], sem).start()
    return pltpu.make_async_copy(dst, dst, sem).wait


def store_grads(meta, grads, keep, send, sems, first, last):
    s = meta[0]
    n_tp, _, size, per = keep[0].shape
    for parity, dst in enumerate((keep, send)):
        for jj, piece in enumerate(dst):
            p = pl.ds(pl.multiple_of((s ^ (2 * jj + parity)) * size, size), size)
            for t in range(n_tp):
                pltpu.make_async_copy(
                    grads.at[first:last, p, t * per : (t + 1) * per],
                    piece.at[t, first:last],
                    sems.at[parity, jj],
                ).start()


def grads_stored(keep, send, sems):
    for parity, dst in enumerate((keep, send)):
        for jj, piece in enumerate(dst):
            pltpu.make_async_copy(piece, piece, sems.at[parity, jj]).wait()


def travelling(inner, width, per):
    half = max(inner // 2, 1)
    return half, (width // SHARD, 3, width // inner, per)


def attend(rng, segq, segk, q, k, v, mixed, lse, s_scr, m_scr, l_scr, acc):
    heads = q.shape[1] // HEAD_DIM
    coef = HEAD_DIM**-0.5 * LOG2E
    of = [slice(h * HEAD_DIM, (h + 1) * HEAD_DIM) for h in range(heads)]

    def fold(x, op):
        x = x.reshape(BLOCK // 8, 8, BLOCK)
        res = x[0]
        for i in range(1, BLOCK // 8):
            res = op(res, x[i])
        return res

    @pl.loop(0, q.shape[0] // BLOCK)
    def _(qb):
        rows = pl.ds(pl.multiple_of(qb * BLOCK, BLOCK), BLOCK)
        lo = rng[0, qb]
        hi = rng[1, qb]
        sq = segq[:, rows]
        m_scr[...] = jnp.full(m_scr.shape, -3e38, F32)
        l_scr[...] = jnp.zeros(l_scr.shape, F32)
        acc[...] = jnp.zeros(acc.shape, F32)

        @pl.loop(lo, hi)
        def _(kc):
            ks = pl.ds(pl.multiple_of(kc * BLOCK, BLOCK), BLOCK)
            bias = jnp.where(segk[ks, :] == sq, 0.0, MASKED)
            for h in range(0, heads, 2):
                pair = (h, h + 1)
                scores = [dot_nt(k[ks, of[i]], q[rows, of[i]]) * coef + bias for i in pair]
                for i, s in zip(pair, scores):
                    s_scr[kc, i] = s
                    m_scr[i] = jnp.maximum(m_scr[i], fold(s, jnp.maximum))

        for h in range(heads):
            m_scr[h] = jnp.broadcast_to(jnp.max(m_scr[h], axis=0, keepdims=True), (8, BLOCK))

        @pl.loop(lo, hi)
        def _(kc):
            ks = pl.ds(pl.multiple_of(kc * BLOCK, BLOCK), BLOCK)
            for h in range(0, heads, 2):
                pair = (h, h + 1)
                probs = [jnp.exp2(s_scr[kc, i] - m_scr[i, :1]) for i in pair]
                outs = [dot_tn(v[ks, of[i]], p.astype(BF16)) for i, p in zip(pair, probs)]
                for i, p, o in zip(pair, probs, outs):
                    l_scr[i] += fold(p, jnp.add)
                    acc[i] += o

        for h in range(heads):
            total = jnp.sum(l_scr[h], axis=0, keepdims=True)
            mixed[rows, of[h]] = jnp.transpose(acc[h] / total).astype(BF16)
            lse[h : h + 1, rows] = m_scr[h, :1] + jnp.log2(total)


def attend_back(rng, segq, segk, lse, delta, q, do, k, v, dq, dk_acc, dv_acc, dq_acc):
    heads = q.shape[1] // HEAD_DIM
    scale = HEAD_DIM**-0.5
    coef = scale * LOG2E
    of = [slice(h * HEAD_DIM, (h + 1) * HEAD_DIM) for h in range(heads)]

    @pl.loop(0, q.shape[0] // BLOCK)
    def _(qb):
        rows = pl.ds(pl.multiple_of(qb * BLOCK, BLOCK), BLOCK)
        lo = rng[0, qb]
        hi = rng[1, qb]
        sq = segq[:, rows]
        dq_acc[...] = jnp.zeros(dq_acc.shape, F32)

        @pl.loop(lo, hi)
        def _(kc):
            ks = pl.ds(pl.multiple_of(kc * BLOCK, BLOCK), BLOCK)
            bias = jnp.where(segk[ks, :] == sq, 0.0, MASKED)

            def probs(h):
                s = dot_nt(k[ks, of[h]], q[rows, of[h]]) * coef
                p = jnp.exp2(s + (bias - lse[h : h + 1, rows]))
                return p, dot_nt(v[ks, of[h]], do[rows, of[h]])

            def products(h, p, dp):
                ds = (p * (dp - delta[h : h + 1, rows])).astype(BF16)
                return (
                    dot_nn(p.astype(BF16), do[rows, of[h]]),
                    dot_nn(ds, q[rows, of[h]]),
                    dot_tn(k[ks, of[h]], ds),
                )

            for h in range(0, heads, 2):
                pair = (h, h + 1)
                both = [probs(i) for i in pair]
                terms = [products(i, *b) for i, b in zip(pair, both)]
                for i, (a, b, c) in zip(pair, terms):
                    dv_acc[ks, of[i]] += a
                    dk_acc[ks, of[i]] += b
                    dq_acc[i] += c

        for h in range(heads):
            dq[rows, of[h]] = (jnp.transpose(dq_acc[h]) * scale).astype(BF16)


def used_chunks(rng):
    tokens = BLOCK * rng.shape[1]
    before = rng[0, 0] * BLOCK < tokens - FAR
    after = rng[1, rng.shape[1] - 1] * BLOCK > 2 * tokens + FAR
    return before, after


def forward_kernel(first, n_pieces, off, meta, rng, segq, segk, *refs):
    if first:
        gain, shift, bq, bv, left, own, right, *refs = refs
    else:
        bq, bv, low_in, *refs = refs
    shards, pieces, refs = refs[:3], refs[3 : 3 + n_pieces], refs[3 + n_pieces :]
    mixed, lse, q_out, k_out, v_out, *refs = refs
    if first:
        low_out, *refs = refs
    q, k, v, low, w, s_scr, m_scr, l_scr, acc, sem, out_sems, *refs = refs
    tokens = q.shape[0]
    before, after = used_chunks(rng)
    lo = jnp.where(before, 0, (tokens - FAR) // BLOCK)
    hi = jnp.where(after, 3 * tokens, 2 * tokens + FAR) // BLOCK

    def copy(i, src, dst):
        return pltpu.make_async_copy(src, dst, out_sems.at[i])

    def chunk(c):
        return pl.ds(pl.multiple_of(c * BLOCK, BLOCK), BLOCK)

    if first:
        (window,) = refs
        ins = [
            copy(i, x, window.at[i * tokens : (i + 1) * tokens])
            for i, x in enumerate((left, own, right))
        ]
    else:
        ins = [copy(3, low_in, low)]
    for x in ins:
        x.start()
    wait = load_weights(meta, shards, off, pieces, w, sem)
    for x in ins:
        x.wait()
    outs = [(q, q_out), (k, k_out), (v, v_out)]
    if first:

        @pl.loop(lo, hi)
        def _(c):
            hat, _ = normalise(window[chunk(c), :].astype(F32))
            low[chunk(c), :] = (hat * gain[...] + shift[...]).astype(BF16)

        outs.append((low, low_out))
        copy(3, *outs[3]).start()
    wait()
    q[...] = (dot_nn(low[tokens : 2 * tokens, :], w[0]) + bq[...]).astype(BF16)
    copy(0, *outs[0]).start()
    def project(rows):
        k[rows, :] = dot_nn(low[rows, :], w[1]).astype(BF16)
        v[rows, :] = (dot_nn(low[rows, :], w[2]) + bv[...]).astype(BF16)

    start, stop = tokens - FAR, 2 * tokens + FAR
    project(slice(start, stop))
    pl.when(before)(lambda: project(slice(0, start)))
    pl.when(after)(lambda: project(slice(stop, 3 * tokens)))

    copy(1, *outs[1]).start()
    copy(2, *outs[2]).start()
    attend(rng, segq, segk, q, k, v, mixed, lse, s_scr, m_scr, l_scr, acc)
    for i, x in enumerate(outs):
        copy(i, *x).wait()


def forward(group, meta, rng, segq, segk, source, bq, bv, shards, pieces):
    first = group == 0
    width = shards[0].shape[0]
    window = segk.shape[0]
    tokens = window // 3
    per = pieces[0].shape[3]
    cols = bq.shape[1]
    heads = cols // HEAD_DIM
    slim, wide = (tokens, cols), (window, cols)
    kept = ((window, width), BF16)
    ins = [meta, rng, segq, segk]
    ins += [*source[:2], bq, bv, *source[2:]] if first else [bq, bv, source]
    return call(
        functools.partial(forward_kernel, first, len(pieces), group * per),
        [(slim, BF16), ((heads, tokens), F32), (slim, BF16), (wide, BF16), (wide, BF16)]
        + [kept] * first,
        [*ins, *shards, *pieces],
        [
            pltpu.VMEM(slim, BF16),
            pltpu.VMEM(wide, BF16),
            pltpu.VMEM(wide, BF16),
            pltpu.VMEM(*kept),
            pltpu.VMEM((3, width, cols), BF16),
            pltpu.VMEM((window // BLOCK, heads, BLOCK, BLOCK), F32),
            pltpu.VMEM((heads, 8, BLOCK), F32),
            pltpu.VMEM((heads, 8, BLOCK), F32),
            pltpu.VMEM((heads, HEAD_DIM, BLOCK), F32),
            pltpu.SemaphoreType.DMA,
            pltpu.SemaphoreType.DMA((4,)),
        ]
        + [pltpu.VMEM(*kept)] * first,
        "forward_attention",
        smem=2,
        anys=3 + len(pieces) + (3 if first else 1),
        out_anys=3 + first,
    )


def feed_kernel(n_pieces, half, groups, meta, inputs, dout, bo, gain, shift, bup, bdn, *refs):
    parts, refs = refs[:groups], refs[groups:]
    shards, pieces, refs = refs[:3], refs[3 : 3 + n_pieces], refs[3 + n_pieces :]
    g_parts, refs = refs[:groups], refs[groups:]
    deltas, refs = refs[:groups], refs[groups:]
    sums, output_out, g_resid_out, *refs = refs
    keep, send, refs = refs[:half], refs[half : 2 * half], refs[2 * half :]
    w, mixed, resid, hat, rstd, second, hidden, g_up, g_sec, low, output, grads, *sems = refs
    first_sem, sem, grad_sems, out_sems = sems
    wo_t, wup, wdn_t = w.at[0], w.at[1], w.at[2]
    wait_first = load_weights(meta, shards, 0, pieces, w.at[:1], first_sem)
    wait = load_weights(meta, shards, 0, pieces, w.at[1:], sem, 1)
    tokens, width = inputs.shape
    per = SHARD // groups
    for g in range(groups):
        for t in range(width // SHARD):
            at = t * SHARD + g * per
            mixed[:, at : at + per] = parts[g][:, t * per : (t + 1) * per]
    sums[...] = jnp.zeros(sums.shape, F32)
    sums[4:5, :] = jnp.sum(dout[...].astype(F32), axis=0, keepdims=True)
    wait_first()
    resid[...] = inputs[...].astype(F32) + dot_nt(mixed[...], wo_t[...]) + bo[...]

    @pl.loop(0, tokens // BLOCK)
    def _(i):
        rows = pl.ds(pl.multiple_of(i * BLOCK, BLOCK), BLOCK)
        h, r = normalise(resid[rows, :])
        hat[rows, :] = h
        rstd[rows, :] = jnp.broadcast_to(r, (BLOCK, 128))
        second[rows, :] = (h * gain[...] + shift[...]).astype(BF16)

    wait()
    for n in range(width // TILE):
        cols = slice(n * TILE, (n + 1) * TILE)
        up = dot_nn(second[...], wup[:, cols]) + bup[:, cols]
        d_hidden = dot_nn(dout[...], wdn_t[:, cols])
        phi = 0.5 + 0.5 * lax.erf(up * (0.5**0.5))
        hidden[:, cols] = (up * phi).astype(BF16)
        slope = phi + up * (jnp.exp(-0.5 * up * up) * (0.5 / math.pi) ** 0.5)
        grad = (d_hidden * slope).astype(BF16)
        g_up[:, cols] = grad
        sums[3:4, cols] = jnp.sum(grad.astype(F32), axis=0, keepdims=True)
    g_sec[...] = dot_nt(g_up[...], wup[...])
    output[...] = (resid[...] + dot_nt(hidden[...], wdn_t[...]) + bdn[...]).astype(BF16)
    out_copy = pltpu.make_async_copy(output, output_out, out_sems.at[0])
    out_copy.start()
    grads[2] = dot_tn(dout[...], hidden[...]).astype(BF16)
    grads[1] = dot_tn(second[...], g_up[...]).astype(BF16)
    store_grads(meta, grads, keep, send, grad_sems, 1, 3)

    @pl.loop(0, tokens // ROWS)
    def _(i):
        rows = pl.ds(pl.multiple_of(i * ROWS, ROWS), ROWS)
        h, g = hat[rows, :], g_sec[rows, :]
        res = dout[rows, :].astype(F32) + norm_back(g, h, rstd[rows, :1], gain[...])
        resid[rows, :] = res
        low[rows, :] = res.astype(BF16)
        for n, x in enumerate((res, g * h, g)):
            sums[n : n + 1, :] += jnp.sum(x, axis=0, keepdims=True)

    resid_copy = pltpu.make_async_copy(resid, g_resid_out, out_sems.at[1])
    resid_copy.start()
    grads[0] = dot_tn(low[...], mixed[...]).astype(BF16)
    store_grads(meta, grads, keep, send, grad_sems, 0, 1)
    grad = dot_nn(low[...], wo_t[...]).astype(BF16)
    prod = grad.astype(F32) * mixed[...].astype(F32)
    high = prod.astype(BF16)
    rest_of = (prod - high.astype(F32)).astype(BF16)
    head_of = lax.broadcasted_iota(jnp.int32, (width, 128), 0) // HEAD_DIM
    member = jnp.where(head_of == lax.broadcasted_iota(jnp.int32, (width, 128), 1), 1.0, 0.0)
    member = member.astype(BF16)
    totals = dot_nn(high, member) + dot_nn(rest_of, member)
    for i in range(0, tokens, 128):
        turned = jnp.transpose(totals[i : i + 128])
        for n in range(width // HEAD_DIM):
            at = n * HEAD_DIM
            t, g, inside = at // SHARD, at % SHARD // per, at % per
            h = (t * per + inside) // HEAD_DIM
            deltas[g][h : h + 1, i : i + 128] = turned[n : n + 1]
    for g in range(groups):
        for t in range(width // SHARD):
            at = t * SHARD + g * per
            g_parts[g][:, t * per : (t + 1) * per] = grad[:, at : at + per]
    out_copy.wait()
    resid_copy.wait()
    grads_stored(keep, send, grad_sems)


def feed_forward(
    meta, inner, inputs, dout, bo, gain, shift, bup, bdn, parts, shards, pieces
):
    tokens, width = inputs.shape
    groups = len(parts)
    half, piece = travelling(inner, width, SHARD)
    travel = [(piece, BF16)] * (2 * half)
    wide = pltpu.VMEM((tokens, width), F32)
    slim = pltpu.VMEM((tokens, width), BF16)
    return call(
        functools.partial(feed_kernel, len(pieces), half, groups),
        [(parts[0].shape, BF16)] * groups
        + [((width // HEAD_DIM // groups, tokens), F32)] * groups
        + [((8, width), F32), ((tokens, width), BF16), ((tokens, width), F32)]
        + travel,
        [meta, inputs, dout, bo, gain, shift, bup, bdn, *parts, *shards, *pieces],
        [
            pltpu.VMEM((3, width, width), BF16),
            slim,
            wide,
            wide,
            pltpu.VMEM((tokens, 128), F32),
            slim,
            slim,
            slim,
            wide,
            slim,
            slim,
            pltpu.VMEM((3, width, width), BF16),
            pltpu.SemaphoreType.DMA,
            pltpu.SemaphoreType.DMA,
            pltpu.SemaphoreType.DMA((2, half)),
            pltpu.SemaphoreType.DMA((2,)),
        ],
        "feed_forward",
        smem=1,
        anys=3 + len(pieces),
        out_anys=2 + 2 * half,
    )


def backward_kernel(half, meta, rng, segq, segk, lse, delta, q, do, k, v, low_in, *refs):
    sums, dq_out, dk_out, dv_out, keep, send, *refs = refs
    keep, send = [[x.at[jj] for jj in range(half)] for x in (keep, send)]
    low, dq, dk, dv, dk_acc, dv_acc, dq_acc, grads, sems, grad_sems = refs
    low_copy = pltpu.make_async_copy(low_in, low, sems.at[3])
    low_copy.start()
    tokens, width = q.shape
    start, stop = tokens - FAR, 2 * tokens + FAR
    near, middle = slice(start, stop), slice(tokens, 2 * tokens)
    before, after = used_chunks(rng)
    scale = HEAD_DIM**-0.5

    def zero(rows):
        dk_acc[rows, :] = jnp.zeros((rows.stop - rows.start, width), F32)
        dv_acc[rows, :] = jnp.zeros((rows.stop - rows.start, width), F32)

    def narrow(rows):
        dk[rows, :] = (dk_acc[rows, :] * scale).astype(BF16)
        dv[rows, :] = dv_acc[rows, :].astype(BF16)

    def ends(act):
        pl.when(before)(lambda: act(slice(0, start)))
        pl.when(after)(lambda: act(slice(stop, 3 * tokens)))

    zero(near)
    ends(zero)
    attend_back(rng, segq, segk, lse, delta, q, do, k, v, dq, dk_acc, dv_acc, dq_acc)
    narrow(near)
    ends(narrow)
    outs = [
        pltpu.make_async_copy(x, out, sems.at[i])
        for i, (x, out) in enumerate(((dq, dq_out), (dk, dk_out), (dv, dv_out)))
    ]
    for x in outs:
        x.start()

    low_copy.wait()
    grads[0] = dot_tn(low[middle, :], dq[...]).astype(BF16)
    grads[1] = dot_tn(low[near, :], dk[near, :]).astype(BF16)
    grads[2] = dot_tn(low[near, :], dv[near, :]).astype(BF16)
    sums[...] = jnp.zeros(sums.shape, F32)
    sums[0:1, :] = jnp.sum(dq[...].astype(F32), axis=0, keepdims=True)
    sums[1:2, :] = jnp.sum(dv[near, :].astype(F32), axis=0, keepdims=True)
    for i, used in enumerate((before, after)):

        @pl.when(used)
        def _():
            rows = slice(i * stop, i * stop + start)
            sums[1:2, :] += jnp.sum(dv[rows, :].astype(F32), axis=0, keepdims=True)
            for m, x in ((1, dk), (2, dv)):
                more = dot_tn(low[rows, :], x[rows, :])
                grads[m] = (grads[m].astype(F32) + more).astype(BF16)

    store_grads(meta, grads, keep, send, grad_sems, 0, 3)
    for x in outs:
        x.wait()
    grads_stored(keep, send, grad_sems)


def backward(meta, rng, segq, segk, lse, delta, q, do, k, v, low, inner):
    tokens, cols = q.shape
    width = low.shape[1]
    window = 3 * tokens
    per = cols // (width // SHARD)
    half, piece = travelling(inner, width, per)
    travel = [((half, *piece), BF16)] * 2
    slim, wide = (tokens, cols), (window, cols)
    return call(
        functools.partial(backward_kernel, half),
        [((8, cols), F32), (slim, BF16), (wide, BF16), (wide, BF16)] + travel,
        [meta, rng, segq, segk, lse, delta, q, do, k, v, low],
        [
            pltpu.VMEM((window, width), BF16),
            pltpu.VMEM(slim, BF16),
            pltpu.VMEM(wide, BF16),
            pltpu.VMEM(wide, BF16),
            pltpu.VMEM(wide, F32),
            pltpu.VMEM(wide, F32),
            pltpu.VMEM((cols // HEAD_DIM, HEAD_DIM, BLOCK), F32),
            pltpu.VMEM((3, width, cols), BF16),
            pltpu.SemaphoreType.DMA((4,)),
            pltpu.SemaphoreType.DMA((2, half)),
        ],
        "backward_attention",
        smem=2,
        anys=1,
        out_anys=5,
    )


def halo_grads_kernel(n_pieces, off, more, meta, rng, *refs):
    if more:
        left_in, right_in, *refs = refs
    ins, refs = refs[:2], refs[2:]
    shards, pieces, refs = refs[:3], refs[3 : 3 + n_pieces], refs[3 + n_pieces :]
    left, right, dk, dv, w, sem, sems = refs
    wait = load_weights(meta, shards, off, pieces, w, sem, 1)
    tokens = left.shape[0]
    before, after = used_chunks(rng)
    loads = [
        pltpu.make_async_copy(x.at[rows], to.at[rows], sems.at[i])
        for i, (x, to) in enumerate(zip(ins, (dk, dv)))
        for rows in (pl.ds(0, tokens), pl.ds(2 * tokens, tokens))
    ]
    for x in loads:
        x.start()
    for x in loads:
        x.wait()
    wait()

    def halo_grads(out, old, to, rows):
        res = dot_nt(dk[rows, :], w[0]) + dot_nt(dv[rows, :], w[1])
        if more:
            res = res + old[to, :].astype(F32)
        out[to, :] = res.astype(BF16)

    lows, highs = slice(0, tokens - FAR), slice(tokens - FAR, tokens)
    firsts, others = slice(0, FAR), slice(FAR, tokens)
    for out, old, used, far_to, near_to, base in (
        (left, left_in if more else None, before, lows, highs, 0),
        (right, right_in if more else None, after, others, firsts, 2 * tokens),
    ):
        halo_grads(out, old, near_to, slice(base + near_to.start, base + near_to.stop))

        @pl.when(used)
        def _():
            halo_grads(out, old, far_to, slice(base + far_to.start, base + far_to.stop))

        @pl.when(jnp.logical_not(used))
        def _():
            if more:
                out[far_to, :] = old[far_to, :]
            else:
                out[far_to, :] = jnp.zeros((tokens - FAR, out.shape[1]), BF16)


def halo_grads(group, meta, rng, old, dk, dv, shards, pieces):
    cols = dk.shape[1]
    width = shards[0].shape[0]
    per = pieces[0].shape[3]
    full = (dk.shape[0] // 3, width)
    return call(
        functools.partial(halo_grads_kernel, len(pieces), group * per, len(old) > 0),
        [(full, BF16), (full, BF16)],
        [meta, rng, *old, dk, dv, *shards, *pieces],
        [
            pltpu.VMEM(dk.shape, BF16),
            pltpu.VMEM(dv.shape, BF16),
            pltpu.VMEM((2, width, cols), BF16),
            pltpu.SemaphoreType.DMA,
            pltpu.SemaphoreType.DMA((2,)),
        ],
        "halo_grads",
        smem=2,
        anys=5 + len(pieces),
    )


def input_grads_kernel(n_pieces, off, count, meta, rng, *refs):
    ins, refs = refs[:8], refs[8:]
    shards, pieces, refs = refs[:3], refs[3 : 3 + n_pieces], refs[3 + n_pieces :]
    own, sums, dq, dk, dv, *refs = refs
    x_left, x_own, x_right, left, right, w, sem, sems = refs
    tokens = dq.shape[0]
    wait = load_weights(meta, shards, off, pieces, w, sem)
    middle = pl.ds(tokens, tokens)
    ins = (ins[0], ins[1].at[middle], ins[2].at[middle], *ins[3:])
    loads = [
        pltpu.make_async_copy(x, to, sems.at[i])
        for i, (x, to) in enumerate(zip(ins, (dq, dk, dv, x_left, x_own, x_right, left, right)))
    ]
    for x in loads:
        x.start()
    before, after = used_chunks(rng)
    wait()
    for x in loads:
        x.wait()
    own[...] = dot_nt(dk[...], w[1]) + dot_nt(dv[...], w[2]) + dot_nt(dq[...], w[0])
    sums[...] = jnp.zeros(sums.shape, F32)

    def tally(grad, x, lo, hi):
        @pl.loop(lo, hi)
        def _(i):
            rows = pl.ds(pl.multiple_of(i * ROWS, ROWS), ROWS)
            hat, _ = normalise(x[rows, :].astype(F32))
            g = grad[rows, :].astype(F32)
            sums[0:1, :] += jnp.sum(g * hat, axis=0, keepdims=True)
            sums[1:2, :] += jnp.sum(g, axis=0, keepdims=True)

    tally(own, x_own, 0, tokens // ROWS)
    if count:
        tally(left, x_left, jnp.where(before, 0, (tokens - FAR) // ROWS), tokens // ROWS)
        tally(right, x_right, 0, jnp.where(after, tokens, FAR) // ROWS)


def input_grads(group, meta, rng, dq, dk, dv, window, halos, count, shards, pieces):
    tokens, cols = dq.shape
    width = shards[0].shape[0]
    per = pieces[0].shape[3]
    full = (tokens, width)
    return call(
        functools.partial(input_grads_kernel, len(pieces), group * per, count),
        [(full, F32), ((8, width), F32)],
        [meta, rng, dq, dk, dv, *window, *halos, *shards, *pieces],
        [pltpu.VMEM(dq.shape, BF16)] * 3
        + [pltpu.VMEM(full, BF16)] * 5
        + [
            pltpu.VMEM((3, width, cols), BF16),
            pltpu.SemaphoreType.DMA,
            pltpu.SemaphoreType.DMA((8,)),
        ],
        "input_grads",
        smem=2,
        anys=11 + len(pieces),
    )


def last_kernel(inputs, g_resid, from_left, from_right, gain, *refs):
    *owns, g_inputs = refs

    @pl.loop(0, inputs.shape[0] // ROWS)
    def _(i):
        rows = pl.ds(pl.multiple_of(i * ROWS, ROWS), ROWS)
        hat, rstd = normalise(inputs[rows, :].astype(F32))
        g = from_left[rows, :].astype(F32) + from_right[rows, :].astype(F32)
        for own in owns:
            g = g + own[rows, :]
        g_inputs[rows, :] = (g_resid[rows, :] + norm_back(g, hat, rstd, gain[...])).astype(BF16)


def last_step(inputs, g_resid, from_left, from_right, gain, owns):
    return call(
        last_kernel,
        [(inputs.shape, BF16)],
        [inputs, g_resid, from_left, from_right, gain, *owns],
        [],
        "input_norm_grads",
    )


def lay_out_kernel(turned, groups, size, meta, *refs):
    outs = refs[-len(turned) :]
    pieces = refs[: -len(turned)]
    n = len(pieces) // groups
    s = meta[0]
    per = pieces[0].shape[-1]
    for g in range(groups):
        to = slice(g * per, (g + 1) * per)
        if n == 1:
            whole = [
                (pieces[g].at[i], slice(i * size, (i + 1) * size))
                for i in range(pieces[g].shape[0])
            ]
        else:
            whole = [
                (pieces[g * n + j], pl.ds(pl.multiple_of((s ^ j) * size, size), size))
                for j in range(n)
            ]
        for piece, at in whole:
            for m, turn in enumerate(turned):
                part = piece[m, :size].astype(F32)
                if turn:
                    outs[m][to, at] = jnp.transpose(part)
                else:
                    outs[m][at, to] = part


def lay_out(meta, width, groups, turned):
    first = groups[0]
    size = width // (len(first) if len(first) > 1 else first[0].shape[0])
    shapes = [(SHARD, width) if turn else (width, SHARD) for turn in turned]
    return call(
        functools.partial(lay_out_kernel, turned, len(groups), size),
        [(shape, F32) for shape in shapes],
        [meta, *[piece for group in groups for piece in group]],
        [],
        "lay_out_grads",
        smem=1,
    )


def pause_kernel(x, out):
    out[...] = x[...]


def pause(x):
    (out,) = call(pause_kernel, [(x.shape, x.dtype)], [x], [], "pause")
    return out


SHARD = 256


def make_body(n_seq, n_tp):
    inner = min(n_seq, 8)
    outer = n_seq // inner
    half = inner // 2
    masks = [2 * jj for jj in range(1, half)]

    def shift(x, by):
        pairs = [(i, i + by) for i in range(n_tp) if 0 <= i + by < n_tp]
        return lax.ppermute(x, "tp", pairs)

    def swap(x, mask):
        return lax.ppermute(x, "seq", [(i, i ^ mask) for i in range(n_seq)])

    def tie(*xs):
        return lax.optimization_barrier(xs)

    def block_of(shards, biases, off, per, s):
        size = shards[0].shape[0] // inner
        cut = jnp.stack([lax.dynamic_slice(w, (s * size, off), (size, per)) for w in shards])
        if biases:
            parts = []
            rest = jnp.stack([b[off : off + per] for b in biases])
            for _ in range(3):
                part = rest.astype(BF16)
                rest = rest - part.astype(F32)
                parts.append(part)
            parts = jnp.stack(parts + [jnp.zeros_like(parts[0])] * 13, axis=1)
            cut = jnp.concatenate([cut, parts], axis=1)
        return jnp.broadcast_to(cut[None], (n_tp, *cut.shape))

    def over_tp(block):
        return lax.all_to_all(block, "tp", 0, 0, tiled=True)

    def others_of(got, size, t):
        return jnp.stack(
            [lax.dynamic_index_in_dim(got, lax.rem(t + r + 1, n_tp), 0, keepdims=False)[:, :size]
             for r in range(n_tp - 1)]
        )

    def biases_of(got, size):
        whole = jnp.sum(got[:, :, size : size + 3].astype(F32), axis=2)
        return [whole[:, m].reshape(1, -1) for m in range(whole.shape[1])]

    def from_chips(x):
        return [x] + [swap(x, mask) for mask in masks]

    def from_cores(even):
        odd = [swap(e, 1) for e in even]
        return [e for pair in zip(even, odd) for e in pair]

    def core_sums(keep, got):
        return [(k.astype(F32) + g.astype(F32)).astype(BF16) for k, g in zip(keep, got)]

    def over_chips(sums):
        return [swap(x, 2 * jj + 2) for jj, x in enumerate(sums)]

    def chip_sum(moved):
        total = moved[0].astype(F32)
        for x in moved[1:]:
            total = total + x.astype(F32)
        total = total.astype(BF16)
        if outer > 1:
            groups = [[i + inner * o for o in range(outer)] for i in range(inner)]
            total = lax.psum(total, "seq", axis_index_groups=groups)
        return total

    def own_shard(total):
        got = lax.all_to_all(total, "tp", 0, 0, tiled=True)
        return jnp.sum(got.astype(F32), axis=0).astype(BF16)

    def body(
        inputs, segment_ids, row_lengths, norm1_gain, norm1_shift, w_query, w_key, w_value,
        b_query, b_value, w_out, b_out, norm2_gain, norm2_shift, w_up, b_up, w_down, b_down,
        out_grad,
    ):
        tokens, width = inputs.shape
        halo = tokens
        t = lax.axis_index("tp")
        s = lax.rem(lax.axis_index("seq"), inner)
        meta = jnp.stack([s, t]).astype(jnp.int32)
        per = SHARD // GROUPS
        every = range(GROUPS)
        zero = jnp.zeros_like(b_query)

        def row(x):
            return x.reshape(1, -1)

        def by_shard(groups):
            cols = [x.reshape(n_tp, per) for x in groups]
            return jnp.concatenate(cols, axis=1).reshape(1, width)

        attn_w = [w_query, w_key, w_value]
        attn_b = [b_query, b_up, b_value]
        size = width // inner
        feed_w = [w_out.T, w_up, w_down.T]
        feed_block = block_of(feed_w, [], 0, SHARD, s)
        attn_p, attn_whole = [], []
        for g in every:
            got = over_tp(block_of(attn_w, attn_b, g * per, per, s))
            got, feed_block = tie(got, feed_block)
            even = from_chips(others_of(got, size, t))
            even[0], even[-1] = tie(even[0], even[-1])
            attn_p.append(from_cores(even))
            attn_whole.append(biases_of(got, size))
        got = over_tp(feed_block)
        inputs_later, got = tie(inputs, got)
        feed_p = from_chips(others_of(got, size, t))
        left = shift(inputs_later, 1)
        right = shift(inputs_later, -1)

        position = jnp.arange(ROW_LEN, dtype=jnp.int32)
        numbers = jnp.where(position < row_lengths[0], segment_ids[0], 4096 + position)
        numbers = jnp.concatenate(
            [jnp.full((halo,), -1, jnp.int32), numbers, jnp.full((halo,), 1 << 20, jnp.int32)]
        )
        seg_win = lax.dynamic_slice_in_dim(numbers, t * tokens, tokens + 2 * halo, 0)
        seg_mine = seg_win[halo : halo + tokens]
        first = seg_mine[::BLOCK]
        last = seg_mine[BLOCK - 1 :: BLOCK]
        low = jnp.sum((seg_win[None, :] < first[:, None]).astype(jnp.int32), axis=1)
        high = jnp.sum((seg_win[None, :] <= last[:, None]).astype(jnp.int32), axis=1)
        rng = jnp.stack([low // BLOCK, (high + BLOCK - 1) // BLOCK])
        segq, segk = seg_mine[None, :], seg_win[:, None]

        gain1, feed_w[0], feed_w[2] = tie(norm1_gain, feed_w[0], feed_w[2])
        source = (row(gain1), row(norm1_shift), left, inputs, right)
        saved = []
        for g in every:
            bq, _, bv = attn_whole[g]
            res = forward(g, meta, rng, segq, segk, source, bq, bv, attn_w, attn_p[g])
            mixed, lse, q, k, v = res[:5]
            if g == 0:
                source = first_low = res[5]
                mixed, *feed_p = tie(mixed, *feed_p)
                feed_p = from_cores(feed_p)
            saved.append((mixed, lse, q, k, v))
        bup = by_shard([x[1] for x in attn_whole])
        res = feed_forward(
            meta, inner, inputs, out_grad, row(b_out), row(norm2_gain), row(norm2_shift), bup,
            row(b_down), [x[0] for x in saved], feed_w, feed_p,
        )
        g_mixed, delta = list(res[:GROUPS]), res[GROUPS : 2 * GROUPS]
        sums_feed, output, g_resid, *travel = res[2 * GROUPS :]

        feed_got = [swap(x, 1) for x in travel[half:]]
        feed_own = (travel[0], feed_got[0])
        feed_moved = over_chips(core_sums(travel[1:half], feed_got[1:]))
        old, owns, sums_qkv, totals = (), [], [], []
        for g in every:
            _, lse, q, k, v = saved[g]
            vec, dq, dk, dv, keep, send = backward(
                meta, rng, segq, segk, lse, delta[g], q, g_mixed[g], k, v, first_low, inner
            )
            sums_qkv.append(vec)
            got = swap(send, 1)
            if g == 0:
                feed_moved, sums_feed = tie(feed_moved, sums_feed)
                got, sums_feed = tie(got, pause(sums_feed))
                feed_total = chip_sum([*feed_own, *feed_moved])
            sums = core_sums(keep[1:], got[1:])
            dk, sums = tie(dk, sums)
            moved = over_chips(sums)
            if g + 1 < GROUPS:
                g_mixed[g + 1], moved = tie(g_mixed[g + 1], moved)
            old = halo_grads(g, meta, rng, old, dk, dv, attn_w, attn_p[g])
            own, sums_in = input_grads(
                g, meta, rng, dq, dk, dv, (left, inputs, right), old, g + 1 == GROUPS,
                attn_w, attn_p[g],
            )
            owns.append(own)
            if g + 1 == GROUPS:
                feed_g = feed_total.reshape(-1, SHARD)
                feed_g = lax.psum_scatter(feed_g, "tp", scatter_dimension=0, tiled=True)
                moved, sums_in, feed_g = tie(moved, sums_in, feed_g)
            totals.append(chip_sum([keep[0], got[0], *moved]))
        from_right = shift(old[0], -1)
        from_left = shift(old[1], 1)
        piece = feed_total.shape[1:]
        feed_g = lax.all_gather(feed_g.reshape(piece), "seq", axis=0)[:inner]
        (g_inputs,) = last_step(
            inputs, g_resid, from_left, from_right, row(norm1_gain), owns
        )

        vectors = [by_shard([x[i] for x in sums_qkv]) for i in range(2)]
        vectors = jnp.concatenate([sums_in[:2], *vectors, sums_feed[:5]])
        if outer > 1:
            groups = [[i + inner * o for o in range(outer)] for i in range(inner)]
            vectors = lax.psum(vectors, "seq", axis_index_groups=groups)
        extra = -(-vectors.size // (48 * per)) * 16
        n_vec = vectors.size
        vectors = jnp.pad(vectors.astype(BF16).reshape(-1), (0, 3 * extra * per - n_vec))
        vectors = jnp.broadcast_to(vectors.reshape(1, 3, extra, per), (n_tp, 3, extra, per))
        totals[-1] = jnp.concatenate([totals[-1], vectors], axis=2)
        shards = [own_shard(x) for x in totals]
        shards[-1], g_inputs = tie(shards[-1], g_inputs)
        g_wo, g_wup, g_wdn = lay_out(meta, width, [[feed_g]], (True, False, True))
        evens = [from_chips(x) for x in shards]
        evens[-1][-1], g_wup = tie(evens[-1][-1], g_wup)
        pieces = [from_cores(x) for x in evens]
        vectors = sum([x[:, size:].astype(F32) for x in pieces[-1]])
        vectors = vectors.reshape(-1)[:n_vec].reshape(-1, width)
        n1g, n1s, g_bq, g_bv, g_bo, n2g, n2s, g_bup, g_bdn = [vectors[i] for i in range(9)]

        g_wq, g_wk, g_wv = lay_out(meta, width, pieces, (False, False, False))

        def shard(x):
            return lax.dynamic_slice_in_dim(x, t * SHARD, SHARD, 0)

        return (
            output, g_inputs, n1g, n1s, g_wq, g_wk, g_wv, shard(g_bq), shard(g_bv),
            g_wo, g_bo, n2g, n2s, g_wup, shard(g_bup), g_wdn, g_bdn,
        )

    return body


def solution(mesh):
    tok = P(("seq", "tp"), None)
    col, row, vec, rep = P(None, "tp"), P("tp", None), P("tp"), P()
    in_specs = (
        tok, P("seq", None), P("seq"), rep, rep, col, col, col, vec, vec,
        row, rep, rep, rep, col, vec, row, rep, tok,
    )
    out_specs = (
        tok, tok, rep, rep, col, col, col, vec, vec,
        row, rep, rep, rep, col, vec, row, rep,
    )
    body = make_body(mesh.shape["seq"], mesh.shape["tp"])
    return jax.shard_map(body, mesh=mesh, in_specs=in_specs, out_specs=out_specs, check_vma=False)
```

```python
import functools
import math

import jax
import jax.numpy as jnp
from jax import lax
from jax.experimental import pallas as pl
from jax.experimental.pallas import tpu as pltpu
from jax.sharding import PartitionSpec as P

HEAD_DIM = 128
ROW_LEN = 2048
NORM_EPS = 1e-05
MASKED = -1000000000.0
LOG2E = 1.4426950408889634
TILE = 256
BLOCK = 256
FAR = 256
ROWS = 128
GROUPS = 1
F32 = jnp.float32
BF16 = jnp.bfloat16
MIB = 1024 * 1024


def dot_nn(a, b):
    return lax.dot_general(a, b, (((1,), (0,)), ((), ())), preferred_element_type=F32)


def dot_nt(a, b):
    return lax.dot_general(a, b, (((1,), (1,)), ((), ())), preferred_element_type=F32)


def dot_tn(a, b):
    return lax.dot_general(a, b, (((0,), (0,)), ((), ())), preferred_element_type=F32)


def normalise(x):
    centre = x - jnp.mean(x, axis=-1, keepdims=True)
    rstd = lax.rsqrt(jnp.mean(centre * centre, axis=-1, keepdims=True) + NORM_EPS)
    return centre * rstd, rstd


def norm_back(grad, hat, rstd, gain):
    t = gain * grad
    mean_t = jnp.mean(t, axis=-1, keepdims=True)
    mean_th = jnp.mean(t * hat, axis=-1, keepdims=True)
    return (t - mean_t - hat * mean_th) * rstd


def call(kernel, outs, ins, scratch, name, smem=0, anys=0, out_anys=0, gflop=50, mib=50):
    spaces = [pltpu.SMEM] * smem + [pltpu.VMEM] * (len(ins) - smem - anys) + [pl.ANY] * anys
    out_spaces = [pltpu.VMEM] * (len(outs) - out_anys) + [pl.ANY] * out_anys
    return pl.pallas_call(
        kernel,
        out_shape=tuple(jax.ShapeDtypeStruct(*o) for o in outs),
        in_specs=[pl.BlockSpec(memory_space=m) for m in spaces],
        out_specs=tuple(pl.BlockSpec(memory_space=m) for m in out_spaces),
        scratch_shapes=scratch,
        compiler_params=pltpu.CompilerParams(vmem_limit_bytes=mib * MIB),
        cost_estimate=pl.CostEstimate(
            flops=gflop * 10**9, bytes_accessed=1000000, transcendentals=0
        ),
        name=name,
    )(*ins)


def load_weights(meta, shards, off, pieces, dst, sem, skipped=0):
    s, t = meta[0], meta[1]
    _, size, per = pieces[0].shape[1:]
    last = skipped + dst.shape[0]
    n_tp = dst.shape[2] // per
    mine = pl.ds(pl.multiple_of(t * per, per), per)
    for m in range(dst.shape[0]):
        source = shards[skipped + m].at[:, off : off + per]
        pltpu.make_async_copy(source, dst.at[m, :, mine], sem).start()
    for j, piece in enumerate(pieces):
        at = pl.ds(pl.multiple_of((s ^ j) * size, size), size)
        for r in range(n_tp - 1):
            u = pl.multiple_of(lax.rem(t + r + 1, n_tp) * per, per)
            source = piece.at[r, skipped:last]
            pltpu.make_async_copy(source, dst.at[:, at, pl.ds(u, per)], sem).start()
    return pltpu.make_async_copy(dst, dst, sem).wait


def store_grads(meta, grads, keep, send, sems, first, last):
    s = meta[0]
    n_tp, _, size, per = keep[0].shape
    for parity, dst in enumerate((keep, send)):
        for jj, piece in enumerate(dst):
            p = pl.ds(pl.multiple_of((s ^ (2 * jj + parity)) * size, size), size)
            for t in range(n_tp):
                pltpu.make_async_copy(
                    grads.at[first:last, p, t * per : (t + 1) * per],
                    piece.at[t, first:last],
                    sems.at[parity, jj],
                ).start()


def grads_stored(keep, send, sems):
    for parity, dst in enumerate((keep, send)):
        for jj, piece in enumerate(dst):
            pltpu.make_async_copy(piece, piece, sems.at[parity, jj]).wait()


def travelling(inner, width, per):
    half = max(inner // 2, 1)
    return half, (width // SHARD, 3, width // inner, per)


def attend(rng, segq, segk, q, k, v, mixed, lse, s_scr, m_scr, l_scr, acc):
    heads = q.shape[1] // HEAD_DIM
    coef = HEAD_DIM**-0.5 * LOG2E
    of = [slice(h * HEAD_DIM, (h + 1) * HEAD_DIM) for h in range(heads)]

    def fold(x, op):
        x = x.reshape(BLOCK // 8, 8, BLOCK)
        res = x[0]
        for i in range(1, BLOCK // 8):
            res = op(res, x[i])
        return res

    @pl.loop(0, q.shape[0] // BLOCK)
    def _(qb):
        rows = pl.ds(pl.multiple_of(qb * BLOCK, BLOCK), BLOCK)
        lo = rng[0, qb]
        hi = rng[1, qb]
        sq = segq[:, rows]
        m_scr[...] = jnp.full(m_scr.shape, -3e38, F32)
        l_scr[...] = jnp.zeros(l_scr.shape, F32)
        acc[...] = jnp.zeros(acc.shape, F32)

        @pl.loop(lo, hi)
        def _(kc):
            ks = pl.ds(pl.multiple_of(kc * BLOCK, BLOCK), BLOCK)
            bias = jnp.where(segk[ks, :] == sq, 0.0, MASKED)
            for h in range(0, heads, 2):
                pair = (h, h + 1)
                scores = [dot_nt(k[ks, of[i]], q[rows, of[i]]) * coef + bias for i in pair]
                for i, s in zip(pair, scores):
                    s_scr[kc, i] = s
                    m_scr[i] = jnp.maximum(m_scr[i], fold(s, jnp.maximum))

        for h in range(heads):
            m_scr[h] = jnp.broadcast_to(jnp.max(m_scr[h], axis=0, keepdims=True), (8, BLOCK))

        @pl.loop(lo, hi)
        def _(kc):
            ks = pl.ds(pl.multiple_of(kc * BLOCK, BLOCK), BLOCK)
            for h in range(0, heads, 2):
                pair = (h, h + 1)
                probs = [jnp.exp2(s_scr[kc, i] - m_scr[i, :1]) for i in pair]
                outs = [dot_tn(v[ks, of[i]], p.astype(BF16)) for i, p in zip(pair, probs)]
                for i, p, o in zip(pair, probs, outs):
                    l_scr[i] += fold(p, jnp.add)
                    acc[i] += o

        for h in range(heads):
            total = jnp.sum(l_scr[h], axis=0, keepdims=True)
            mixed[rows, of[h]] = jnp.transpose(acc[h] / total).astype(BF16)
            lse[h : h + 1, rows] = m_scr[h, :1] + jnp.log2(total)


def attend_back(rng, segq, segk, lse, delta, q, do, k, v, dq, dk_acc, dv_acc, dq_acc):
    heads = q.shape[1] // HEAD_DIM
    scale = HEAD_DIM**-0.5
    coef = scale * LOG2E
    of = [slice(h * HEAD_DIM, (h + 1) * HEAD_DIM) for h in range(heads)]

    @pl.loop(0, q.shape[0] // BLOCK)
    def _(qb):
        rows = pl.ds(pl.multiple_of(qb * BLOCK, BLOCK), BLOCK)
        lo = rng[0, qb]
        hi = rng[1, qb]
        sq = segq[:, rows]
        dq_acc[...] = jnp.zeros(dq_acc.shape, F32)

        @pl.loop(lo, hi)
        def _(kc):
            ks = pl.ds(pl.multiple_of(kc * BLOCK, BLOCK), BLOCK)
            bias = jnp.where(segk[ks, :] == sq, 0.0, MASKED)

            def probs(h):
                s = dot_nt(k[ks, of[h]], q[rows, of[h]]) * coef
                p = jnp.exp2(s + (bias - lse[h : h + 1, rows]))
                return p, dot_nt(v[ks, of[h]], do[rows, of[h]])

            def products(h, p, dp):
                ds = (p * (dp - delta[h : h + 1, rows])).astype(BF16)
                return (
                    dot_nn(p.astype(BF16), do[rows, of[h]]),
                    dot_nn(ds, q[rows, of[h]]),
                    dot_tn(k[ks, of[h]], ds),
                )

            for h in range(0, heads, 2):
                pair = (h, h + 1)
                both = [probs(i) for i in pair]
                terms = [products(i, *b) for i, b in zip(pair, both)]
                for i, (a, b, c) in zip(pair, terms):
                    dv_acc[ks, of[i]] += a
                    dk_acc[ks, of[i]] += b
                    dq_acc[i] += c

        for h in range(heads):
            dq[rows, of[h]] = (jnp.transpose(dq_acc[h]) * scale).astype(BF16)


def used_chunks(rng):
    tokens = BLOCK * rng.shape[1]
    before = rng[0, 0] * BLOCK < tokens - FAR
    after = rng[1, rng.shape[1] - 1] * BLOCK > 2 * tokens + FAR
    return before, after


def forward_kernel(first, n_pieces, off, meta, rng, segq, segk, *refs):
    if first:
        gain, shift, bq, bv, left, own, right, *refs = refs
    else:
        bq, bv, low_in, *refs = refs
    shards, pieces, refs = refs[:3], refs[3 : 3 + n_pieces], refs[3 + n_pieces :]
    mixed, lse, q_out, k_out, v_out, *refs = refs
    if first:
        low_out, *refs = refs
    q, k, v, low, w, s_scr, m_scr, l_scr, acc, sem, out_sems, *refs = refs
    tokens = q.shape[0]
    before, after = used_chunks(rng)
    lo = jnp.where(before, 0, (tokens - FAR) // BLOCK)
    hi = jnp.where(after, 3 * tokens, 2 * tokens + FAR) // BLOCK

    def copy(i, src, dst):
        return pltpu.make_async_copy(src, dst, out_sems.at[i])

    def chunk(c):
        return pl.ds(pl.multiple_of(c * BLOCK, BLOCK), BLOCK)

    if first:
        (window,) = refs
        ins = [
            copy(i, x, window.at[i * tokens : (i + 1) * tokens])
            for i, x in enumerate((left, own, right))
        ]
    else:
        ins = [copy(3, low_in, low)]
    for x in ins:
        x.start()
    wait = load_weights(meta, shards, off, pieces, w, sem)
    for x in ins:
        x.wait()
    outs = [(q, q_out), (k, k_out), (v, v_out)]
    if first:

        @pl.loop(lo, hi)
        def _(c):
            hat, _ = normalise(window[chunk(c), :].astype(F32))
            low[chunk(c), :] = (hat * gain[...] + shift[...]).astype(BF16)

        outs.append((low, low_out))
        copy(3, *outs[3]).start()
    wait()
    q[...] = (dot_nn(low[tokens : 2 * tokens, :], w[0]) + bq[...]).astype(BF16)
    copy(0, *outs[0]).start()
    def project(rows):
        k[rows, :] = dot_nn(low[rows, :], w[1]).astype(BF16)
        v[rows, :] = (dot_nn(low[rows, :], w[2]) + bv[...]).astype(BF16)

    start, stop = tokens - FAR, 2 * tokens + FAR
    project(slice(start, stop))
    pl.when(before)(lambda: project(slice(0, start)))
    pl.when(after)(lambda: project(slice(stop, 3 * tokens)))

    copy(1, *outs[1]).start()
    copy(2, *outs[2]).start()
    attend(rng, segq, segk, q, k, v, mixed, lse, s_scr, m_scr, l_scr, acc)
    for i, x in enumerate(outs):
        copy(i, *x).wait()


def forward(group, meta, rng, segq, segk, source, bq, bv, shards, pieces):
    first = group == 0
    width = shards[0].shape[0]
    window = segk.shape[0]
    tokens = window // 3
    per = pieces[0].shape[3]
    cols = bq.shape[1]
    heads = cols // HEAD_DIM
    slim, wide = (tokens, cols), (window, cols)
    kept = ((window, width), BF16)
    ins = [meta, rng, segq, segk]
    ins += [*source[:2], bq, bv, *source[2:]] if first else [bq, bv, source]
    return call(
        functools.partial(forward_kernel, first, len(pieces), group * per),
        [(slim, BF16), ((heads, tokens), F32), (slim, BF16), (wide, BF16), (wide, BF16)]
        + [kept] * first,
        [*ins, *shards, *pieces],
        [
            pltpu.VMEM(slim, BF16),
            pltpu.VMEM(wide, BF16),
            pltpu.VMEM(wide, BF16),
            pltpu.VMEM(*kept),
            pltpu.VMEM((3, width, cols), BF16),
            pltpu.VMEM((window // BLOCK, heads, BLOCK, BLOCK), F32),
            pltpu.VMEM((heads, 8, BLOCK), F32),
            pltpu.VMEM((heads, 8, BLOCK), F32),
            pltpu.VMEM((heads, HEAD_DIM, BLOCK), F32),
            pltpu.SemaphoreType.DMA,
            pltpu.SemaphoreType.DMA((4,)),
        ]
        + [pltpu.VMEM(*kept)] * first,
        "forward_attention",
        mib=46,
        smem=2,
        anys=3 + len(pieces) + (3 if first else 1),
        out_anys=3 + first,
    )


def feed_kernel(n_pieces, half, groups, meta, inputs, dout, bo, gain, shift, bup, bdn, *refs):
    parts, refs = refs[:groups], refs[groups:]
    shards, pieces, refs = refs[:3], refs[3 : 3 + n_pieces], refs[3 + n_pieces :]
    g_parts, refs = refs[:groups], refs[groups:]
    deltas, refs = refs[:groups], refs[groups:]
    sums, output_out, g_resid_out, *refs = refs
    keep, send, refs = refs[:half], refs[half : 2 * half], refs[2 * half :]
    w, mixed, resid, hat, rstd, second, hidden, g_up, g_sec, low, output, grads, *sems = refs
    first_sem, sem, grad_sems, out_sems = sems
    wo_t, wup, wdn_t = w.at[0], w.at[1], w.at[2]
    wait_first = load_weights(meta, shards, 0, pieces, w.at[:1], first_sem)
    wait = load_weights(meta, shards, 0, pieces, w.at[1:], sem, 1)
    tokens, width = inputs.shape
    per = SHARD // groups
    for g in range(groups):
        for t in range(width // SHARD):
            at = t * SHARD + g * per
            mixed[:, at : at + per] = parts[g][:, t * per : (t + 1) * per]
    sums[...] = jnp.zeros(sums.shape, F32)
    sums[4:5, :] = jnp.sum(dout[...].astype(F32), axis=0, keepdims=True)
    wait_first()
    resid[...] = inputs[...].astype(F32) + dot_nt(mixed[...], wo_t[...]) + bo[...]

    @pl.loop(0, tokens // BLOCK)
    def _(i):
        rows = pl.ds(pl.multiple_of(i * BLOCK, BLOCK), BLOCK)
        h, r = normalise(resid[rows, :])
        hat[rows, :] = h
        rstd[rows, :] = jnp.broadcast_to(r, (BLOCK, 128))
        second[rows, :] = (h * gain[...] + shift[...]).astype(BF16)

    wait()
    for n in range(width // TILE):
        cols = slice(n * TILE, (n + 1) * TILE)
        up = dot_nn(second[...], wup[:, cols]) + bup[:, cols]
        d_hidden = dot_nn(dout[...], wdn_t[:, cols])
        phi = 0.5 + 0.5 * lax.erf(up * (0.5**0.5))
        hidden[:, cols] = (up * phi).astype(BF16)
        slope = phi + up * (jnp.exp(-0.5 * up * up) * (0.5 / math.pi) ** 0.5)
        grad = (d_hidden * slope).astype(BF16)
        g_up[:, cols] = grad
        sums[3:4, cols] = jnp.sum(grad.astype(F32), axis=0, keepdims=True)
    g_sec[...] = dot_nt(g_up[...], wup[...])
    output[...] = (resid[...] + dot_nt(hidden[...], wdn_t[...]) + bdn[...]).astype(BF16)
    out_copy = pltpu.make_async_copy(output, output_out, out_sems.at[0])
    out_copy.start()
    grads[2] = dot_tn(dout[...], hidden[...]).astype(BF16)
    grads[1] = dot_tn(second[...], g_up[...]).astype(BF16)
    store_grads(meta, grads, keep, send, grad_sems, 1, 3)

    @pl.loop(0, tokens // ROWS)
    def _(i):
        rows = pl.ds(pl.multiple_of(i * ROWS, ROWS), ROWS)
        h, g = hat[rows, :], g_sec[rows, :]
        res = dout[rows, :].astype(F32) + norm_back(g, h, rstd[rows, :1], gain[...])
        resid[rows, :] = res
        low[rows, :] = res.astype(BF16)
        for n, x in enumerate((res, g * h, g)):
            sums[n : n + 1, :] += jnp.sum(x, axis=0, keepdims=True)

    resid_copy = pltpu.make_async_copy(resid, g_resid_out, out_sems.at[1])
    resid_copy.start()
    grads[0] = dot_tn(low[...], mixed[...]).astype(BF16)
    store_grads(meta, grads, keep, send, grad_sems, 0, 1)
    grad = dot_nn(low[...], wo_t[...]).astype(BF16)
    prod = grad.astype(F32) * mixed[...].astype(F32)
    high = prod.astype(BF16)
    rest_of = (prod - high.astype(F32)).astype(BF16)
    head_of = lax.broadcasted_iota(jnp.int32, (width, 128), 0) // HEAD_DIM
    member = jnp.where(head_of == lax.broadcasted_iota(jnp.int32, (width, 128), 1), 1.0, 0.0)
    member = member.astype(BF16)
    totals = dot_nn(high, member) + dot_nn(rest_of, member)
    for i in range(0, tokens, 128):
        turned = jnp.transpose(totals[i : i + 128])
        for n in range(width // HEAD_DIM):
            at = n * HEAD_DIM
            t, g, inside = at // SHARD, at % SHARD // per, at % per
            h = (t * per + inside) // HEAD_DIM
            deltas[g][h : h + 1, i : i + 128] = turned[n : n + 1]
    for g in range(groups):
        for t in range(width // SHARD):
            at = t * SHARD + g * per
            g_parts[g][:, t * per : (t + 1) * per] = grad[:, at : at + per]
    out_copy.wait()
    resid_copy.wait()
    grads_stored(keep, send, grad_sems)


def feed_forward(
    meta, inner, inputs, dout, bo, gain, shift, bup, bdn, parts, shards, pieces
):
    tokens, width = inputs.shape
    groups = len(parts)
    half, piece = travelling(inner, width, SHARD)
    travel = [(piece, BF16)] * (2 * half)
    wide = pltpu.VMEM((tokens, width), F32)
    slim = pltpu.VMEM((tokens, width), BF16)
    return call(
        functools.partial(feed_kernel, len(pieces), half, groups),
        [(parts[0].shape, BF16)] * groups
        + [((width // HEAD_DIM // groups, tokens), F32)] * groups
        + [((8, width), F32), ((tokens, width), BF16), ((tokens, width), F32)]
        + travel,
        [meta, inputs, dout, bo, gain, shift, bup, bdn, *parts, *shards, *pieces],
        [
            pltpu.VMEM((3, width, width), BF16),
            slim,
            wide,
            wide,
            pltpu.VMEM((tokens, 128), F32),
            slim,
            slim,
            slim,
            wide,
            slim,
            slim,
            pltpu.VMEM((3, width, width), BF16),
            pltpu.SemaphoreType.DMA,
            pltpu.SemaphoreType.DMA,
            pltpu.SemaphoreType.DMA((2, half)),
            pltpu.SemaphoreType.DMA((2,)),
        ],
        "feed_forward",
        mib=48,
        smem=1,
        anys=3 + len(pieces),
        out_anys=2 + 2 * half,
    )


def backward_kernel(half, meta, rng, segq, segk, lse, delta, q, do, k, v, low_in, *refs):
    sums, dq_out, dk_out, dv_out, keep, send, *refs = refs
    keep, send = [[x.at[jj] for jj in range(half)] for x in (keep, send)]
    low, dq, dk, dv, dk_acc, dv_acc, dq_acc, grads, sems, grad_sems = refs
    low_copy = pltpu.make_async_copy(low_in, low, sems.at[3])
    low_copy.start()
    tokens, width = q.shape
    start, stop = tokens - FAR, 2 * tokens + FAR
    near, middle = slice(start, stop), slice(tokens, 2 * tokens)
    before, after = used_chunks(rng)
    scale = HEAD_DIM**-0.5

    def zero(rows):
        dk_acc[rows, :] = jnp.zeros((rows.stop - rows.start, width), F32)
        dv_acc[rows, :] = jnp.zeros((rows.stop - rows.start, width), F32)

    def narrow(rows):
        dk[rows, :] = (dk_acc[rows, :] * scale).astype(BF16)
        dv[rows, :] = dv_acc[rows, :].astype(BF16)

    def ends(act):
        pl.when(before)(lambda: act(slice(0, start)))
        pl.when(after)(lambda: act(slice(stop, 3 * tokens)))

    zero(near)
    ends(zero)
    attend_back(rng, segq, segk, lse, delta, q, do, k, v, dq, dk_acc, dv_acc, dq_acc)
    narrow(near)
    ends(narrow)
    outs = [
        pltpu.make_async_copy(x, out, sems.at[i])
        for i, (x, out) in enumerate(((dq, dq_out), (dk, dk_out), (dv, dv_out)))
    ]
    for x in outs:
        x.start()

    low_copy.wait()
    grads[0] = dot_tn(low[middle, :], dq[...]).astype(BF16)
    grads[1] = dot_tn(low[near, :], dk[near, :]).astype(BF16)
    grads[2] = dot_tn(low[near, :], dv[near, :]).astype(BF16)
    sums[...] = jnp.zeros(sums.shape, F32)
    sums[0:1, :] = jnp.sum(dq[...].astype(F32), axis=0, keepdims=True)
    sums[1:2, :] = jnp.sum(dv[near, :].astype(F32), axis=0, keepdims=True)
    for i, used in enumerate((before, after)):

        @pl.when(used)
        def _():
            rows = slice(i * stop, i * stop + start)
            sums[1:2, :] += jnp.sum(dv[rows, :].astype(F32), axis=0, keepdims=True)
            for m, x in ((1, dk), (2, dv)):
                more = dot_tn(low[rows, :], x[rows, :])
                grads[m] = (grads[m].astype(F32) + more).astype(BF16)

    store_grads(meta, grads, keep, send, grad_sems, 0, 3)
    for x in outs:
        x.wait()
    grads_stored(keep, send, grad_sems)


def backward(meta, rng, segq, segk, lse, delta, q, do, k, v, low, inner):
    tokens, cols = q.shape
    width = low.shape[1]
    window = 3 * tokens
    per = cols // (width // SHARD)
    half, piece = travelling(inner, width, per)
    travel = [((half, *piece), BF16)] * 2
    slim, wide = (tokens, cols), (window, cols)
    return call(
        functools.partial(backward_kernel, half),
        [((8, cols), F32), (slim, BF16), (wide, BF16), (wide, BF16)] + travel,
        [meta, rng, segq, segk, lse, delta, q, do, k, v, low],
        [
            pltpu.VMEM((window, width), BF16),
            pltpu.VMEM(slim, BF16),
            pltpu.VMEM(wide, BF16),
            pltpu.VMEM(wide, BF16),
            pltpu.VMEM(wide, F32),
            pltpu.VMEM(wide, F32),
            pltpu.VMEM((cols // HEAD_DIM, HEAD_DIM, BLOCK), F32),
            pltpu.VMEM((3, width, cols), BF16),
            pltpu.SemaphoreType.DMA((4,)),
            pltpu.SemaphoreType.DMA((2, half)),
        ],
        "backward_attention",
        mib=50,
        smem=2,
        anys=1,
        out_anys=5,
    )


def halo_grads_kernel(n_pieces, off, more, meta, rng, *refs):
    if more:
        left_in, right_in, *refs = refs
    ins, refs = refs[:2], refs[2:]
    shards, pieces, refs = refs[:3], refs[3 : 3 + n_pieces], refs[3 + n_pieces :]
    left, right, dk, dv, w, sem, sems = refs
    wait = load_weights(meta, shards, off, pieces, w, sem, 1)
    tokens = left.shape[0]
    before, after = used_chunks(rng)
    loads = [
        pltpu.make_async_copy(x.at[rows], to.at[rows], sems.at[i])
        for i, (x, to) in enumerate(zip(ins, (dk, dv)))
        for rows in (pl.ds(0, tokens), pl.ds(2 * tokens, tokens))
    ]
    for x in loads:
        x.start()
    for x in loads:
        x.wait()
    wait()

    def halo_grads(out, old, to, rows):
        res = dot_nt(dk[rows, :], w[0]) + dot_nt(dv[rows, :], w[1])
        if more:
            res = res + old[to, :].astype(F32)
        out[to, :] = res.astype(BF16)

    lows, highs = slice(0, tokens - FAR), slice(tokens - FAR, tokens)
    firsts, others = slice(0, FAR), slice(FAR, tokens)
    for out, old, used, far_to, near_to, base in (
        (left, left_in if more else None, before, lows, highs, 0),
        (right, right_in if more else None, after, others, firsts, 2 * tokens),
    ):
        halo_grads(out, old, near_to, slice(base + near_to.start, base + near_to.stop))

        @pl.when(used)
        def _():
            halo_grads(out, old, far_to, slice(base + far_to.start, base + far_to.stop))

        @pl.when(jnp.logical_not(used))
        def _():
            if more:
                out[far_to, :] = old[far_to, :]
            else:
                out[far_to, :] = jnp.zeros((tokens - FAR, out.shape[1]), BF16)


def halo_grads(group, meta, rng, old, dk, dv, shards, pieces):
    cols = dk.shape[1]
    width = shards[0].shape[0]
    per = pieces[0].shape[3]
    full = (dk.shape[0] // 3, width)
    return call(
        functools.partial(halo_grads_kernel, len(pieces), group * per, len(old) > 0),
        [(full, BF16), (full, BF16)],
        [meta, rng, *old, dk, dv, *shards, *pieces],
        [
            pltpu.VMEM(dk.shape, BF16),
            pltpu.VMEM(dv.shape, BF16),
            pltpu.VMEM((2, width, cols), BF16),
            pltpu.SemaphoreType.DMA,
            pltpu.SemaphoreType.DMA((2,)),
        ],
        "halo_grads",
        mib=24,
        smem=2,
        anys=5 + len(pieces),
    )


def input_grads_kernel(n_pieces, off, count, meta, rng, *refs):
    ins, refs = refs[:8], refs[8:]
    shards, pieces, refs = refs[:3], refs[3 : 3 + n_pieces], refs[3 + n_pieces :]
    own, sums, dq, dk, dv, *refs = refs
    x_left, x_own, x_right, left, right, w, sem, sems = refs
    tokens = dq.shape[0]
    wait = load_weights(meta, shards, off, pieces, w, sem)
    middle = pl.ds(tokens, tokens)
    ins = (ins[0], ins[1].at[middle], ins[2].at[middle], *ins[3:])
    loads = [
        pltpu.make_async_copy(x, to, sems.at[i])
        for i, (x, to) in enumerate(zip(ins, (dq, dk, dv, x_left, x_own, x_right, left, right)))
    ]
    for x in loads:
        x.start()
    before, after = used_chunks(rng)
    wait()
    for x in loads:
        x.wait()
    own[...] = dot_nt(dk[...], w[1]) + dot_nt(dv[...], w[2]) + dot_nt(dq[...], w[0])
    sums[...] = jnp.zeros(sums.shape, F32)

    def tally(grad, x, lo, hi):
        @pl.loop(lo, hi)
        def _(i):
            rows = pl.ds(pl.multiple_of(i * ROWS, ROWS), ROWS)
            hat, _ = normalise(x[rows, :].astype(F32))
            g = grad[rows, :].astype(F32)
            sums[0:1, :] += jnp.sum(g * hat, axis=0, keepdims=True)
            sums[1:2, :] += jnp.sum(g, axis=0, keepdims=True)

    tally(own, x_own, 0, tokens // ROWS)
    if count:
        tally(left, x_left, jnp.where(before, 0, (tokens - FAR) // ROWS), tokens // ROWS)
        tally(right, x_right, 0, jnp.where(after, tokens, FAR) // ROWS)


def input_grads(group, meta, rng, dq, dk, dv, window, halos, count, shards, pieces):
    tokens, cols = dq.shape
    width = shards[0].shape[0]
    per = pieces[0].shape[3]
    full = (tokens, width)
    return call(
        functools.partial(input_grads_kernel, len(pieces), group * per, count),
        [(full, F32), ((8, width), F32)],
        [meta, rng, dq, dk, dv, *window, *halos, *shards, *pieces],
        [pltpu.VMEM(dq.shape, BF16)] * 3
        + [pltpu.VMEM(full, BF16)] * 5
        + [
            pltpu.VMEM((3, width, cols), BF16),
            pltpu.SemaphoreType.DMA,
            pltpu.SemaphoreType.DMA((8,)),
        ],
        "input_grads",
        mib=28,
        smem=2,
        anys=11 + len(pieces),
    )


def last_kernel(inputs, g_resid, from_left, from_right, gain, *refs):
    *owns, g_inputs = refs

    @pl.loop(0, inputs.shape[0] // ROWS)
    def _(i):
        rows = pl.ds(pl.multiple_of(i * ROWS, ROWS), ROWS)
        hat, rstd = normalise(inputs[rows, :].astype(F32))
        g = from_left[rows, :].astype(F32) + from_right[rows, :].astype(F32)
        for own in owns:
            g = g + own[rows, :]
        g_inputs[rows, :] = (g_resid[rows, :] + norm_back(g, hat, rstd, gain[...])).astype(BF16)


def last_step(inputs, g_resid, from_left, from_right, gain, owns):
    return call(
        last_kernel,
        [(inputs.shape, BF16)],
        [inputs, g_resid, from_left, from_right, gain, *owns],
        [],
        "input_norm_grads",
        mib=16,
    )


def lay_out_kernel(turned, groups, size, meta, *refs):
    outs = refs[-len(turned) :]
    pieces = refs[: -len(turned)]
    n = len(pieces) // groups
    s = meta[0]
    per = pieces[0].shape[-1]
    for g in range(groups):
        to = slice(g * per, (g + 1) * per)
        if n == 1:
            whole = [
                (pieces[g].at[i], slice(i * size, (i + 1) * size))
                for i in range(pieces[g].shape[0])
            ]
        else:
            whole = [
                (pieces[g * n + j], pl.ds(pl.multiple_of((s ^ j) * size, size), size))
                for j in range(n)
            ]
        for piece, at in whole:
            for m, turn in enumerate(turned):
                part = piece[m, :size].astype(F32)
                if turn:
                    outs[m][to, at] = jnp.transpose(part)
                else:
                    outs[m][at, to] = part


def lay_out(meta, width, groups, turned):
    first = groups[0]
    size = width // (len(first) if len(first) > 1 else first[0].shape[0])
    shapes = [(SHARD, width) if turn else (width, SHARD) for turn in turned]
    return call(
        functools.partial(lay_out_kernel, turned, len(groups), size),
        [(shape, F32) for shape in shapes],
        [meta, *[piece for group in groups for piece in group]],
        [],
        "lay_out_grads",
        mib=12,
        smem=1,
    )


def pause_kernel(x, out):
    out[...] = x[...]


def pause(x):
    (out,) = call(pause_kernel, [(x.shape, x.dtype)], [x], [], "pause", mib=1)
    return out


SHARD = 256


def make_body(n_seq, n_tp):
    inner = min(n_seq, 8)
    outer = n_seq // inner
    half = inner // 2
    masks = [2 * jj for jj in range(1, half)]

    def shift(x, by):
        pairs = [(i, i + by) for i in range(n_tp) if 0 <= i + by < n_tp]
        return lax.ppermute(x, "tp", pairs)

    def swap(x, mask):
        return lax.ppermute(x, "seq", [(i, i ^ mask) for i in range(n_seq)])

    def tie(*xs):
        return lax.optimization_barrier(xs)

    def block_of(shards, biases, off, per, s):
        size = shards[0].shape[0] // inner
        cut = jnp.stack([lax.dynamic_slice(w, (s * size, off), (size, per)) for w in shards])
        if biases:
            parts = []
            rest = jnp.stack([b[off : off + per] for b in biases])
            for _ in range(3):
                part = rest.astype(BF16)
                rest = rest - part.astype(F32)
                parts.append(part)
            parts = jnp.stack(parts + [jnp.zeros_like(parts[0])] * 13, axis=1)
            cut = jnp.concatenate([cut, parts], axis=1)
        return jnp.broadcast_to(cut[None], (n_tp, *cut.shape))

    def over_tp(block):
        return lax.all_to_all(block, "tp", 0, 0, tiled=True)

    def others_of(got, size, t):
        return jnp.stack(
            [lax.dynamic_index_in_dim(got, lax.rem(t + r + 1, n_tp), 0, keepdims=False)[:, :size]
             for r in range(n_tp - 1)]
        )

    def biases_of(got, size):
        whole = jnp.sum(got[:, :, size : size + 3].astype(F32), axis=2)
        return [whole[:, m].reshape(1, -1) for m in range(whole.shape[1])]

    def from_chips(x):
        return [x] + [swap(x, mask) for mask in masks]

    def from_cores(even):
        odd = [swap(e, 1) for e in even]
        return [e for pair in zip(even, odd) for e in pair]

    def core_sums(keep, got):
        return [(k.astype(F32) + g.astype(F32)).astype(BF16) for k, g in zip(keep, got)]

    def over_chips(sums):
        return [swap(x, 2 * jj + 2) for jj, x in enumerate(sums)]

    def chip_sum(moved):
        total = moved[0].astype(F32)
        for x in moved[1:]:
            total = total + x.astype(F32)
        total = total.astype(BF16)
        if outer > 1:
            groups = [[i + inner * o for o in range(outer)] for i in range(inner)]
            total = lax.psum(total, "seq", axis_index_groups=groups)
        return total

    def own_shard(total):
        got = lax.all_to_all(total, "tp", 0, 0, tiled=True)
        return jnp.sum(got.astype(F32), axis=0).astype(BF16)

    def body(
        inputs, segment_ids, row_lengths, norm1_gain, norm1_shift, w_query, w_key, w_value,
        b_query, b_value, w_out, b_out, norm2_gain, norm2_shift, w_up, b_up, w_down, b_down,
        out_grad,
    ):
        tokens, width = inputs.shape
        halo = tokens
        t = lax.axis_index("tp")
        s = lax.rem(lax.axis_index("seq"), inner)
        meta = jnp.stack([s, t]).astype(jnp.int32)
        per = SHARD // GROUPS
        every = range(GROUPS)
        zero = jnp.zeros_like(b_query)

        def row(x):
            return x.reshape(1, -1)

        def by_shard(groups):
            cols = [x.reshape(n_tp, per) for x in groups]
            return jnp.concatenate(cols, axis=1).reshape(1, width)

        attn_w = [w_query, w_key, w_value]
        attn_b = [b_query, b_up, b_value]
        size = width // inner
        feed_w = [w_out.T, w_up, w_down.T]
        feed_block = block_of(feed_w, [], 0, SHARD, s)
        attn_p, attn_whole = [], []
        for g in every:
            got = over_tp(block_of(attn_w, attn_b, g * per, per, s))
            got, feed_block = tie(got, feed_block)
            even = from_chips(others_of(got, size, t))
            even[0], even[-1] = tie(even[0], even[-1])
            attn_p.append(from_cores(even))
            attn_whole.append(biases_of(got, size))
        got = over_tp(feed_block)
        inputs_later, got = tie(inputs, got)
        feed_p = from_chips(others_of(got, size, t))
        left = shift(inputs_later, 1)
        right = shift(inputs_later, -1)

        position = jnp.arange(ROW_LEN, dtype=jnp.int32)
        numbers = jnp.where(position < row_lengths[0], segment_ids[0], 4096 + position)
        numbers = jnp.concatenate(
            [jnp.full((halo,), -1, jnp.int32), numbers, jnp.full((halo,), 1 << 20, jnp.int32)]
        )
        seg_win = lax.dynamic_slice_in_dim(numbers, t * tokens, tokens + 2 * halo, 0)
        seg_mine = seg_win[halo : halo + tokens]
        first = seg_mine[::BLOCK]
        last = seg_mine[BLOCK - 1 :: BLOCK]
        low = jnp.sum((seg_win[None, :] < first[:, None]).astype(jnp.int32), axis=1)
        high = jnp.sum((seg_win[None, :] <= last[:, None]).astype(jnp.int32), axis=1)
        rng = jnp.stack([low // BLOCK, (high + BLOCK - 1) // BLOCK])
        segq, segk = seg_mine[None, :], seg_win[:, None]

        gain1, feed_w[0], feed_w[2] = tie(norm1_gain, feed_w[0], feed_w[2])
        source = (row(gain1), row(norm1_shift), left, inputs, right)
        saved = []
        for g in every:
            bq, _, bv = attn_whole[g]
            res = forward(g, meta, rng, segq, segk, source, bq, bv, attn_w, attn_p[g])
            mixed, lse, q, k, v = res[:5]
            if g == 0:
                source = first_low = res[5]
                mixed, *feed_p = tie(mixed, *feed_p)
                feed_p = from_cores(feed_p)
            saved.append((mixed, lse, q, k, v))
        bup = by_shard([x[1] for x in attn_whole])
        res = feed_forward(
            meta, inner, inputs, out_grad, row(b_out), row(norm2_gain), row(norm2_shift), bup,
            row(b_down), [x[0] for x in saved], feed_w, feed_p,
        )
        g_mixed, delta = list(res[:GROUPS]), res[GROUPS : 2 * GROUPS]
        sums_feed, output, g_resid, *travel = res[2 * GROUPS :]

        feed_got = [swap(x, 1) for x in travel[half:]]
        feed_own = (travel[0], feed_got[0])
        feed_moved = over_chips(core_sums(travel[1:half], feed_got[1:]))
        old, owns, sums_qkv, totals = (), [], [], []
        for g in every:
            _, lse, q, k, v = saved[g]
            vec, dq, dk, dv, keep, send = backward(
                meta, rng, segq, segk, lse, delta[g], q, g_mixed[g], k, v, first_low, inner
            )
            sums_qkv.append(vec)
            got = swap(send, 1)
            if g == 0:
                feed_moved, sums_feed = tie(feed_moved, sums_feed)
                got, sums_feed = tie(got, pause(sums_feed))
                feed_total = chip_sum([*feed_own, *feed_moved])
            sums = core_sums(keep[1:], got[1:])
            dk, sums = tie(dk, sums)
            moved = over_chips(sums)
            if g + 1 < GROUPS:
                g_mixed[g + 1], moved = tie(g_mixed[g + 1], moved)
            old = halo_grads(g, meta, rng, old, dk, dv, attn_w, attn_p[g])
            own, sums_in = input_grads(
                g, meta, rng, dq, dk, dv, (left, inputs, right), old, g + 1 == GROUPS,
                attn_w, attn_p[g],
            )
            owns.append(own)
            if g + 1 == GROUPS:
                feed_g = feed_total.reshape(-1, SHARD)
                feed_g = lax.psum_scatter(feed_g, "tp", scatter_dimension=0, tiled=True)
                moved, sums_in, feed_g = tie(moved, sums_in, feed_g)
            totals.append(chip_sum([keep[0], got[0], *moved]))
        from_right = shift(old[0], -1)
        from_left = shift(old[1], 1)
        piece = feed_total.shape[1:]
        feed_g = lax.all_gather(feed_g.reshape(piece), "seq", axis=0)[:inner]
        (g_inputs,) = last_step(
            inputs, g_resid, from_left, from_right, row(norm1_gain), owns
        )

        vectors = [by_shard([x[i] for x in sums_qkv]) for i in range(2)]
        vectors = jnp.concatenate([sums_in[:2], *vectors, sums_feed[:5]])
        if outer > 1:
            groups = [[i + inner * o for o in range(outer)] for i in range(inner)]
            vectors = lax.psum(vectors, "seq", axis_index_groups=groups)
        extra = -(-vectors.size // (48 * per)) * 16
        n_vec = vectors.size
        vectors = jnp.pad(vectors.astype(BF16).reshape(-1), (0, 3 * extra * per - n_vec))
        vectors = jnp.broadcast_to(vectors.reshape(1, 3, extra, per), (n_tp, 3, extra, per))
        totals[-1] = jnp.concatenate([totals[-1], vectors], axis=2)
        shards = [own_shard(x) for x in totals]
        shards[-1], g_inputs = tie(shards[-1], g_inputs)
        g_wo, g_wup, g_wdn = lay_out(meta, width, [[feed_g]], (True, False, True))
        evens = [from_chips(x) for x in shards]
        evens[-1][-1], g_wup = tie(evens[-1][-1], g_wup)
        pieces = [from_cores(x) for x in evens]
        vectors = sum([x[:, size:].astype(F32) for x in pieces[-1]])
        vectors = vectors.reshape(-1)[:n_vec].reshape(-1, width)
        n1g, n1s, g_bq, g_bv, g_bo, n2g, n2s, g_bup, g_bdn = [vectors[i] for i in range(9)]

        g_wq, g_wk, g_wv = lay_out(meta, width, pieces, (False, False, False))

        def shard(x):
            return lax.dynamic_slice_in_dim(x, t * SHARD, SHARD, 0)

        return (
            output, g_inputs, n1g, n1s, g_wq, g_wk, g_wv, shard(g_bq), shard(g_bv),
            g_wo, g_bo, n2g, n2s, g_wup, shard(g_bup), g_wdn, g_bdn,
        )

    return body


def solution(mesh):
    tok = P(("seq", "tp"), None)
    col, row, vec, rep = P(None, "tp"), P("tp", None), P("tp"), P()
    in_specs = (
        tok, P("seq", None), P("seq"), rep, rep, col, col, col, vec, vec,
        row, rep, rep, rep, col, vec, row, rep, tok,
    )
    out_specs = (
        tok, tok, rep, rep, col, col, col, vec, vec,
        row, rep, rep, rep, col, vec, row, rep,
    )
    body = make_body(mesh.shape["seq"], mesh.shape["tp"])
    return jax.shard_map(body, mesh=mesh, in_specs=in_specs, out_specs=out_specs, check_vma=False)
```

```python
import functools
import math

import jax
import jax.numpy as jnp
from jax import lax
from jax.experimental import pallas as pl
from jax.experimental.pallas import tpu as pltpu
from jax.sharding import PartitionSpec as P

HEAD_DIM = 128
ROW_LEN = 2048
NORM_EPS = 1e-05
MASKED = -1000000000.0
LOG2E = 1.4426950408889634
TILE = 256
BLOCK = 256
FAR = 256
ROWS = 128
GROUPS = 1
F32 = jnp.float32
BF16 = jnp.bfloat16
MIB = 1024 * 1024


def dot_nn(a, b):
    return lax.dot_general(a, b, (((1,), (0,)), ((), ())), preferred_element_type=F32)


def dot_nt(a, b):
    return lax.dot_general(a, b, (((1,), (1,)), ((), ())), preferred_element_type=F32)


def dot_tn(a, b):
    return lax.dot_general(a, b, (((0,), (0,)), ((), ())), preferred_element_type=F32)


def normalise(x):
    centre = x - jnp.mean(x, axis=-1, keepdims=True)
    rstd = lax.rsqrt(jnp.mean(centre * centre, axis=-1, keepdims=True) + NORM_EPS)
    return centre * rstd, rstd


def norm_back(grad, hat, rstd, gain):
    t = gain * grad
    mean_t = jnp.mean(t, axis=-1, keepdims=True)
    mean_th = jnp.mean(t * hat, axis=-1, keepdims=True)
    return (t - mean_t - hat * mean_th) * rstd


def call(kernel, outs, ins, scratch, name, smem=0, anys=0, out_anys=0, gflop=50, mib=50):
    spaces = [pltpu.SMEM] * smem + [pltpu.VMEM] * (len(ins) - smem - anys) + [pl.ANY] * anys
    out_spaces = [pltpu.VMEM] * (len(outs) - out_anys) + [pl.ANY] * out_anys
    return pl.pallas_call(
        kernel,
        out_shape=tuple(jax.ShapeDtypeStruct(*o) for o in outs),
        in_specs=[pl.BlockSpec(memory_space=m) for m in spaces],
        out_specs=tuple(pl.BlockSpec(memory_space=m) for m in out_spaces),
        scratch_shapes=scratch,
        compiler_params=pltpu.CompilerParams(vmem_limit_bytes=mib * MIB),
        cost_estimate=pl.CostEstimate(
            flops=gflop * 10**9, bytes_accessed=1000000, transcendentals=0
        ),
        name=name,
    )(*ins)


def load_weights(meta, shards, off, pieces, dst, sem, skipped=0):
    s, t = meta[0], meta[1]
    _, size, per = pieces[0].shape[1:]
    last = skipped + dst.shape[0]
    n_tp = dst.shape[2] // per
    mine = pl.ds(pl.multiple_of(t * per, per), per)
    for m in range(dst.shape[0]):
        source = shards[skipped + m].at[:, off : off + per]
        pltpu.make_async_copy(source, dst.at[m, :, mine], sem).start()
    for j, piece in enumerate(pieces):
        at = pl.ds(pl.multiple_of((s ^ j) * size, size), size)
        for r in range(n_tp - 1):
            u = pl.multiple_of(lax.rem(t + r + 1, n_tp) * per, per)
            source = piece.at[r, skipped:last]
            pltpu.make_async_copy(source, dst.at[:, at, pl.ds(u, per)], sem).start()
    return pltpu.make_async_copy(dst, dst, sem).wait


def store_grads(meta, grads, keep, send, sems, first, last):
    s = meta[0]
    n_tp, _, size, per = keep[0].shape
    for parity, dst in enumerate((keep, send)):
        for jj, piece in enumerate(dst):
            p = pl.ds(pl.multiple_of((s ^ (2 * jj + parity)) * size, size), size)
            for t in range(n_tp):
                pltpu.make_async_copy(
                    grads.at[first:last, p, t * per : (t + 1) * per],
                    piece.at[t, first:last],
                    sems.at[parity, jj],
                ).start()


def grads_stored(keep, send, sems):
    for parity, dst in enumerate((keep, send)):
        for jj, piece in enumerate(dst):
            pltpu.make_async_copy(piece, piece, sems.at[parity, jj]).wait()


def travelling(inner, width, per):
    half = max(inner // 2, 1)
    return half, (width // SHARD, 3, width // inner, per)


def attend(rng, segq, segk, q, k, v, mixed, lse, s_scr, m_scr, l_scr, acc):
    heads = q.shape[1] // HEAD_DIM
    coef = HEAD_DIM**-0.5 * LOG2E
    of = [slice(h * HEAD_DIM, (h + 1) * HEAD_DIM) for h in range(heads)]

    def fold(x, op):
        x = x.reshape(BLOCK // 8, 8, BLOCK)
        res = x[0]
        for i in range(1, BLOCK // 8):
            res = op(res, x[i])
        return res

    @pl.loop(0, q.shape[0] // BLOCK)
    def _(qb):
        rows = pl.ds(pl.multiple_of(qb * BLOCK, BLOCK), BLOCK)
        lo = rng[0, qb]
        hi = rng[1, qb]
        sq = segq[:, rows]
        m_scr[...] = jnp.full(m_scr.shape, -3e38, F32)
        l_scr[...] = jnp.zeros(l_scr.shape, F32)
        acc[...] = jnp.zeros(acc.shape, F32)

        @pl.loop(lo, hi)
        def _(kc):
            ks = pl.ds(pl.multiple_of(kc * BLOCK, BLOCK), BLOCK)
            bias = jnp.where(segk[ks, :] == sq, 0.0, MASKED)
            for h in range(0, heads, 2):
                pair = (h, h + 1)
                scores = [dot_nt(k[ks, of[i]], q[rows, of[i]]) * coef + bias for i in pair]
                for i, s in zip(pair, scores):
                    s_scr[kc, i] = s
                    m_scr[i] = jnp.maximum(m_scr[i], fold(s, jnp.maximum))

        for h in range(heads):
            m_scr[h] = jnp.broadcast_to(jnp.max(m_scr[h], axis=0, keepdims=True), (8, BLOCK))

        @pl.loop(lo, hi)
        def _(kc):
            ks = pl.ds(pl.multiple_of(kc * BLOCK, BLOCK), BLOCK)
            for h in range(0, heads, 2):
                pair = (h, h + 1)
                probs = [jnp.exp2(s_scr[kc, i] - m_scr[i, :1]) for i in pair]
                outs = [dot_tn(v[ks, of[i]], p.astype(BF16)) for i, p in zip(pair, probs)]
                for i, p, o in zip(pair, probs, outs):
                    l_scr[i] += fold(p, jnp.add)
                    acc[i] += o

        for h in range(heads):
            total = jnp.sum(l_scr[h], axis=0, keepdims=True)
            mixed[rows, of[h]] = jnp.transpose(acc[h] / total).astype(BF16)
            lse[h : h + 1, rows] = m_scr[h, :1] + jnp.log2(total)


def attend_back(rng, segq, segk, lse, delta, q, do, k, v, dq, dk_acc, dv_acc, dq_acc):
    heads = q.shape[1] // HEAD_DIM
    scale = HEAD_DIM**-0.5
    coef = scale * LOG2E
    of = [slice(h * HEAD_DIM, (h + 1) * HEAD_DIM) for h in range(heads)]

    @pl.loop(0, q.shape[0] // BLOCK)
    def _(qb):
        rows = pl.ds(pl.multiple_of(qb * BLOCK, BLOCK), BLOCK)
        lo = rng[0, qb]
        hi = rng[1, qb]
        sq = segq[:, rows]
        dq_acc[...] = jnp.zeros(dq_acc.shape, F32)

        @pl.loop(lo, hi)
        def _(kc):
            ks = pl.ds(pl.multiple_of(kc * BLOCK, BLOCK), BLOCK)
            bias = jnp.where(segk[ks, :] == sq, 0.0, MASKED)

            def probs(h):
                s = dot_nt(k[ks, of[h]], q[rows, of[h]]) * coef
                p = jnp.exp2(s + (bias - lse[h : h + 1, rows]))
                return p, dot_nt(v[ks, of[h]], do[rows, of[h]])

            def products(h, p, dp):
                ds = (p * (dp - delta[h : h + 1, rows])).astype(BF16)
                return (
                    dot_nn(p.astype(BF16), do[rows, of[h]]),
                    dot_nn(ds, q[rows, of[h]]),
                    dot_tn(k[ks, of[h]], ds),
                )

            for h in range(0, heads, 2):
                pair = (h, h + 1)
                both = [probs(i) for i in pair]
                terms = [products(i, *b) for i, b in zip(pair, both)]
                for i, (a, b, c) in zip(pair, terms):
                    dv_acc[ks, of[i]] += a
                    dk_acc[ks, of[i]] += b
                    dq_acc[i] += c

        for h in range(heads):
            dq[rows, of[h]] = (jnp.transpose(dq_acc[h]) * scale).astype(BF16)


def used_chunks(rng):
    tokens = BLOCK * rng.shape[1]
    before = rng[0, 0] * BLOCK < tokens - FAR
    after = rng[1, rng.shape[1] - 1] * BLOCK > 2 * tokens + FAR
    return before, after


def forward_kernel(first, n_pieces, off, meta, rng, segq, segk, *refs):
    if first:
        gain, shift, bq, bv, left, own, right, *refs = refs
    else:
        bq, bv, low_in, *refs = refs
    shards, pieces, refs = refs[:3], refs[3 : 3 + n_pieces], refs[3 + n_pieces :]
    mixed, lse, q_out, k_out, v_out, *refs = refs
    if first:
        low_out, *refs = refs
    q, k, v, low, w, s_scr, m_scr, l_scr, acc, sem, out_sems, *refs = refs
    tokens = q.shape[0]
    before, after = used_chunks(rng)
    lo = jnp.where(before, 0, (tokens - FAR) // BLOCK)
    hi = jnp.where(after, 3 * tokens, 2 * tokens + FAR) // BLOCK

    def copy(i, src, dst):
        return pltpu.make_async_copy(src, dst, out_sems.at[i])

    def chunk(c):
        return pl.ds(pl.multiple_of(c * BLOCK, BLOCK), BLOCK)

    if first:
        (window,) = refs
        ins = [
            copy(i, x, window.at[i * tokens : (i + 1) * tokens])
            for i, x in enumerate((left, own, right))
        ]
    else:
        ins = [copy(3, low_in, low)]
    for x in ins:
        x.start()
    wait = load_weights(meta, shards, off, pieces, w, sem)
    for x in ins:
        x.wait()
    outs = [(q, q_out), (k, k_out), (v, v_out)]
    if first:

        @pl.loop(lo, hi)
        def _(c):
            hat, _ = normalise(window[chunk(c), :].astype(F32))
            low[chunk(c), :] = (hat * gain[...] + shift[...]).astype(BF16)

        outs.append((low, low_out))
        copy(3, *outs[3]).start()
    wait()
    q[...] = (dot_nn(low[tokens : 2 * tokens, :], w[0]) + bq[...]).astype(BF16)
    copy(0, *outs[0]).start()
    def project(rows):
        k[rows, :] = dot_nn(low[rows, :], w[1]).astype(BF16)
        v[rows, :] = (dot_nn(low[rows, :], w[2]) + bv[...]).astype(BF16)

    start, stop = tokens - FAR, 2 * tokens + FAR
    project(slice(start, stop))
    pl.when(before)(lambda: project(slice(0, start)))
    pl.when(after)(lambda: project(slice(stop, 3 * tokens)))

    copy(1, *outs[1]).start()
    copy(2, *outs[2]).start()
    attend(rng, segq, segk, q, k, v, mixed, lse, s_scr, m_scr, l_scr, acc)
    for i, x in enumerate(outs):
        copy(i, *x).wait()


def forward(group, meta, rng, segq, segk, source, bq, bv, shards, pieces):
    first = group == 0
    width = shards[0].shape[0]
    window = segk.shape[0]
    tokens = window // 3
    per = pieces[0].shape[3]
    cols = bq.shape[1]
    heads = cols // HEAD_DIM
    slim, wide = (tokens, cols), (window, cols)
    kept = ((window, width), BF16)
    ins = [meta, rng, segq, segk]
    ins += [*source[:2], bq, bv, *source[2:]] if first else [bq, bv, source]
    return call(
        functools.partial(forward_kernel, first, len(pieces), group * per),
        [(slim, BF16), ((heads, tokens), F32), (slim, BF16), (wide, BF16), (wide, BF16)]
        + [kept] * first,
        [*ins, *shards, *pieces],
        [
            pltpu.VMEM(slim, BF16),
            pltpu.VMEM(wide, BF16),
            pltpu.VMEM(wide, BF16),
            pltpu.VMEM(*kept),
            pltpu.VMEM((3, width, cols), BF16),
            pltpu.VMEM((window // BLOCK, heads, BLOCK, BLOCK), F32),
            pltpu.VMEM((heads, 8, BLOCK), F32),
            pltpu.VMEM((heads, 8, BLOCK), F32),
            pltpu.VMEM((heads, HEAD_DIM, BLOCK), F32),
            pltpu.SemaphoreType.DMA,
            pltpu.SemaphoreType.DMA((4,)),
        ]
        + [pltpu.VMEM(*kept)] * first,
        "forward_attention",
        mib=46,
        smem=2,
        anys=3 + len(pieces) + (3 if first else 1),
        out_anys=3 + first,
    )


def feed_kernel(n_pieces, half, groups, meta, inputs, dout, bo, gain, shift, bup, bdn, *refs):
    parts, refs = refs[:groups], refs[groups:]
    shards, pieces, refs = refs[:3], refs[3 : 3 + n_pieces], refs[3 + n_pieces :]
    g_parts, refs = refs[:groups], refs[groups:]
    deltas, refs = refs[:groups], refs[groups:]
    sums, output_out, g_resid_out, *refs = refs
    keep, send, refs = refs[:half], refs[half : 2 * half], refs[2 * half :]
    w, mixed, resid, hat, rstd, second, hidden, g_up, g_sec, low, output, grads, *sems = refs
    first_sem, sem, grad_sems, out_sems = sems
    wo_t, wup, wdn_t = w.at[0], w.at[1], w.at[2]
    wait_first = load_weights(meta, shards, 0, pieces, w.at[:1], first_sem)
    wait = load_weights(meta, shards, 0, pieces, w.at[1:], sem, 1)
    tokens, width = inputs.shape
    per = SHARD // groups
    for g in range(groups):
        for t in range(width // SHARD):
            at = t * SHARD + g * per
            mixed[:, at : at + per] = parts[g][:, t * per : (t + 1) * per]
    sums[...] = jnp.zeros(sums.shape, F32)
    sums[4:5, :] = jnp.sum(dout[...].astype(F32), axis=0, keepdims=True)
    wait_first()
    resid[...] = inputs[...].astype(F32) + dot_nt(mixed[...], wo_t[...]) + bo[...]

    @pl.loop(0, tokens // BLOCK)
    def _(i):
        rows = pl.ds(pl.multiple_of(i * BLOCK, BLOCK), BLOCK)
        h, r = normalise(resid[rows, :])
        hat[rows, :] = h
        rstd[rows, :] = jnp.broadcast_to(r, (BLOCK, 128))
        second[rows, :] = (h * gain[...] + shift[...]).astype(BF16)

    wait()
    for n in range(width // TILE):
        cols = slice(n * TILE, (n + 1) * TILE)
        up = dot_nn(second[...], wup[:, cols]) + bup[:, cols]
        d_hidden = dot_nn(dout[...], wdn_t[:, cols])
        phi = 0.5 + 0.5 * lax.erf(up * (0.5**0.5))
        hidden[:, cols] = (up * phi).astype(BF16)
        slope = phi + up * (jnp.exp(-0.5 * up * up) * (0.5 / math.pi) ** 0.5)
        grad = (d_hidden * slope).astype(BF16)
        g_up[:, cols] = grad
        sums[3:4, cols] = jnp.sum(grad.astype(F32), axis=0, keepdims=True)
    g_sec[...] = dot_nt(g_up[...], wup[...])
    output[...] = (resid[...] + dot_nt(hidden[...], wdn_t[...]) + bdn[...]).astype(BF16)
    out_copy = pltpu.make_async_copy(output, output_out, out_sems.at[0])
    out_copy.start()
    grads[2] = dot_tn(dout[...], hidden[...]).astype(BF16)
    grads[1] = dot_tn(second[...], g_up[...]).astype(BF16)
    store_grads(meta, grads, keep, send, grad_sems, 1, 3)

    @pl.loop(0, tokens // ROWS)
    def _(i):
        rows = pl.ds(pl.multiple_of(i * ROWS, ROWS), ROWS)
        h, g = hat[rows, :], g_sec[rows, :]
        res = dout[rows, :].astype(F32) + norm_back(g, h, rstd[rows, :1], gain[...])
        resid[rows, :] = res
        low[rows, :] = res.astype(BF16)
        for n, x in enumerate((res, g * h, g)):
            sums[n : n + 1, :] += jnp.sum(x, axis=0, keepdims=True)

    resid_copy = pltpu.make_async_copy(resid, g_resid_out, out_sems.at[1])
    resid_copy.start()
    grads[0] = dot_tn(low[...], mixed[...]).astype(BF16)
    store_grads(meta, grads, keep, send, grad_sems, 0, 1)
    grad = dot_nn(low[...], wo_t[...]).astype(BF16)
    prod = grad.astype(F32) * mixed[...].astype(F32)
    high = prod.astype(BF16)
    rest_of = (prod - high.astype(F32)).astype(BF16)
    head_of = lax.broadcasted_iota(jnp.int32, (width, 128), 0) // HEAD_DIM
    member = jnp.where(head_of == lax.broadcasted_iota(jnp.int32, (width, 128), 1), 1.0, 0.0)
    member = member.astype(BF16)
    totals = dot_nn(high, member) + dot_nn(rest_of, member)
    for i in range(0, tokens, 128):
        turned = jnp.transpose(totals[i : i + 128])
        for n in range(width // HEAD_DIM):
            at = n * HEAD_DIM
            t, g, inside = at // SHARD, at % SHARD // per, at % per
            h = (t * per + inside) // HEAD_DIM
            deltas[g][h : h + 1, i : i + 128] = turned[n : n + 1]
    for g in range(groups):
        for t in range(width // SHARD):
            at = t * SHARD + g * per
            g_parts[g][:, t * per : (t + 1) * per] = grad[:, at : at + per]
    out_copy.wait()
    resid_copy.wait()
    grads_stored(keep, send, grad_sems)


def feed_forward(
    meta, inner, inputs, dout, bo, gain, shift, bup, bdn, parts, shards, pieces
):
    tokens, width = inputs.shape
    groups = len(parts)
    half, piece = travelling(inner, width, SHARD)
    travel = [(piece, BF16)] * (2 * half)
    wide = pltpu.VMEM((tokens, width), F32)
    slim = pltpu.VMEM((tokens, width), BF16)
    return call(
        functools.partial(feed_kernel, len(pieces), half, groups),
        [(parts[0].shape, BF16)] * groups
        + [((width // HEAD_DIM // groups, tokens), F32)] * groups
        + [((8, width), F32), ((tokens, width), BF16), ((tokens, width), F32)]
        + travel,
        [meta, inputs, dout, bo, gain, shift, bup, bdn, *parts, *shards, *pieces],
        [
            pltpu.VMEM((3, width, width), BF16),
            slim,
            wide,
            wide,
            pltpu.VMEM((tokens, 128), F32),
            slim,
            slim,
            slim,
            wide,
            slim,
            slim,
            pltpu.VMEM((3, width, width), BF16),
            pltpu.SemaphoreType.DMA,
            pltpu.SemaphoreType.DMA,
            pltpu.SemaphoreType.DMA((2, half)),
            pltpu.SemaphoreType.DMA((2,)),
        ],
        "feed_forward",
        mib=48,
        smem=1,
        anys=3 + len(pieces),
        out_anys=2 + 2 * half,
    )


def backward_kernel(half, meta, rng, segq, segk, lse, delta, q, do, k, v, low_in, *refs):
    sums, dq_out, dk_out, dv_out, keep, send, *refs = refs
    keep, send = [[x.at[jj] for jj in range(half)] for x in (keep, send)]
    low, dq, dk, dv, dk_acc, dv_acc, dq_acc, grads, sems, grad_sems = refs
    low_copy = pltpu.make_async_copy(low_in, low, sems.at[3])
    low_copy.start()
    tokens, width = q.shape
    start, stop = tokens - FAR, 2 * tokens + FAR
    near, middle = slice(start, stop), slice(tokens, 2 * tokens)
    before, after = used_chunks(rng)
    scale = HEAD_DIM**-0.5

    def zero(rows):
        dk_acc[rows, :] = jnp.zeros((rows.stop - rows.start, width), F32)
        dv_acc[rows, :] = jnp.zeros((rows.stop - rows.start, width), F32)

    def narrow(rows):
        dk[rows, :] = (dk_acc[rows, :] * scale).astype(BF16)
        dv[rows, :] = dv_acc[rows, :].astype(BF16)

    def ends(act):
        pl.when(before)(lambda: act(slice(0, start)))
        pl.when(after)(lambda: act(slice(stop, 3 * tokens)))

    zero(near)
    ends(zero)
    attend_back(rng, segq, segk, lse, delta, q, do, k, v, dq, dk_acc, dv_acc, dq_acc)
    narrow(near)
    ends(narrow)
    outs = [
        pltpu.make_async_copy(x, out, sems.at[i])
        for i, (x, out) in enumerate(((dq, dq_out), (dk, dk_out), (dv, dv_out)))
    ]
    for x in outs:
        x.start()

    low_copy.wait()
    grads[0] = dot_tn(low[middle, :], dq[...]).astype(BF16)
    grads[1] = dot_tn(low[near, :], dk[near, :]).astype(BF16)
    grads[2] = dot_tn(low[near, :], dv[near, :]).astype(BF16)
    sums[...] = jnp.zeros(sums.shape, F32)
    sums[0:1, :] = jnp.sum(dq[...].astype(F32), axis=0, keepdims=True)
    sums[1:2, :] = jnp.sum(dv[near, :].astype(F32), axis=0, keepdims=True)
    for i, used in enumerate((before, after)):

        @pl.when(used)
        def _():
            rows = slice(i * stop, i * stop + start)
            sums[1:2, :] += jnp.sum(dv[rows, :].astype(F32), axis=0, keepdims=True)
            for m, x in ((1, dk), (2, dv)):
                more = dot_tn(low[rows, :], x[rows, :])
                grads[m] = (grads[m].astype(F32) + more).astype(BF16)

    store_grads(meta, grads, keep, send, grad_sems, 0, 3)
    for x in outs:
        x.wait()
    grads_stored(keep, send, grad_sems)


def backward(meta, rng, segq, segk, lse, delta, q, do, k, v, low, inner):
    tokens, cols = q.shape
    width = low.shape[1]
    window = 3 * tokens
    per = cols // (width // SHARD)
    half, piece = travelling(inner, width, per)
    travel = [((half, *piece), BF16)] * 2
    slim, wide = (tokens, cols), (window, cols)
    return call(
        functools.partial(backward_kernel, half),
        [((8, cols), F32), (slim, BF16), (wide, BF16), (wide, BF16)] + travel,
        [meta, rng, segq, segk, lse, delta, q, do, k, v, low],
        [
            pltpu.VMEM((window, width), BF16),
            pltpu.VMEM(slim, BF16),
            pltpu.VMEM(wide, BF16),
            pltpu.VMEM(wide, BF16),
            pltpu.VMEM(wide, F32),
            pltpu.VMEM(wide, F32),
            pltpu.VMEM((cols // HEAD_DIM, HEAD_DIM, BLOCK), F32),
            pltpu.VMEM((3, width, cols), BF16),
            pltpu.SemaphoreType.DMA((4,)),
            pltpu.SemaphoreType.DMA((2, half)),
        ],
        "backward_attention",
        mib=50,
        smem=2,
        anys=1,
        out_anys=5,
    )


def halo_grads_kernel(n_pieces, off, more, meta, rng, *refs):
    if more:
        left_in, right_in, *refs = refs
    ins, refs = refs[:2], refs[2:]
    shards, pieces, refs = refs[:3], refs[3 : 3 + n_pieces], refs[3 + n_pieces :]
    left, right, dk, dv, w, sem, sems = refs
    wait = load_weights(meta, shards, off, pieces, w, sem, 1)
    tokens = left.shape[0]
    before, after = used_chunks(rng)
    loads = [
        pltpu.make_async_copy(x.at[rows], to.at[rows], sems.at[i])
        for i, (x, to) in enumerate(zip(ins, (dk, dv)))
        for rows in (pl.ds(0, tokens), pl.ds(2 * tokens, tokens))
    ]
    for x in loads:
        x.start()
    for x in loads:
        x.wait()
    wait()

    def halo_grads(out, old, to, rows):
        res = dot_nt(dk[rows, :], w[0]) + dot_nt(dv[rows, :], w[1])
        if more:
            res = res + old[to, :].astype(F32)
        out[to, :] = res.astype(BF16)

    lows, highs = slice(0, tokens - FAR), slice(tokens - FAR, tokens)
    firsts, others = slice(0, FAR), slice(FAR, tokens)
    for out, old, used, far_to, near_to, base in (
        (left, left_in if more else None, before, lows, highs, 0),
        (right, right_in if more else None, after, others, firsts, 2 * tokens),
    ):
        halo_grads(out, old, near_to, slice(base + near_to.start, base + near_to.stop))

        @pl.when(used)
        def _():
            halo_grads(out, old, far_to, slice(base + far_to.start, base + far_to.stop))

        @pl.when(jnp.logical_not(used))
        def _():
            if more:
                out[far_to, :] = old[far_to, :]
            else:
                out[far_to, :] = jnp.zeros((tokens - FAR, out.shape[1]), BF16)


def halo_grads(group, meta, rng, old, dk, dv, shards, pieces):
    cols = dk.shape[1]
    width = shards[0].shape[0]
    per = pieces[0].shape[3]
    full = (dk.shape[0] // 3, width)
    return call(
        functools.partial(halo_grads_kernel, len(pieces), group * per, len(old) > 0),
        [(full, BF16), (full, BF16)],
        [meta, rng, *old, dk, dv, *shards, *pieces],
        [
            pltpu.VMEM(dk.shape, BF16),
            pltpu.VMEM(dv.shape, BF16),
            pltpu.VMEM((2, width, cols), BF16),
            pltpu.SemaphoreType.DMA,
            pltpu.SemaphoreType.DMA((2,)),
        ],
        "halo_grads",
        mib=24,
        smem=2,
        anys=5 + len(pieces),
    )


def input_grads_kernel(n_pieces, off, count, meta, rng, *refs):
    ins, refs = refs[:8], refs[8:]
    shards, pieces, refs = refs[:3], refs[3 : 3 + n_pieces], refs[3 + n_pieces :]
    own, sums, dq, dk, dv, *refs = refs
    x_left, x_own, x_right, left, right, w, sem, sems = refs
    tokens = dq.shape[0]
    wait = load_weights(meta, shards, off, pieces, w, sem)
    middle = pl.ds(tokens, tokens)
    ins = (ins[0], ins[1].at[middle], ins[2].at[middle], *ins[3:])
    loads = [
        pltpu.make_async_copy(x, to, sems.at[i])
        for i, (x, to) in enumerate(zip(ins, (dq, dk, dv, x_left, x_own, x_right, left, right)))
    ]
    for x in loads:
        x.start()
    before, after = used_chunks(rng)
    wait()
    for x in loads:
        x.wait()
    own[...] = dot_nt(dk[...], w[1]) + dot_nt(dv[...], w[2]) + dot_nt(dq[...], w[0])
    sums[...] = jnp.zeros(sums.shape, F32)

    def tally(grad, x, lo, hi):
        @pl.loop(lo, hi)
        def _(i):
            rows = pl.ds(pl.multiple_of(i * ROWS, ROWS), ROWS)
            hat, _ = normalise(x[rows, :].astype(F32))
            g = grad[rows, :].astype(F32)
            sums[0:1, :] += jnp.sum(g * hat, axis=0, keepdims=True)
            sums[1:2, :] += jnp.sum(g, axis=0, keepdims=True)

    tally(own, x_own, 0, tokens // ROWS)
    if count:
        tally(left, x_left, jnp.where(before, 0, (tokens - FAR) // ROWS), tokens // ROWS)
        tally(right, x_right, 0, jnp.where(after, tokens, FAR) // ROWS)


def input_grads(group, meta, rng, dq, dk, dv, window, halos, count, shards, pieces):
    tokens, cols = dq.shape
    width = shards[0].shape[0]
    per = pieces[0].shape[3]
    full = (tokens, width)
    return call(
        functools.partial(input_grads_kernel, len(pieces), group * per, count),
        [(full, F32), ((8, width), F32)],
        [meta, rng, dq, dk, dv, *window, *halos, *shards, *pieces],
        [pltpu.VMEM(dq.shape, BF16)] * 3
        + [pltpu.VMEM(full, BF16)] * 5
        + [
            pltpu.VMEM((3, width, cols), BF16),
            pltpu.SemaphoreType.DMA,
            pltpu.SemaphoreType.DMA((8,)),
        ],
        "input_grads",
        mib=28,
        smem=2,
        anys=11 + len(pieces),
    )


def last_kernel(inputs, g_resid, from_left, from_right, gain, *refs):
    *owns, g_inputs = refs

    @pl.loop(0, inputs.shape[0] // ROWS)
    def _(i):
        rows = pl.ds(pl.multiple_of(i * ROWS, ROWS), ROWS)
        hat, rstd = normalise(inputs[rows, :].astype(F32))
        g = from_left[rows, :].astype(F32) + from_right[rows, :].astype(F32)
        for own in owns:
            g = g + own[rows, :]
        g_inputs[rows, :] = (g_resid[rows, :] + norm_back(g, hat, rstd, gain[...])).astype(BF16)


def last_step(inputs, g_resid, from_left, from_right, gain, owns):
    return call(
        last_kernel,
        [(inputs.shape, BF16)],
        [inputs, g_resid, from_left, from_right, gain, *owns],
        [],
        "input_norm_grads",
        mib=16,
    )


def lay_out_kernel(size, turned, meta, gathered, *refs):
    count = len(turned)
    *refs, vectors = refs
    pieces, first, second = refs[: -2 * count], refs[-2 * count : -count], refs[-count:]
    s = meta[0]
    vectors[...] = sum([piece[:, size:].astype(F32) for piece in pieces])
    for i in range(gathered.shape[0]):
        at = slice(i * size, (i + 1) * size)
        for m, turn in enumerate(turned):
            part = gathered[i, m].astype(F32)
            if turn:
                first[m][:, at] = jnp.transpose(part)
            else:
                first[m][at, :] = part
    for j, piece in enumerate(pieces):
        at = pl.ds(pl.multiple_of((s ^ j) * size, size), size)
        for m in range(count):
            second[m][at, :] = piece[m, :size].astype(F32)


def lay_out(meta, width, gathered, pieces, turned):
    col, row = ((width, SHARD), F32), ((SHARD, width), F32)
    count, rows, per = pieces[0].shape
    size = width // len(pieces)
    return call(
        functools.partial(lay_out_kernel, size, turned),
        [row if turn else col for turn in turned]
        + [col] * len(turned)
        + [((count, rows - size, per), F32)],
        [meta, gathered, *pieces],
        [],
        "lay_out_grads",
        mib=20,
        smem=1,
    )


def pause_kernel(x, out):
    out[...] = x[...]


def pause(x):
    (out,) = call(pause_kernel, [(x.shape, x.dtype)], [x], [], "pause", mib=1)
    return out


SHARD = 256


def make_body(n_seq, n_tp):
    inner = min(n_seq, 8)
    outer = n_seq // inner
    half = inner // 2
    masks = [2 * jj for jj in range(1, half)]

    def shift(x, by):
        pairs = [(i, i + by) for i in range(n_tp) if 0 <= i + by < n_tp]
        return lax.ppermute(x, "tp", pairs)

    def swap(x, mask):
        return lax.ppermute(x, "seq", [(i, i ^ mask) for i in range(n_seq)])

    def tie(*xs):
        return lax.optimization_barrier(xs)

    def block_of(shards, biases, off, per, s):
        size = shards[0].shape[0] // inner
        cut = jnp.stack([lax.dynamic_slice(w, (s * size, off), (size, per)) for w in shards])
        if biases:
            parts = []
            rest = jnp.stack([b[off : off + per] for b in biases])
            for _ in range(3):
                part = rest.astype(BF16)
                rest = rest - part.astype(F32)
                parts.append(part)
            parts = jnp.stack(parts + [jnp.zeros_like(parts[0])] * 13, axis=1)
            cut = jnp.concatenate([cut, parts], axis=1)
        return jnp.broadcast_to(cut[None], (n_tp, *cut.shape))

    def over_tp(block):
        return lax.all_to_all(block, "tp", 0, 0, tiled=True)

    def others_of(got, size, t):
        return jnp.stack(
            [lax.dynamic_index_in_dim(got, lax.rem(t + r + 1, n_tp), 0, keepdims=False)[:, :size]
             for r in range(n_tp - 1)]
        )

    def biases_of(got, size):
        whole = jnp.sum(got[:, :, size : size + 3].astype(F32), axis=2)
        return [whole[:, m].reshape(1, -1) for m in range(whole.shape[1])]

    def from_chips(x):
        return [x] + [swap(x, mask) for mask in masks]

    def from_cores(even):
        odd = [swap(e, 1) for e in even]
        return [e for pair in zip(even, odd) for e in pair]

    def core_sums(keep, got):
        return [(k.astype(F32) + g.astype(F32)).astype(BF16) for k, g in zip(keep, got)]

    def over_chips(sums):
        return [swap(x, 2 * jj + 2) for jj, x in enumerate(sums)]

    def chip_sum(moved):
        total = moved[0].astype(F32)
        for x in moved[1:]:
            total = total + x.astype(F32)
        total = total.astype(BF16)
        if outer > 1:
            groups = [[i + inner * o for o in range(outer)] for i in range(inner)]
            total = lax.psum(total, "seq", axis_index_groups=groups)
        return total

    def own_shard(total):
        got = lax.all_to_all(total, "tp", 0, 0, tiled=True)
        return jnp.sum(got.astype(F32), axis=0).astype(BF16)

    def body(
        inputs, segment_ids, row_lengths, norm1_gain, norm1_shift, w_query, w_key, w_value,
        b_query, b_value, w_out, b_out, norm2_gain, norm2_shift, w_up, b_up, w_down, b_down,
        out_grad,
    ):
        tokens, width = inputs.shape
        halo = tokens
        t = lax.axis_index("tp")
        s = lax.rem(lax.axis_index("seq"), inner)
        meta = jnp.stack([s, t]).astype(jnp.int32)
        per = SHARD // GROUPS
        every = range(GROUPS)
        zero = jnp.zeros_like(b_query)

        def row(x):
            return x.reshape(1, -1)

        def by_shard(groups):
            cols = [x.reshape(n_tp, per) for x in groups]
            return jnp.concatenate(cols, axis=1).reshape(1, width)

        attn_w = [w_query, w_key, w_value]
        attn_b = [b_query, b_up, b_value]
        size = width // inner
        feed_w = [w_out.T, w_up, w_down.T]
        feed_block = block_of(feed_w, [], 0, SHARD, s)
        attn_p, attn_whole = [], []
        for g in every:
            got = over_tp(block_of(attn_w, attn_b, g * per, per, s))
            got, feed_block = tie(got, feed_block)
            even = from_chips(others_of(got, size, t))
            even[0], even[-1] = tie(even[0], even[-1])
            attn_p.append(from_cores(even))
            attn_whole.append(biases_of(got, size))
        got = over_tp(feed_block)
        inputs_later, got = tie(inputs, got)
        feed_p = from_chips(others_of(got, size, t))
        left = shift(inputs_later, 1)
        right = shift(inputs_later, -1)

        position = jnp.arange(ROW_LEN, dtype=jnp.int32)
        numbers = jnp.where(position < row_lengths[0], segment_ids[0], 4096 + position)
        numbers = jnp.concatenate(
            [jnp.full((halo,), -1, jnp.int32), numbers, jnp.full((halo,), 1 << 20, jnp.int32)]
        )
        seg_win = lax.dynamic_slice_in_dim(numbers, t * tokens, tokens + 2 * halo, 0)
        seg_mine = seg_win[halo : halo + tokens]
        first = seg_mine[::BLOCK]
        last = seg_mine[BLOCK - 1 :: BLOCK]
        low = jnp.sum((seg_win[None, :] < first[:, None]).astype(jnp.int32), axis=1)
        high = jnp.sum((seg_win[None, :] <= last[:, None]).astype(jnp.int32), axis=1)
        rng = jnp.stack([low // BLOCK, (high + BLOCK - 1) // BLOCK])
        segq, segk = seg_mine[None, :], seg_win[:, None]

        gain1, feed_w[0], feed_w[2] = tie(norm1_gain, feed_w[0], feed_w[2])
        source = (row(gain1), row(norm1_shift), left, inputs, right)
        saved = []
        for g in every:
            bq, _, bv = attn_whole[g]
            res = forward(g, meta, rng, segq, segk, source, bq, bv, attn_w, attn_p[g])
            mixed, lse, q, k, v = res[:5]
            if g == 0:
                source = first_low = res[5]
                mixed, *feed_p[1:] = tie(mixed, *feed_p[1:])
                feed_p = from_cores(feed_p)
            saved.append((mixed, lse, q, k, v))
        bup = by_shard([x[1] for x in attn_whole])
        res = feed_forward(
            meta, inner, inputs, out_grad, row(b_out), row(norm2_gain), row(norm2_shift), bup,
            row(b_down), [x[0] for x in saved], feed_w, feed_p,
        )
        g_mixed, delta = list(res[:GROUPS]), res[GROUPS : 2 * GROUPS]
        sums_feed, output, g_resid, *travel = res[2 * GROUPS :]

        feed_got = [swap(x, 1) for x in travel[half:]]
        feed_own = (travel[0], feed_got[0])
        feed_moved = over_chips(core_sums(travel[1:half], feed_got[1:]))
        old, owns, sums_qkv, totals = (), [], [], []
        for g in every:
            _, lse, q, k, v = saved[g]
            vec, dq, dk, dv, keep, send = backward(
                meta, rng, segq, segk, lse, delta[g], q, g_mixed[g], k, v, first_low, inner
            )
            sums_qkv.append(vec)
            got = swap(send, 1)
            if g == 0:
                feed_moved, sums_feed = tie(feed_moved, sums_feed)
                got, sums_feed = tie(got, pause(sums_feed))
                feed_total = chip_sum([*feed_own, *feed_moved])
            sums = core_sums(keep[1:], got[1:])
            dk, sums = tie(dk, sums)
            moved = over_chips(sums)
            if g + 1 < GROUPS:
                g_mixed[g + 1], moved = tie(g_mixed[g + 1], moved)
            old = halo_grads(g, meta, rng, old, dk, dv, attn_w, attn_p[g])
            own, sums_in = input_grads(
                g, meta, rng, dq, dk, dv, (left, inputs, right), old, g + 1 == GROUPS,
                attn_w, attn_p[g],
            )
            owns.append(own)
            if g + 1 == GROUPS:
                feed_g = feed_total.reshape(-1, SHARD)
                feed_g = lax.psum_scatter(feed_g, "tp", scatter_dimension=0, tiled=True)
                moved, sums_in, feed_g = tie(moved, sums_in, feed_g)
            totals.append(chip_sum([keep[0], got[0], *moved]))
        from_right = shift(old[0], -1)
        from_left = shift(old[1], 1)
        piece = feed_total.shape[1:]
        feed_g = lax.all_gather(feed_g.reshape(piece), "seq", axis=0)[:inner]
        (g_inputs,) = last_step(
            inputs, g_resid, from_left, from_right, row(norm1_gain), owns
        )

        vectors = [by_shard([x[i] for x in sums_qkv]) for i in range(2)]
        vectors = jnp.concatenate([sums_in[:2], *vectors, sums_feed[:5]])
        if outer > 1:
            groups = [[i + inner * o for o in range(outer)] for i in range(inner)]
            vectors = lax.psum(vectors, "seq", axis_index_groups=groups)
        extra = -(-vectors.size // (48 * per)) * 16
        n_vec = vectors.size
        vectors = jnp.pad(vectors.astype(BF16).reshape(-1), (0, 3 * extra * per - n_vec))
        vectors = jnp.broadcast_to(vectors.reshape(1, 3, extra, per), (n_tp, 3, extra, per))
        totals[-1] = jnp.concatenate([totals[-1], vectors], axis=2)
        shards = [own_shard(x) for x in totals]
        shards[-1], g_inputs = tie(shards[-1], g_inputs)
        evens = [from_chips(x) for x in shards]
        pieces = [from_cores(x) for x in evens]
        g_wo, g_wup, g_wdn, g_wq, g_wk, g_wv, vectors = lay_out(
            meta, width, feed_g, pieces[-1], (True, False, True)
        )
        vectors = vectors.reshape(-1)[:n_vec].reshape(-1, width)
        n1g, n1s, g_bq, g_bv, g_bo, n2g, n2s, g_bup, g_bdn = [vectors[i] for i in range(9)]

        def shard(x):
            return lax.dynamic_slice_in_dim(x, t * SHARD, SHARD, 0)

        return (
            output, g_inputs, n1g, n1s, g_wq, g_wk, g_wv, shard(g_bq), shard(g_bv),
            g_wo, g_bo, n2g, n2s, g_wup, shard(g_bup), g_wdn, g_bdn,
        )

    return body


def solution(mesh):
    tok = P(("seq", "tp"), None)
    col, row, vec, rep = P(None, "tp"), P("tp", None), P("tp"), P()
    in_specs = (
        tok, P("seq", None), P("seq"), rep, rep, col, col, col, vec, vec,
        row, rep, rep, rep, col, vec, row, rep, tok,
    )
    out_specs = (
        tok, tok, rep, rep, col, col, col, vec, vec,
        row, rep, rep, rep, col, vec, row, rep,
    )
    body = make_body(mesh.shape["seq"], mesh.shape["tp"])
    return jax.shard_map(body, mesh=mesh, in_specs=in_specs, out_specs=out_specs, check_vma=False)
```
